32 devices in a mesh: wide: 16 (over z, x, core), narrow: 2 (over y).
Axes of the slice: x: 2, y: 2, z: 4, core: 2. Of those that a mesh axis runs over, the one named last changes fastest.
Arguments:
- small_maps: bfloat16 [256, 16, 16, 256], P('wide', None, None, 'narrow'), may hold values from -6 to 6
- large_maps: bfloat16 [64, 32, 32, 256], P('wide', None, None, 'narrow'), may hold values from -6 to 6
- small_steps: int32 [256], P('wide'), may hold values from 0 to 999
- large_steps: int32 [64], P('wide'), may hold values from 0 to 999
- live_counts: int32 [16, 2], P('wide'), may hold values from 2 to 16, as said below
- small_cotangent: bfloat16 [256, 16, 16, 256], P('wide', None, None, 'narrow'), may hold values from -6 to 6
- large_cotangent: bfloat16 [64, 32, 32, 256], P('wide', None, None, 'narrow'), may hold values from -6 to 6
- first_conv: float32 [256, 2304], P('narrow', 'wide'), may hold values from -0.125 to 0.125
- second_conv: float32 [256, 2304], P('narrow', 'wide'), may hold values from -0.125 to 0.125
- time_dense: float32 [1024, 256], P('wide', 'narrow'), may hold values from -0.1875 to 0.1875
- attn_qkv: float32 [256, 768], P(None, ('wide', 'narrow')), may hold values from -0.375 to 0.375
- attn_proj: float32 [256, 256], P(None, ('wide', 'narrow')), may hold values from -3 to 3
- vectors: float32 [12, 256], P(None, ('wide', 'narrow')), may hold values from -2 to 2
- first_conv_mean: float32 [256, 2304], P('narrow', 'wide')
- first_conv_square: float32 [256, 2304], P('narrow', 'wide')
- second_conv_mean: float32 [256, 2304], P('narrow', 'wide')
- second_conv_square: float32 [256, 2304], P('narrow', 'wide')
- time_dense_mean: float32 [1024, 256], P('wide', 'narrow')
- time_dense_square: float32 [1024, 256], P('wide', 'narrow')
- attn_qkv_mean: float32 [256, 768], P(None, ('wide', 'narrow'))
- attn_qkv_square: float32 [256, 768], P(None, ('wide', 'narrow'))
- attn_proj_mean: float32 [256, 256], P(None, ('wide', 'narrow'))
- attn_proj_square: float32 [256, 256], P(None, ('wide', 'narrow'))
- vectors_mean: float32 [12, 256], P(None, ('wide', 'narrow'))
- vectors_square: float32 [12, 256], P(None, ('wide', 'narrow'))
Outputs:
- small_out: bfloat16 [256, 16, 16, 256], P('wide', None, None, 'narrow')
- large_out: bfloat16 [64, 32, 32, 256], P('wide', None, None, 'narrow')
- small_input_grad: float32 [256, 16, 16, 256], P('wide', None, None, 'narrow')
- large_input_grad: float32 [64, 32, 32, 256], P('wide', None, None, 'narrow')
- first_conv_new: float32 [256, 2304], P('narrow', 'wide')
- first_conv_mean_new: float32 [256, 2304], P('narrow', 'wide')
- first_conv_square_new: float32 [256, 2304], P('narrow', 'wide')
- second_conv_new: float32 [256, 2304], P('narrow', 'wide')
- second_conv_mean_new: float32 [256, 2304], P('narrow', 'wide')
- second_conv_square_new: float32 [256, 2304], P('narrow', 'wide')
- time_dense_new: float32 [1024, 256], P('wide', 'narrow')
- time_dense_mean_new: float32 [1024, 256], P('wide', 'narrow')
- time_dense_square_new: float32 [1024, 256], P('wide', 'narrow')
- attn_qkv_new: float32 [256, 768], P(None, ('wide', 'narrow'))
- attn_qkv_mean_new: float32 [256, 768], P(None, ('wide', 'narrow'))
- attn_qkv_square_new: float32 [256, 768], P(None, ('wide', 'narrow'))
- attn_proj_new: float32 [256, 256], P(None, ('wide', 'narrow'))
- attn_proj_mean_new: float32 [256, 256], P(None, ('wide', 'narrow'))
- attn_proj_square_new: float32 [256, 256], P(None, ('wide', 'narrow'))
- vectors_new: float32 [12, 256], P(None, ('wide', 'narrow'))
- vectors_mean_new: float32 [12, 256], P(None, ('wide', 'narrow'))
- vectors_square_new: float32 [12, 256], P(None, ('wide', 'narrow'))
The draws below stay inside these ranges and needn't reach their ends.
Inputs may be any that keep to these rules, and one draw needn't show every extreme that they name: `live_counts`: live maps fill the first slots of their index of wide; at some index of wide every slot of both sizes is live.
All inputs are finite; a program needn't handle non-finite values.
Results may differ from the reference program's by a relative error of at most 0.029.
Values may be sent and summed in bfloat16 or wider, within the bound.
No kernel may reach another device: no remote copies, remote signals or barrier semaphores. Data moves between devices by JAX's collectives and lax.ppermute only.
A program may use at most 192 MiB of HBM per device.

```python
import math
from functools import partial
import jax
import jax.numpy as jnp
from jax import lax

CHANNELS = 256
GROUPS = 32
TIME_WIDTH = 1024
SMALL_SIDE = 16
LARGE_SIDE = 32
SMALL_SLOTS = 16
LARGE_SLOTS = 4
STEP_NUMBER = 10
VECTOR_ROWS = 12
SMALL_TOTAL = 256
LARGE_TOTAL = 64
PIXELS = 131072
N_WIDE = 16


def draw_live_counts(key, part):
    sub_key = jax.random.fold_in(key, 20)
    key_small, key_large, key_full = jax.random.split(sub_key, 3)
    row_count = SMALL_TOTAL // SMALL_SLOTS
    small_live = jax.random.randint(key_small, (row_count,), (SMALL_SLOTS + 1) // 2, SMALL_SLOTS + 1)
    large_live = jax.random.randint(key_large, (row_count,), LARGE_SLOTS // 2, LARGE_SLOTS + 1)
    fullest = jax.random.randint(key_full, (), 0, row_count)
    chosen = jnp.arange(row_count) == fullest
    small_live = jnp.where(chosen, SMALL_SLOTS, small_live)
    large_live = jnp.where(chosen, LARGE_SLOTS, large_live)
    return jnp.stack([small_live, large_live], axis=1).astype(jnp.int32)


def draw_vectors(key, part):
    sub_key = jax.random.fold_in(key, 21)
    key_gain, key_shift = jax.random.split(sub_key)
    gains = jnp.exp(jax.random.uniform(key_gain, (VECTOR_ROWS, CHANNELS), jnp.float32, -0.69, 0.69))
    shifts = 0.5 * jnp.clip(jax.random.normal(key_shift, (VECTOR_ROWS, CHANNELS), jnp.float32), -4.0, 4.0)
    row_ids = jnp.arange(VECTOR_ROWS)
    gain_rows = (row_ids < 6) & (row_ids % 2 == 0)
    return jnp.where(gain_rows[:, None], gains, shifts)


def moment_draw(key, salt, row_count, col_count, grad_size, second):
    sub_key = jax.random.fold_in(key, salt)
    if second:
        factor = jnp.exp(jax.random.uniform(sub_key, (row_count, col_count), jnp.float32, 0.0, 1.386))
        return factor * (grad_size * grad_size / 999.0)
    noise = jnp.clip(jax.random.normal(sub_key, (row_count, col_count), jnp.float32), -4.0, 4.0)
    return noise * (grad_size / 9.0)


def draw_first_conv_mean(key, part):
    return moment_draw(key, 1, CHANNELS, 9 * CHANNELS, 0.7 * math.sqrt(PIXELS), False)


def draw_first_conv_square(key, part):
    return moment_draw(key, 2, CHANNELS, 9 * CHANNELS, 0.7 * math.sqrt(PIXELS), True)


def draw_second_conv_mean(key, part):
    return moment_draw(key, 3, CHANNELS, 9 * CHANNELS, 0.7 * math.sqrt(PIXELS), False)


def draw_second_conv_square(key, part):
    return moment_draw(key, 4, CHANNELS, 9 * CHANNELS, 0.7 * math.sqrt(PIXELS), True)


def draw_time_dense_mean(key, part):
    return moment_draw(key, 5, TIME_WIDTH, CHANNELS, 0.45 * math.sqrt(PIXELS), False)


def draw_time_dense_square(key, part):
    return moment_draw(key, 6, TIME_WIDTH, CHANNELS, 0.45 * math.sqrt(PIXELS), True)


def draw_attn_qkv_mean(key, part):
    return moment_draw(key, 7, CHANNELS, 3 * CHANNELS, 0.7 * math.sqrt(PIXELS), False)


def draw_attn_qkv_square(key, part):
    return moment_draw(key, 8, CHANNELS, 3 * CHANNELS, 0.7 * math.sqrt(PIXELS), True)


def draw_attn_proj_mean(key, part):
    return moment_draw(key, 9, CHANNELS, CHANNELS, 0.15 * math.sqrt(PIXELS), False)


def draw_attn_proj_square(key, part):
    return moment_draw(key, 10, CHANNELS, CHANNELS, 0.15 * math.sqrt(PIXELS), True)


def draw_vectors_mean(key, part):
    return moment_draw(key, 11, VECTOR_ROWS, CHANNELS, 0.7 * math.sqrt(PIXELS), False)


def draw_vectors_square(key, part):
    return moment_draw(key, 12, VECTOR_ROWS, CHANNELS, 0.7 * math.sqrt(PIXELS), True)


def touch_ends(drawn, stream_key, least, largest):
    longest = drawn.shape.index(max(drawn.shape))
    spots = []
    for shift in (0, 1):
        where = [jax.random.randint(jax.random.fold_in(stream_key, axis), (), 0, length) for axis, length in enumerate(drawn.shape)]
        where[longest] = (where[longest] + shift) % drawn.shape[longest]
        spots.append(tuple(where))
    return drawn.at[spots[0]].set(least).at[spots[1]].set(largest)


def spiked(entries, stream_key, source, target, blocks, factor):
    def block_of(position):
        return (jnp.arange(entries.shape[position]) // (entries.shape[position] // blocks)).reshape((-1,) + (1,) * (entries.ndim - 1 - position))

    near = jax.random.permutation(stream_key, blocks)[block_of(target)]
    other_side = (block_of(target) + blocks // 2) % blocks
    return jnp.where((block_of(source) == near) | (block_of(source) == other_side), factor * entries, entries)


def levels(stream_key, extent, pieces, least, high):
    loudness = 1.0
    for dim, shards_of in pieces:
        steps = jax.random.uniform(jax.random.fold_in(jax.random.fold_in(stream_key, 6), dim), (shards_of,), jnp.float32, least / len(pieces), high / len(pieces))
        loudness = loudness * jnp.repeat(jnp.exp(steps), extent[dim] // shards_of).reshape((-1,) + (1,) * (len(extent) - 1 - dim))
    return loudness


def bell_draw(own_key, dims, scale, reach, pieces=(), kind=jnp.bfloat16):
    array = scale * jax.random.normal(own_key, dims, jnp.float32)
    if pieces:
        array = array * levels(own_key, dims, pieces, -0.22, 0.18)
    return jnp.clip(array, -reach, reach).astype(kind)


def bell_draw_with(own_key, dims, width, limit, pieces, heavy, kind=jnp.bfloat16):
    array = width * jax.random.normal(own_key, dims, jnp.float32)
    if pieces:
        array = array * levels(own_key, dims, pieces, -0.22, 0.18)
    return jnp.clip(spiked(array, jax.random.fold_in(own_key, 3), *heavy), -limit, limit).astype(kind)


def setup_inputs(seed: int = 0) -> dict:
    keys = jax.random.split(jax.random.key(seed), 26)
    return {
        "small_maps": bell_draw(keys[0], (SMALL_TOTAL, SMALL_SIDE, SMALL_SIDE, CHANNELS), 1.0, 6.0, ((0, 16), (3, 2))),
        "large_maps": bell_draw(keys[1], (LARGE_TOTAL, LARGE_SIDE, LARGE_SIDE, CHANNELS), 1.0, 6.0, ((0, 16), (3, 2))),
        "small_steps": touch_ends(jax.random.randint(keys[2], (SMALL_TOTAL,), 0, 1000), jax.random.fold_in(keys[2], 1), 0, 999).astype(jnp.int32),
        "large_steps": touch_ends(jax.random.randint(keys[3], (LARGE_TOTAL,), 0, 1000), jax.random.fold_in(keys[3], 1), 0, 999).astype(jnp.int32),
        "live_counts": draw_live_counts(jax.random.fold_in(keys[25], 71), 0),
        "small_cotangent": bell_draw_with(keys[5], (SMALL_TOTAL, SMALL_SIDE, SMALL_SIDE, CHANNELS), 1.0, 6.0, ((0, 16), (3, 2)), (0, 3, 16, 2.0)),
        "large_cotangent": bell_draw_with(keys[6], (LARGE_TOTAL, LARGE_SIDE, LARGE_SIDE, CHANNELS), 1.0, 6.0, ((0, 16), (3, 2)), (0, 3, 16, 2.0)),
        "first_conv": bell_draw(keys[7], (CHANNELS, 9 * CHANNELS), (9 * CHANNELS) ** -0.5, 0.125, ((0, 2), (1, 16)), jnp.float32),
        "second_conv": bell_draw(keys[8], (CHANNELS, 9 * CHANNELS), (9 * CHANNELS) ** -0.5, 0.125, ((0, 2), (1, 16)), jnp.float32),
        "time_dense": bell_draw(keys[9], (TIME_WIDTH, CHANNELS), TIME_WIDTH ** -0.5, 0.1875, ((0, 16), (1, 2)), jnp.float32),
        "attn_qkv": bell_draw(keys[10], (CHANNELS, 3 * CHANNELS), CHANNELS ** -0.5, 0.375, ((1, 32),), jnp.float32),
        "attn_proj": bell_draw(keys[11], (CHANNELS, CHANNELS), 4 ** -0.5, 3.0, ((1, 32),), jnp.float32),
        "vectors": draw_vectors(jax.random.fold_in(keys[25], 71), 0),
        "first_conv_mean": draw_first_conv_mean(jax.random.fold_in(keys[25], 71), 0),
        "first_conv_square": draw_first_conv_square(jax.random.fold_in(keys[25], 71), 0),
        "second_conv_mean": draw_second_conv_mean(jax.random.fold_in(keys[25], 71), 0),
        "second_conv_square": draw_second_conv_square(jax.random.fold_in(keys[25], 71), 0),
        "time_dense_mean": draw_time_dense_mean(jax.random.fold_in(keys[25], 71), 0),
        "time_dense_square": draw_time_dense_square(jax.random.fold_in(keys[25], 71), 0),
        "attn_qkv_mean": draw_attn_qkv_mean(jax.random.fold_in(keys[25], 71), 0),
        "attn_qkv_square": draw_attn_qkv_square(jax.random.fold_in(keys[25], 71), 0),
        "attn_proj_mean": draw_attn_proj_mean(jax.random.fold_in(keys[25], 71), 0),
        "attn_proj_square": draw_attn_proj_square(jax.random.fold_in(keys[25], 71), 0),
        "vectors_mean": draw_vectors_mean(jax.random.fold_in(keys[25], 71), 0),
        "vectors_square": draw_vectors_square(jax.random.fold_in(keys[25], 71), 0),
    }


@jax.custom_vjp
def low(v):
    return lax.optimization_barrier(v.astype(jnp.bfloat16)).astype(jnp.float32)

@jax.custom_vjp
def low_back(v):
    return v

def low_keep(v):
    return (low(v), None)

def low_pass(kept, grad):
    return (grad,)

def back_keep(v):
    return (v, None)

def back_low(kept, grad):
    return (low(grad),)
low.defvjp(low_keep, low_pass)
low_back.defvjp(back_keep, back_low)
NORM_EPS = 1e-05
ADAM_ONE = 0.9
ADAM_TWO = 0.999
ADAM_EPS = 1e-08
DECAY = 0.01
RATE_CONV = 0.08
RATE_TIME = 0.1
RATE_QKV = 0.2
RATE_PROJ = 1.0
RATE_VECTOR = 1.5
LOG_PERIOD = math.log(10000.0)
PRECISE = lax.Precision.HIGHEST

def time_features(step_ids, feature_width):
    half_width = feature_width // 2
    frequency = jnp.exp(jnp.arange(half_width, dtype=jnp.float32) * (-LOG_PERIOD / (half_width - 1)))
    angles = step_ids.astype(jnp.float32)[:, None] * frequency[None, :]
    return jnp.concatenate([jnp.sin(angles), jnp.cos(angles)], axis=1)

def group_norm(inputs, gain, shift):
    map_count, height, breadth, channel_count = inputs.shape
    grouped = inputs.reshape(map_count, height * breadth, GROUPS, channel_count // GROUPS)
    center = lax.optimization_barrier(jnp.mean(grouped, axis=(1, 3), keepdims=True))
    spread = lax.optimization_barrier(jnp.mean(jnp.square(grouped - center), axis=(1, 3), keepdims=True))
    normal = ((grouped - center) * lax.rsqrt(spread + NORM_EPS)).reshape(inputs.shape)
    return normal * gain + shift

def conv_apply(inputs, weight):
    channel_count = weight.shape[0]
    kernel = weight.reshape(channel_count, 3, 3, channel_count).transpose(1, 2, 0, 3)
    return lax.conv_general_dilated(inputs, kernel, (1, 1), 'SAME', dimension_numbers=('NHWC', 'HWIO', 'NHWC'), precision=PRECISE)

def attend_one(triple):
    queries, key_rows, values = triple
    score_scale = 1.0 / math.sqrt(queries.shape[-1])
    scores = low_back(jnp.dot(queries, key_rows.T, precision=PRECISE) * score_scale)
    row_max = lax.optimization_barrier(jnp.max(scores, axis=1, keepdims=True))
    exponent = jnp.exp(scores - row_max)
    softmax_probs = exponent / lax.optimization_barrier(jnp.sum(exponent, axis=1, keepdims=True))
    return jnp.dot(low(softmax_probs), values, precision=PRECISE)

def block_apply(weights, batch):
    kernel_one, kernel_two, time_weight, qkv_weight, proj_weight, vector = weights
    inputs, time_feats = batch
    channel_count = inputs.shape[3]
    act_one = low(jax.nn.silu(group_norm(inputs, vector[0], vector[1])))
    time_add = jnp.dot(time_feats, time_weight, precision=PRECISE) + vector[7]
    hidden = low_back(conv_apply(act_one, kernel_one) + vector[6] + time_add[:, None, None, :])
    act_two = low(jax.nn.silu(group_norm(hidden, vector[2], vector[3])))
    block_sum = inputs + low_back(conv_apply(act_two, kernel_two) + vector[8])
    normed = low(low_back(group_norm(block_sum, vector[4], vector[5])))
    flat_rows = normed.reshape(normed.shape[0], -1, channel_count)
    projected = jnp.einsum('npc,cd->npd', flat_rows, qkv_weight, precision=PRECISE)
    queries = low(low_back(projected[..., :channel_count] + vector[9]))
    key_rows = low(low_back(projected[..., channel_count:2 * channel_count]))
    values = low(low_back(projected[..., 2 * channel_count:] + vector[10]))
    mixture = low(low_back(lax.map(jax.checkpoint(attend_one), (queries, key_rows, values))))
    branch = low(jnp.einsum('npc,cd->npd', mixture, proj_weight, precision=PRECISE) + vector[11])
    return block_sum + branch.reshape(block_sum.shape)

def forward(masters, inputs, feats_pair):
    weights = tuple((low(master) for master in masters))
    results = []
    per_block = N_WIDE // 4
    for maps, time_feats in zip(inputs, feats_pair):
        blocked = maps.reshape((-1, per_block) + maps.shape[1:])
        feat_block = time_feats.reshape(-1, per_block, time_feats.shape[1])
        mapped = lax.map(jax.checkpoint(partial(block_apply, weights)), (blocked, feat_block))
        results.append(mapped.reshape(maps.shape))
    return tuple(results)

def live_mask(count_column, slot_count, total):
    slot_ids = jnp.arange(total, dtype=jnp.int32) % slot_count
    owner = jnp.arange(total, dtype=jnp.int32) // slot_count
    return (slot_ids < count_column[owner]).astype(jnp.float32)

def adam_step(weight, grad, mean, square, rate, decay):
    mean_new = ADAM_ONE * mean + (1.0 - ADAM_ONE) * grad
    square_new = ADAM_TWO * square + (1.0 - ADAM_TWO) * grad * grad
    first_fix = mean_new / (1.0 - ADAM_ONE ** STEP_NUMBER)
    second_fix = square_new / (1.0 - ADAM_TWO ** STEP_NUMBER)
    weight_new = weight - rate * (first_fix / (jnp.sqrt(second_fix) + ADAM_EPS) + decay * weight)
    return (weight_new, mean_new, square_new)

def reference(small_maps, large_maps, small_steps, large_steps, live_counts, small_cotangent, large_cotangent, first_conv, second_conv, time_dense, attn_qkv, attn_proj, vectors, first_conv_mean, first_conv_square, second_conv_mean, second_conv_square, time_dense_mean, time_dense_square, attn_qkv_mean, attn_qkv_square, attn_proj_mean, attn_proj_square, vectors_mean, vectors_square):
    small_live = live_mask(live_counts[:, 0], SMALL_SLOTS, SMALL_TOTAL)
    large_live = live_mask(live_counts[:, 1], LARGE_SLOTS, LARGE_TOTAL)
    feature_width = time_dense.shape[0]
    feats_pair = (low(jax.nn.silu(time_features(small_steps, feature_width))), low(jax.nn.silu(time_features(large_steps, feature_width))))
    masters = (first_conv, second_conv, time_dense, attn_qkv, attn_proj, vectors)
    inputs = (small_maps.astype(jnp.float32), large_maps.astype(jnp.float32))
    outputs, pull = jax.vjp(partial(forward, feats_pair=feats_pair), masters, inputs)
    small_grad_in = small_cotangent.astype(jnp.float32) * small_live[:, None, None, None]
    large_grad_in = large_cotangent.astype(jnp.float32) * large_live[:, None, None, None]
    master_grads, input_grads = pull((small_grad_in, large_grad_in))
    small_out = (outputs[0] * small_live[:, None, None, None]).astype(jnp.bfloat16)
    large_out = (outputs[1] * large_live[:, None, None, None]).astype(jnp.bfloat16)
    conv_one_new = adam_step(first_conv, master_grads[0], first_conv_mean, first_conv_square, RATE_CONV, DECAY)
    conv_two_new = adam_step(second_conv, master_grads[1], second_conv_mean, second_conv_square, RATE_CONV, DECAY)
    time_new = adam_step(time_dense, master_grads[2], time_dense_mean, time_dense_square, RATE_TIME, DECAY)
    qkv_new = adam_step(attn_qkv, master_grads[3], attn_qkv_mean, attn_qkv_square, RATE_QKV, DECAY)
    proj_new = adam_step(attn_proj, master_grads[4], attn_proj_mean, attn_proj_square, RATE_PROJ, DECAY)
    vector_new = adam_step(vectors, master_grads[5], vectors_mean, vectors_square, RATE_VECTOR, 0.0)
    return (small_out, large_out, input_grads[0], input_grads[1], conv_one_new[0], conv_one_new[1], conv_one_new[2], conv_two_new[0], conv_two_new[1], conv_two_new[2], time_new[0], time_new[1], time_new[2], qkv_new[0], qkv_new[1], qkv_new[2], proj_new[0], proj_new[1], proj_new[2], vector_new[0], vector_new[1], vector_new[2])
```

```python
import functools
import math

import jax
import jax.numpy as jnp
from jax import lax
from jax.experimental import pallas as pl
from jax.experimental.pallas import tpu as pltpu
from jax.sharding import PartitionSpec as P

GROUPS = 32
STEP_NUMBER = 10
NORM_EPS = 1e-05
ADAM_ONE = 0.9
ADAM_TWO = 0.999
ADAM_EPS = 1e-08
DECAY = 0.01
RATE_CONV = 0.08
RATE_TIME = 0.1
RATE_QKV = 0.2
RATE_PROJ = 1.0
RATE_VECTOR = 1.5
LOG_PERIOD = math.log(10000.0)
PRECISE = lax.Precision.HIGHEST
BF = jnp.bfloat16
F32 = jnp.float32
BLOCK_ROWS = 1024
VMEM_LIMIT = 60 * 2**20
NT = (((1,), (1,)), ((), ()))
TN = (((0,), (0,)), ((), ()))


def dot(a, b, dims=(((1,), (0,)), ((), ()))):
    return lax.dot_general(a, b, dims, preferred_element_type=F32)


def swap_narrow(x):
    return lax.ppermute(x, "narrow", [(0, 1), (1, 0)])


def swap_wide(x, bit):
    count = lax.axis_size("wide")
    return lax.ppermute(x, "wide", [(i, i ^ (1 << bit)) for i in range(count)])


def swap(x, step):
    return swap_narrow(x) if step == "n" else swap_wide(x, step)


def gather_order():
    bits = (lax.axis_size("wide") - 1).bit_length()
    return ["n"] + list(range(bits - 2, 0, -1)) + [bits - 1, 0] if bits > 1 else ["n", 0]


def gather_slots(block, order):
    slots = block[None]
    for step in order:
        slots = jnp.concatenate([slots, swap(slots, step)], axis=0)
    return slots


def slot_of(order, delta_wide, delta_narrow):
    slot = 0
    for i, step in enumerate(order):
        bit = delta_narrow if step == "n" else (delta_wide >> step) & 1
        slot = slot + (bit << i)
    return slot


def scatter_slots(slots, order):
    for step in reversed(order):
        half = slots.shape[0] // 2
        arrived = swap(slots[half:].astype(BF), step)
        slots = slots[:half].astype(F32) + arrived.astype(F32)
    return slots[0]


def slot_table(order):
    here_wide = lax.axis_index("wide")
    here_narrow = lax.axis_index("narrow")
    wide = jnp.arange(lax.axis_size("wide"), dtype=jnp.int32)[:, None] ^ here_wide
    narrow = jnp.arange(lax.axis_size("narrow"), dtype=jnp.int32)[None, :] ^ here_narrow
    return slot_of(order, wide, narrow).reshape(-1)


def device_table(order):
    here_wide = lax.axis_index("wide")
    here_narrow = lax.axis_index("narrow")
    slots = jnp.arange(lax.axis_size("wide") * lax.axis_size("narrow"), dtype=jnp.int32)
    wide = jnp.zeros_like(slots)
    narrow = jnp.zeros_like(slots)
    for i, step in enumerate(order):
        bit = (slots >> i) & 1
        if step == "n":
            narrow = narrow + bit
        else:
            wide = wide + (bit << step)
    return (wide ^ here_wide) * 2 + (narrow ^ here_narrow)


def unpack_kernel(table, src, *outs, parts):
    def body(place, carry):
        slot = table[place]
        for out, (start, stop, joined) in zip(outs, parts):
            block = src[slot, start:stop, :]
            if joined:
                lanes = pl.ds(pl.multiple_of((place & 1) * 128, 128), 128)
                out[place >> 1, :, lanes] = block
            else:
                out[place] = block
        return carry

    lax.fori_loop(0, src.shape[0], body, 0)


def run_unpack(slots, table, parts):
    count, _, width = slots.shape
    shapes = []
    for start, stop, joined in parts:
        shape = (count // 2, stop - start, 256) if joined else (count, stop - start, width)
        shapes.append(jax.ShapeDtypeStruct(shape, slots.dtype))
    return pl.pallas_call(
        functools.partial(unpack_kernel, parts=parts),
        in_specs=[
            pl.BlockSpec(memory_space=pltpu.SMEM),
            pl.BlockSpec(memory_space=pltpu.VMEM),
        ],
        out_specs=[pl.BlockSpec(memory_space=pltpu.VMEM)] * len(parts),
        out_shape=shapes,
        compiler_params=pltpu.CompilerParams(vmem_limit_bytes=VMEM_LIMIT),
    )(table, slots)


def pack_kernel(table, *refs, joined):
    ins = refs[: len(joined)]
    outs = refs[len(joined) :]

    def body(slot, carry):
        place = table[slot]
        for src, out, lanes_joined in zip(ins, outs, joined):
            if lanes_joined:
                lanes = pl.ds(pl.multiple_of((place & 1) * 128, 128), 128)
                out[slot] = src[place >> 1, :, lanes].astype(BF)
            else:
                out[slot] = src[place].astype(BF)
        return carry

    lax.fori_loop(0, outs[0].shape[0], body, 0)


def run_pack(arrays, table, joined):
    shapes = []
    for array, halves in zip(arrays, joined):
        count, rows, width = array.shape
        shape = (count * 2, rows, 128) if halves else (count, rows, width)
        shapes.append(jax.ShapeDtypeStruct(shape, BF))
    return pl.pallas_call(
        functools.partial(pack_kernel, joined=joined),
        in_specs=[pl.BlockSpec(memory_space=pltpu.SMEM)]
        + [pl.BlockSpec(memory_space=pltpu.VMEM)] * len(arrays),
        out_specs=[pl.BlockSpec(memory_space=pltpu.VMEM)] * len(arrays),
        out_shape=shapes,
        compiler_params=pltpu.CompilerParams(vmem_limit_bytes=VMEM_LIMIT),
    )(table, *arrays)


def group_total(s):
    lane = lax.broadcasted_iota(jnp.int32, s.shape, 1)
    width = s.shape[1]
    for k in (1, 2, 4):
        s = s + jnp.where((lane & k) == 0, pltpu.roll(s, width - k, 1), pltpu.roll(s, k, 1))
    return s


def rows_sum(z):
    return jnp.sum(z, axis=0, keepdims=True)


def stack_rows(rows):
    return rows[0] if len(rows) == 1 else jnp.concatenate(rows, axis=0)


def norm_stats(get, n, pixels):
    scale = 1.0 / (8 * pixels)
    mean = group_total(stack_rows([rows_sum(get(m)) for m in range(n)])) * scale
    spread = []
    for m in range(n):
        centered = get(m) - mean[m : m + 1, :]
        spread.append(rows_sum(centered * centered))
    inverse = lax.rsqrt(group_total(stack_rows(spread)) * scale + NORM_EPS)
    return mean, inverse


def sigmoid(v):
    return 1.0 / (1.0 + jnp.exp(-v))


def shift_store(dst, m, value, height, breadth, forward):
    pixels = height * breadth
    channels = value.shape[1]
    column = lax.broadcasted_iota(jnp.int32, value.shape, 0) & (breadth - 1)
    before = jnp.where(column == 0, 0.0, pltpu.roll(value, 1, 0)).astype(BF)
    after = jnp.where(column == breadth - 1, 0.0, pltpu.roll(value, pixels - 1, 0)).astype(BF)
    lo, hi = (before, after) if forward else (after, before)
    rows = slice(breadth, breadth + pixels)
    dst[m, rows, 0:channels] = lo
    dst[m, rows, channels : 2 * channels] = value.astype(BF)
    dst[m, rows, 2 * channels :] = hi


def zero_edges(dst, height, breadth):
    n, rows, width = dst.shape
    edge = jnp.zeros((n, breadth, width), BF)
    dst[:, 0:breadth, :] = edge
    dst[:, rows - breadth :, :] = edge


def join_halves(place, own, other, dst):
    rows = dst.shape[0]

    @pl.when(place == 0)
    def _():
        dst[:, 0:128] = own[...].reshape(rows, 128)
        dst[:, 128:256] = other[...].reshape(rows, 128)

    @pl.when(place != 0)
    def _():
        dst[:, 0:128] = other[...].reshape(rows, 128)
        dst[:, 128:256] = own[...].reshape(rows, 128)


def conv_forward(shifted, kt, n, height, breadth):
    pixels = height * breadth
    total = None
    for p in range(3):
        for q in range(3):
            tap = 3 * p + q
            window = shifted[:, p * breadth : p * breadth + pixels, q * 256 : (q + 1) * 256]
            part = dot(window.reshape(n * pixels, 256), kt[tap * 256 : (tap + 1) * 256, :], NT)
            total = part if total is None else total + part
    return total


def grad_window(shifted, p, n, height, breadth):
    pixels = height * breadth
    start = (2 - p) * breadth
    return shifted[:, start : start + pixels, :].reshape(n * pixels, 768)


def conv_back(shifted, kt, n, height, breadth):
    window = jnp.concatenate(
        [grad_window(shifted, p, n, height, breadth) for p in range(3)], axis=1
    )
    return dot(window, kt[...])


def conv_weight(shifted, act, acc, n, height, breadth):
    for p in range(3):
        window = grad_window(shifted, p, n, height, breadth)
        acc[p * 768 : (p + 1) * 768, :] += dot(window, act, TN)


def first_kernel(sc, xa, xb, kt, vec, c1_o, u1_o, zh_o, inv_o, x_s, shifted, *, n, height, breadth):
    pixels = height * breadth
    join_halves(sc[0], xa, xb, x_s)

    @pl.when(pl.program_id(0) == 0)
    def _():
        zero_edges(shifted, height, breadth)

    def get(m):
        return x_s[m * pixels : (m + 1) * pixels, :].astype(F32)

    mean, inverse = norm_stats(get, n, pixels)
    inv_o[0, 0:n, :] = inverse
    for m in range(n):
        rows = slice(m * pixels, (m + 1) * pixels)
        zh = (get(m) - mean[m : m + 1, :]) * inverse[m : m + 1, :]
        zh_o[rows, :] = zh.astype(BF)
        a1 = zh * vec[0:1, :] + vec[1:2, :]
        u1 = a1 * sigmoid(a1)
        u1_o[rows, :] = u1.astype(BF)
        shift_store(shifted, m, u1, height, breadth, True)
    c1_o[...] = conv_forward(shifted, kt, n, height, breadth)


def middle_kernel(
    sc, c1, te, xa, xb, ga, gb, kt, wqkv, wo, vec, aq_i, ao_i, av_i,
    u2_o, zh2_o, inv2_o, gc2_o, mine_o, send_o, aq, ao, av,
    x_s, gy_s, shifted, h_s, zh3_s, hn_s, qkv_s, o_s, go_s, j_s, gk_s, gv_s,
    *, n, height, breadth, own, which, first_call,
):
    pixels = height * breadth
    total = n * pixels
    step = pl.program_id(0)
    join_halves(sc[0], xa, xb, x_s)
    join_halves(sc[0], ga, gb, gy_s)

    @pl.when(step == 0)
    def _():
        zero_edges(shifted, height, breadth)
        aq[...] = jnp.zeros_like(aq) if first_call else aq_i[...]
        ao[...] = jnp.zeros_like(ao) if first_call else ao_i[...]
        av[...] = jnp.zeros_like(av) if first_call else av_i[...]

    live = []
    for m in range(n):
        rows = slice(m * pixels, (m + 1) * pixels)
        slot = sc[0] * own + step * n + m
        live.append((slot < sc[1 + which]).astype(F32))
        gy_s[rows, :] = (gy_s[rows, :].astype(F32) * live[m]).astype(BF)

    def get_c1(m):
        return c1[m * pixels : (m + 1) * pixels, :] + te[0, m : m + 1, :]

    mean, inverse = norm_stats(get_c1, n, pixels)
    inv2_o[0, 0:n, :] = inverse
    for m in range(n):
        rows = slice(m * pixels, (m + 1) * pixels)
        zh = (get_c1(m) - mean[m : m + 1, :]) * inverse[m : m + 1, :]
        zh2_o[rows, :] = zh.astype(BF)
        a2 = zh * vec[2:3, :] + vec[3:4, :]
        u2 = a2 * sigmoid(a2)
        u2_o[rows, :] = u2.astype(BF)
        shift_store(shifted, m, u2, height, breadth, True)
    h_s[...] = (
        conv_forward(shifted, kt, n, height, breadth) + vec[8:9, :] + x_s[...].astype(F32)
    )

    def get_h(m):
        return h_s[m * pixels : (m + 1) * pixels, :]

    mean, inverse3 = norm_stats(get_h, n, pixels)
    for m in range(n):
        rows = slice(m * pixels, (m + 1) * pixels)
        zh = (get_h(m) - mean[m : m + 1, :]) * inverse3[m : m + 1, :]
        zh3_s[rows, :] = zh
        hn_s[rows, :] = (zh * vec[4:5, :] + vec[5:6, :]).astype(BF)
    for part in range(3):
        lanes = slice(part * 256, (part + 1) * 256)
        projected = dot(hn_s[...], wqkv[lanes, :], NT)
        if part == 0:
            projected = projected + vec[9:10, :]
        if part == 2:
            projected = projected + vec[10:11, :]
        qkv_s[:, lanes] = projected.astype(BF)
    go_s[...] = dot(gy_s[...], wo[...]).astype(BF)

    chunk = min(pixels, 256)
    scale = 1.0 / math.sqrt(256)
    for m in range(n):
        rows = slice(m * pixels, (m + 1) * pixels)
        keys = qkv_s[rows, 256:512]
        values = qkv_s[rows, 512:768]
        for c in range(pixels // chunk):
            part = slice(m * pixels + c * chunk, m * pixels + (c + 1) * chunk)
            queries = qkv_s[part, 0:256]
            scores = dot(queries, keys, NT)
            top = jnp.max(scores, axis=1, keepdims=True)
            exponent = jnp.exp((scores - top) * scale)
            probs = exponent * (1.0 / jnp.sum(exponent, axis=1, keepdims=True))
            low = probs.astype(BF)
            o_s[part, :] = dot(low, values).astype(BF)
            grad_o = go_s[part, :]
            grad_p = dot(grad_o, values, NT)
            inner = jnp.sum(probs * grad_p, axis=1, keepdims=True)
            grad_s = (probs * (grad_p - inner)).astype(BF)
            j_s[part, 0:256] = (dot(grad_s, keys) * scale).astype(BF)
            grad_k = dot(grad_s, queries, TN)
            grad_v = dot(low, grad_o, TN)
            if c == 0:
                gk_s[...] = grad_k
                gv_s[...] = grad_v
            else:
                gk_s[...] += grad_k
                gv_s[...] += grad_v
        j_s[rows, 256:512] = (gk_s[...] * scale).astype(BF)
        j_s[rows, 512:768] = gv_s[...].astype(BF)

    branch = (dot(o_s[...], wo[...], NT) + vec[11:12, :]).astype(BF).astype(F32)
    for m in range(n):
        rows = slice(m * pixels, (m + 1) * pixels)
        out = ((h_s[rows, :] + branch[rows, :]) * live[m]).astype(BF)

        @pl.when(sc[0] == 0)
        def _(out=out, m=m):
            mine_o[m] = out[:, 0:128].reshape(height, breadth, 128)
            send_o[m] = out[:, 128:256].reshape(height, breadth, 128)

        @pl.when(sc[0] != 0)
        def _(out=out, m=m):
            mine_o[m] = out[:, 128:256].reshape(height, breadth, 128)
            send_o[m] = out[:, 0:128].reshape(height, breadth, 128)

    ao[...] += dot(gy_s[...], o_s[...], TN)
    aq[...] += dot(j_s[...], hn_s[...], TN)
    av[9:10, :] += rows_sum(j_s[:, 0:256].astype(F32))
    av[10:11, :] += rows_sum(j_s[:, 512:768].astype(F32))
    av[11:12, :] += rows_sum(gy_s[...].astype(F32))
    grad_hn = dot(j_s[...], wqkv[...]).astype(BF)

    gain = vec[4:5, :]
    one = []
    two = []
    for m in range(n):
        rows = slice(m * pixels, (m + 1) * pixels)
        d = grad_hn[rows, :].astype(F32)
        one.append(rows_sum(d))
        two.append(rows_sum(d * zh3_s[rows, :]))
    one = stack_rows(one)
    two = stack_rows(two)
    av[4:5, :] += rows_sum(two)
    av[5:6, :] += rows_sum(one)
    mean_one = group_total(one * gain) * (1.0 / (8 * pixels))
    mean_two = group_total(two * gain) * (1.0 / (8 * pixels))
    bias = jnp.zeros((1, 256), F32)
    for m in range(n):
        rows = slice(m * pixels, (m + 1) * pixels)
        d = grad_hn[rows, :].astype(F32)
        gz = inverse3[m : m + 1, :] * (
            d * gain - mean_one[m : m + 1, :] - zh3_s[rows, :] * mean_two[m : m + 1, :]
        )
        low = (gz + gy_s[rows, :].astype(F32)).astype(BF)
        gc2_o[rows, :] = low
        bias = bias + rows_sum(low.astype(F32))
    av[8:9, :] += bias


def norm_silu_back(grad_act, zh_ref, inv_ref, gain, shift, n, pixels):
    one = []
    two = []
    grads = []
    for m in range(n):
        rows = slice(m * pixels, (m + 1) * pixels)
        zh = zh_ref[rows, :].astype(F32)
        a = zh * gain + shift
        s = sigmoid(a)
        d = grad_act[rows, :] * (s * (1.0 + a * (1.0 - s)))
        grads.append(d)
        one.append(rows_sum(d))
        two.append(rows_sum(d * zh))
    one = stack_rows(one)
    two = stack_rows(two)
    mean_one = group_total(one * gain) * (1.0 / (8 * pixels))
    mean_two = group_total(two * gain) * (1.0 / (8 * pixels))
    result = []
    for m in range(n):
        rows = slice(m * pixels, (m + 1) * pixels)
        zh = zh_ref[rows, :].astype(F32)
        result.append(
            inv_ref[0, m : m + 1, :]
            * (grads[m] * gain - mean_one[m : m + 1, :] - zh * mean_two[m : m + 1, :])
        )
    return result, rows_sum(one), rows_sum(two)


def second_back_kernel(
    sc, gc2, u2, zh2, inv2, kt, vec, ak_i, av_i,
    gc1_o, ge_o, ak, av, shifted, *, n, height, breadth, first_call,
):
    pixels = height * breadth

    @pl.when(pl.program_id(0) == 0)
    def _():
        zero_edges(shifted, height, breadth)
        ak[...] = jnp.zeros_like(ak) if first_call else ak_i[...]
        av[...] = jnp.zeros_like(av) if first_call else av_i[...]

    for m in range(n):
        rows = slice(m * pixels, (m + 1) * pixels)
        shift_store(shifted, m, gc2[rows, :].astype(F32), height, breadth, False)
    grad_act = conv_back(shifted, kt, n, height, breadth)
    conv_weight(shifted, u2[...], ak, n, height, breadth)
    grads, one, two = norm_silu_back(grad_act, zh2, inv2, vec[2:3, :], vec[3:4, :], n, pixels)
    av[2:3, :] += two
    av[3:4, :] += one
    for m in range(n):
        rows = slice(m * pixels, (m + 1) * pixels)
        low = grads[m].astype(BF)
        gc1_o[rows, :] = low
        ge = rows_sum(low.astype(F32))
        ge_o[0, m : m + 1, :] = ge
        av[6:7, :] += ge
        av[7:8, :] += ge


def first_weight_kernel(sc, gc1, u1, ak_i, ak, shifted, *, n, height, breadth, first_call):
    pixels = height * breadth

    @pl.when(pl.program_id(0) == 0)
    def _():
        zero_edges(shifted, height, breadth)
        ak[...] = jnp.zeros_like(ak) if first_call else ak_i[...]

    for m in range(n):
        rows = slice(m * pixels, (m + 1) * pixels)
        shift_store(shifted, m, gc1[rows, :].astype(F32), height, breadth, False)
    conv_weight(shifted, u1[...], ak, n, height, breadth)


def first_back_kernel(
    sc, gc1, zh1, inv1, gc2, kt, vec, av_i, mine_o, send_o, av, shifted,
    *, n, height, breadth, first_call,
):
    pixels = height * breadth

    @pl.when(pl.program_id(0) == 0)
    def _():
        zero_edges(shifted, height, breadth)
        av[...] = jnp.zeros_like(av) if first_call else av_i[...]

    for m in range(n):
        rows = slice(m * pixels, (m + 1) * pixels)
        shift_store(shifted, m, gc1[rows, :].astype(F32), height, breadth, False)
    grad_act = conv_back(shifted, kt, n, height, breadth)
    grads, one, two = norm_silu_back(grad_act, zh1, inv1, vec[0:1, :], vec[1:2, :], n, pixels)
    av[0:1, :] += two
    av[1:2, :] += one
    for m in range(n):
        rows = slice(m * pixels, (m + 1) * pixels)
        grad = grads[m] + gc2[rows, :].astype(F32)

        @pl.when(sc[0] == 0)
        def _(grad=grad, m=m):
            mine_o[m] = grad[:, 0:128].reshape(height, breadth, 128)
            send_o[m] = grad[:, 128:256].astype(BF).reshape(height, breadth, 128)

        @pl.when(sc[0] != 0)
        def _(grad=grad, m=m):
            mine_o[m] = grad[:, 128:256].reshape(height, breadth, 128)
            send_o[m] = grad[:, 0:128].astype(BF).reshape(height, breadth, 128)


class Group:
    def __init__(self, shape, which):
        self.maps, self.height, self.breadth, self.half = shape
        self.which = which
        self.own = self.maps // 2
        self.pixels = self.height * self.breadth
        self.n = max(1, min(self.own, BLOCK_ROWS // self.pixels))
        self.steps = self.own // self.n
        self.rows = self.n * self.pixels
        self.all_rows = self.own * self.pixels
        self.params = dict(n=self.n, height=self.height, breadth=self.breadth)

    def row_spec(self):
        return pl.BlockSpec((self.rows, 256), lambda i, sc: (i, 0))

    def row_shape(self, dtype):
        return jax.ShapeDtypeStruct((self.all_rows, 256), dtype)

    def map_spec(self, placed):
        steps = self.steps
        shape = (self.n, self.height, self.breadth, 128)
        if placed:
            return pl.BlockSpec(shape, lambda i, sc: (sc[0] * steps + i, 0, 0, 0))
        return pl.BlockSpec(shape, lambda i, sc: (i, 0, 0, 0))

    def map_shape(self, placed, dtype):
        count = self.maps if placed else self.own
        return jax.ShapeDtypeStruct((count, self.height, self.breadth, 128), dtype)

    def stat_spec(self):
        return pl.BlockSpec((1, 8, 256), lambda i, sc: (i, 0, 0))

    def stat_shape(self):
        return jax.ShapeDtypeStruct((self.steps, 8, 256), F32)

    def shifted(self):
        return pltpu.VMEM((self.n, (self.height + 2) * self.breadth, 768), BF)

    def call(self, body, in_specs, out_specs, out_shape, scratch, flops):
        return pl.pallas_call(
            body,
            grid_spec=pltpu.PrefetchScalarGridSpec(
                num_scalar_prefetch=1,
                grid=(self.steps,),
                in_specs=in_specs,
                out_specs=out_specs,
                scratch_shapes=scratch,
            ),
            out_shape=out_shape,
            compiler_params=pltpu.CompilerParams(vmem_limit_bytes=VMEM_LIMIT),
            cost_estimate=pl.CostEstimate(
                flops=flops, bytes_accessed=self.all_rows * 256 * 8, transcendentals=0
            ),
        )


def whole(shape):
    zeros = (0,) * len(shape)
    return pl.BlockSpec(shape, lambda i, sc: zeros)


def run_first(g, sc, x, x_other, kt, vec):
    return g.call(
        functools.partial(first_kernel, **g.params),
        [g.map_spec(True), g.map_spec(False), whole((2304, 256)), whole((16, 256))],
        [g.row_spec(), g.row_spec(), g.row_spec(), g.stat_spec()],
        [g.row_shape(F32), g.row_shape(BF), g.row_shape(BF), g.stat_shape()],
        [pltpu.VMEM((g.rows, 256), BF), g.shifted()],
        2 * g.all_rows * 2304 * 256,
    )(sc, x, x_other, kt, vec)


def run_middle(g, sc, c1, te, x, x_other, gy, gy_other, kt, wqkv, wo, vec, acc, first_call):
    row = g.row_spec()
    big = pltpu.VMEM((g.rows, 256), F32)
    low = pltpu.VMEM((g.rows, 256), BF)
    wide = pltpu.VMEM((g.rows, 768), BF)
    acc_specs = [whole((768, 256)), whole((256, 256)), whole((16, 256))]
    return g.call(
        functools.partial(
            middle_kernel, own=g.own, which=g.which, first_call=first_call, **g.params
        ),
        [
            row, pl.BlockSpec((1, g.n, 256), lambda i, sc: (i, 0, 0)),
            g.map_spec(True), g.map_spec(False), g.map_spec(True), g.map_spec(False),
            whole((2304, 256)), whole((768, 256)), whole((256, 256)), whole((16, 256)),
        ] + acc_specs,
        [row, row, g.stat_spec(), row, g.map_spec(True), g.map_spec(False)] + acc_specs,
        [
            g.row_shape(BF), g.row_shape(BF), g.stat_shape(), g.row_shape(BF),
            g.map_shape(True, BF), g.map_shape(False, BF),
            jax.ShapeDtypeStruct((768, 256), F32), jax.ShapeDtypeStruct((256, 256), F32),
            jax.ShapeDtypeStruct((16, 256), F32),
        ],
        [
            low, low, g.shifted(), big, big, low, wide, low, low, wide,
            pltpu.VMEM((g.pixels, 256), F32), pltpu.VMEM((g.pixels, 256), F32),
        ],
        2 * g.all_rows * 256 * (2304 + 256 * 12 + 6 * g.pixels),
    )(sc, c1, te, x, x_other, gy, gy_other, kt, wqkv, wo, vec, *acc)


def run_second_back(g, sc, gc2, u2, zh2, inv2, kt, vec, acc, first_call):
    row = g.row_spec()
    acc_specs = [whole((2304, 256)), whole((16, 256))]
    return g.call(
        functools.partial(second_back_kernel, first_call=first_call, **g.params),
        [row, row, row, g.stat_spec(), whole((2304, 256)), whole((16, 256))] + acc_specs,
        [row, pl.BlockSpec((1, g.n, 256), lambda i, sc: (i, 0, 0))] + acc_specs,
        [
            g.row_shape(BF), jax.ShapeDtypeStruct((g.steps, g.n, 256), F32),
            jax.ShapeDtypeStruct((2304, 256), F32), jax.ShapeDtypeStruct((16, 256), F32),
        ],
        [g.shifted()],
        4 * g.all_rows * 256 * 2304,
    )(sc, gc2, u2, zh2, inv2, kt, vec, *acc)


def run_first_weight(g, sc, gc1, u1, acc, first_call):
    row = g.row_spec()
    return g.call(
        functools.partial(first_weight_kernel, first_call=first_call, **g.params),
        [row, row, whole((2304, 256))],
        whole((2304, 256)),
        jax.ShapeDtypeStruct((2304, 256), F32),
        [g.shifted()],
        2 * g.all_rows * 256 * 2304,
    )(sc, gc1, u1, acc)


def run_first_back(g, sc, gc1, zh1, inv1, gc2, kt, vec, acc, first_call):
    row = g.row_spec()
    return g.call(
        functools.partial(first_back_kernel, first_call=first_call, **g.params),
        [row, row, g.stat_spec(), row, whole((2304, 256)), whole((16, 256)), whole((16, 256))],
        [g.map_spec(True), g.map_spec(False), whole((16, 256))],
        [g.map_shape(True, F32), g.map_shape(False, BF), jax.ShapeDtypeStruct((16, 256), F32)],
        [g.shifted()],
        2 * g.all_rows * 256 * 2304,
    )(sc, gc1, zh1, inv1, gc2, kt, vec, acc)


def features(steps, index, half_width):
    frequency = jnp.exp(
        (index % half_width).astype(F32) * (-LOG_PERIOD / (half_width - 1))
    )
    angles = steps.astype(F32)[:, None] * frequency[None, :]
    return jax.nn.silu(
        jnp.where(index[None, :] < half_width, jnp.sin(angles), jnp.cos(angles))
    ).astype(BF)


def adam_step(weight, grad, mean, square, rate, decay):
    mean_new = ADAM_ONE * mean + (1.0 - ADAM_ONE) * grad
    square_new = ADAM_TWO * square + (1.0 - ADAM_TWO) * grad * grad
    first_fix = mean_new / (1.0 - ADAM_ONE**STEP_NUMBER)
    second_fix = square_new / (1.0 - ADAM_TWO**STEP_NUMBER)
    weight_new = weight - rate * (first_fix / (jnp.sqrt(second_fix) + ADAM_EPS) + decay * weight)
    return (weight_new, mean_new, square_new)


def other_part(x, here):
    own = x.shape[0] // 2
    part = lax.dynamic_slice_in_dim(x, (1 - here) * own, own, 0)
    return swap_narrow(part)


def put_part(full, arrived, here):
    own = arrived.shape[0]
    return lax.dynamic_update_slice_in_dim(
        full, arrived.astype(full.dtype), (1 - here) * own, 0
    )


def per_device(
    small_maps, large_maps, small_steps, large_steps, live_counts,
    small_cotangent, large_cotangent,
    first_conv, second_conv, time_dense, attn_qkv, attn_proj, vectors,
    first_conv_mean, first_conv_square, second_conv_mean, second_conv_square,
    time_dense_mean, time_dense_square, attn_qkv_mean, attn_qkv_square,
    attn_proj_mean, attn_proj_square, vectors_mean, vectors_square,
):
    n_wide = lax.axis_size("wide")
    here = lax.axis_index("narrow")
    here_wide = lax.axis_index("wide")
    channels = attn_qkv.shape[0]
    half = first_conv.shape[0]
    cols = first_conv.shape[1]
    time_rows = time_dense.shape[0]
    feature_width = time_rows * n_wide
    qcols = attn_qkv.shape[1]
    pcols = attn_proj.shape[1]
    vcols = vectors.shape[1]
    order = gather_order()
    small = Group(small_maps.shape, 0)
    large = Group(large_maps.shape, 1)
    sc = jnp.concatenate([here[None].astype(jnp.int32), live_counts[0]])

    xs = other_part(small_maps, here)
    vec_rows = jnp.pad(
        vectors.astype(BF).T, ((0, 16 - vcols), (0, 128 - vectors.shape[0]))
    )
    g_one = gather_slots(jnp.concatenate([first_conv.astype(BF).T, vec_rows], axis=0), order)
    g_two = gather_slots(
        jnp.concatenate([second_conv.astype(BF).T, time_dense.astype(BF)], axis=0), order
    )
    g_three = gather_slots(
        jnp.concatenate([attn_qkv.astype(BF).T, attn_proj.astype(BF).T], axis=0), order
    )
    table = slot_table(order)
    kt_one, vec = run_unpack(
        g_one, table, ((0, cols, True), (cols, cols + 16, False))
    )
    kt_one = kt_one.reshape(n_wide * cols, 2 * half)
    vec = vec[:, :vcols, :16].reshape(channels, 16).T.astype(F32)
    kt_two, wt = run_unpack(
        g_two, table, ((0, cols, True), (cols, cols + time_rows, True))
    )
    kt_two = kt_two.reshape(n_wide * cols, 2 * half)
    wt = wt.reshape(feature_width, 2 * half)
    (attn,) = run_unpack(g_three, table, ((0, qcols + pcols, False),))
    wqkv = attn[:, :qcols].reshape(3 * channels, channels)
    wo = attn[:, qcols:].reshape(channels, channels)

    own_small = lax.dynamic_slice_in_dim(small_steps, here * small.own, small.own, 0)
    own_large = lax.dynamic_slice_in_dim(large_steps, here * large.own, large.own, 0)
    own_steps = jnp.concatenate([own_small, own_large])
    te = (
        jnp.dot(
            features(own_steps, jnp.arange(feature_width), feature_width // 2),
            wt,
            preferred_element_type=F32,
        )
        + vec[7]
        + vec[6]
    )
    te_small = te[: small.own].reshape(small.steps, small.n, channels)
    te_large = te[small.own :].reshape(large.steps, large.n, channels)

    gs = other_part(small_cotangent, here)
    xl = other_part(large_maps, here)
    gl = other_part(large_cotangent, here)

    zero_q = jnp.zeros((768, 256), F32)
    zero_o = jnp.zeros((256, 256), F32)
    zero_v = jnp.zeros((16, 256), F32)
    zero_k = jnp.zeros((2304, 256), F32)

    s_c1, s_u1, s_zh1, s_inv1 = run_first(small, sc, small_maps, xs, kt_one, vec)
    (s_u2, s_zh2, s_inv2, s_gc2, s_mine, s_send, aq, ao, av) = run_middle(
        small, sc, s_c1, te_small, small_maps, xs, small_cotangent, gs, kt_two, wqkv, wo, vec,
        (zero_q, zero_o, zero_v), True,
    )
    small_out = put_part(s_mine, swap_narrow(s_send), here)
    l_c1, l_u1, l_zh1, l_inv1 = run_first(large, sc, large_maps, xl, kt_one, vec)
    (l_u2, l_zh2, l_inv2, l_gc2, l_mine, l_send, aq, ao, av) = run_middle(
        large, sc, l_c1, te_large, large_maps, xl, large_cotangent, gl, kt_two, wqkv, wo, vec,
        (aq, ao, av), False,
    )
    large_out = put_part(l_mine, swap_narrow(l_send), here)
    devices = device_table(order)
    grads_three = run_pack(
        (aq.reshape(-1, qcols, 256), ao.reshape(-1, pcols, 256)), devices, (False, False)
    )
    sum_three = scatter_slots(jnp.concatenate(grads_three, axis=1), order)

    s_gc1, s_ge, ak, av = run_second_back(
        small, sc, s_gc2, s_u2, s_zh2, s_inv2, kt_two, vec, (zero_k, av), False
    )
    s_mine, s_send, av = run_first_back(
        small, sc, s_gc1, s_zh1, s_inv1, s_gc2, kt_one, vec, av, False
    )
    small_grad = put_part(s_mine, swap_narrow(s_send), here)
    l_gc1, l_ge, ak, av = run_second_back(
        large, sc, l_gc2, l_u2, l_zh2, l_inv2, kt_two, vec, (ak, av), False
    )

    def conv_slots(grad):
        return run_pack((grad.reshape(n_wide, cols, 2 * half),), devices, (True,))[0]

    sum_two = scatter_slots(conv_slots(ak), order)
    ge = jnp.concatenate([s_ge.reshape(small.own, 256), l_ge.reshape(large.own, 256)], axis=0)
    ge_two = jnp.stack([ge[:, :half], ge[:, half:]])
    mine = lax.dynamic_index_in_dim(ge_two, here, 0, keepdims=False)
    other = swap_narrow(lax.dynamic_index_in_dim(ge_two, 1 - here, 0, keepdims=False))
    wide_order = [step for step in order if step != "n"]
    ge_all = gather_slots(jnp.stack([mine, other]), wide_order).reshape(-1, half)
    steps_two = jnp.stack([own_steps, swap_narrow(own_steps)])
    steps_all = gather_slots(steps_two, wide_order).reshape(-1)

    ak_one = run_first_weight(small, sc, s_gc1, s_u1, zero_k, True)
    ak_one = run_first_weight(large, sc, l_gc1, l_u1, ak_one, False)
    sum_one = scatter_slots(conv_slots(ak_one), order)
    l_mine, l_send, av = run_first_back(
        large, sc, l_gc1, l_zh1, l_inv1, l_gc2, kt_one, vec, av, False
    )
    large_grad = put_part(l_mine, swap_narrow(l_send), here)
    vec_blocks = jnp.pad(
        av[:12].T.astype(BF).reshape(-1, vcols, 12), ((0, 0), (0, 8 - vcols), (0, 116))
    )
    sum_vec = scatter_slots(run_pack((vec_blocks,), devices, (False,))[0], order)[:vcols, :12].T

    rows = here_wide * time_rows + jnp.arange(time_rows)
    time_sum = jnp.dot(
        features(steps_all, rows, feature_width // 2).astype(F32).T,
        ge_all,
        precision=PRECISE,
    )
    one_new = adam_step(
        first_conv, sum_one.T, first_conv_mean, first_conv_square, RATE_CONV, DECAY
    )
    two_new = adam_step(
        second_conv, sum_two.T, second_conv_mean, second_conv_square, RATE_CONV, DECAY
    )
    time_new = adam_step(
        time_dense, time_sum, time_dense_mean, time_dense_square, RATE_TIME, DECAY
    )
    qkv_new = adam_step(
        attn_qkv, sum_three[:qcols].T, attn_qkv_mean, attn_qkv_square, RATE_QKV, DECAY
    )
    proj_new = adam_step(
        attn_proj, sum_three[qcols:].T, attn_proj_mean, attn_proj_square, RATE_PROJ, DECAY
    )
    vec_new = adam_step(vectors, sum_vec, vectors_mean, vectors_square, RATE_VECTOR, 0.0)
    return (
        small_out, large_out, small_grad, large_grad,
        *one_new, *two_new, *time_new, *qkv_new, *proj_new, *vec_new,
    )


def solution(mesh):
    maps = P("wide", None, None, "narrow")
    conv = P("narrow", "wide")
    dense = P("wide", "narrow")
    attn = P(None, ("wide", "narrow"))
    return jax.shard_map(
        per_device,
        mesh=mesh,
        in_specs=(
            maps, maps, P("wide"), P("wide"), P("wide", None), maps, maps,
            conv, conv, dense, attn, attn, attn,
            conv, conv, conv, conv, dense, dense, attn, attn, attn, attn, attn, attn,
        ),
        out_specs=(maps,) * 4 + (conv,) * 6 + (dense,) * 3 + (attn,) * 9,
        check_vma=False,
    )
```

```python
import functools
import math

import jax
import jax.numpy as jnp
from jax import lax
from jax.experimental import pallas as pl
from jax.experimental.pallas import tpu as pltpu
from jax.sharding import PartitionSpec as P

GROUPS = 32
STEP_NUMBER = 10
NORM_EPS = 1e-05
ADAM_ONE = 0.9
ADAM_TWO = 0.999
ADAM_EPS = 1e-08
DECAY = 0.01
RATE_CONV = 0.08
RATE_TIME = 0.1
RATE_QKV = 0.2
RATE_PROJ = 1.0
RATE_VECTOR = 1.5
LOG_PERIOD = math.log(10000.0)
PRECISE = lax.Precision.HIGHEST
BF = jnp.bfloat16
F32 = jnp.float32
BLOCK_ROWS = 1024
VMEM_LIMIT = 60 * 2**20
NT = (((1,), (1,)), ((), ()))
TN = (((0,), (0,)), ((), ()))


def dot(a, b, dims=(((1,), (0,)), ((), ()))):
    return lax.dot_general(a, b, dims, preferred_element_type=F32)


def swap_narrow(x):
    return lax.ppermute(x, "narrow", [(0, 1), (1, 0)])


def swap_wide(x, bit):
    count = lax.axis_size("wide")
    return lax.ppermute(x, "wide", [(i, i ^ (1 << bit)) for i in range(count)])


def swap(x, step):
    return swap_narrow(x) if step == "n" else swap_wide(x, step)


def tie(x, after):
    return lax.optimization_barrier((x, after))[0]


def gather_order():
    bits = (lax.axis_size("wide") - 1).bit_length()
    steps = list(range(bits - 1, -1, -1))
    place = max(0, bits - 2)
    return steps[:place] + ["n"] + steps[place:]


def gather_pairs(blocks, order):
    slots = [block[None] for block in blocks]
    arrived = []
    log = []
    for i, step in enumerate(order):
        if i:
            slots = [jnp.concatenate(pair, axis=0) for pair in zip(slots, arrived)]
        arrived = []
        for block in slots:
            if arrived:
                block = tie(block, arrived[-1])
            arrived.append(swap(block, step))
        log.append(arrived)
    return list(zip(slots, arrived)), log


def scatter_pair(keep, send, order):
    for i, step in enumerate(reversed(order)):
        if i:
            half = keep.shape[0] // 2
            keep, send = keep[:half], keep[half:].astype(BF)
        keep = keep.astype(F32) + swap(send, step).astype(F32)
    return keep[0]


def slot_of(order, delta_wide, delta_narrow):
    slot = 0
    for i, step in enumerate(order):
        bit = delta_narrow if step == "n" else (delta_wide >> step) & 1
        slot = slot + (bit << i)
    return slot


def slot_table(order):
    here_wide = lax.axis_index("wide")
    here_narrow = lax.axis_index("narrow")
    wide = jnp.arange(lax.axis_size("wide"), dtype=jnp.int32)[:, None] ^ here_wide
    narrow = jnp.arange(lax.axis_size("narrow"), dtype=jnp.int32)[None, :] ^ here_narrow
    return slot_of(order, wide, narrow).reshape(-1)


def device_table(order):
    here_wide = lax.axis_index("wide")
    here_narrow = lax.axis_index("narrow")
    slots = jnp.arange(lax.axis_size("wide") * lax.axis_size("narrow"), dtype=jnp.int32)
    wide = jnp.zeros_like(slots)
    narrow = jnp.zeros_like(slots)
    for i, step in enumerate(order):
        bit = (slots >> i) & 1
        if step == "n":
            narrow = narrow + bit
        else:
            wide = wide + (bit << step)
    return (wide ^ here_wide) * 2 + (narrow ^ here_narrow)


def unpack_kernel(table, src, *outs, parts):
    def body(place, carry):
        slot = table[place]
        for out, (start, stop, joined) in zip(outs, parts):
            block = src[slot, start:stop, :]
            if joined:
                lanes = pl.ds(pl.multiple_of((place & 1) * 128, 128), 128)
                out[place >> 1, :, lanes] = block
            else:
                out[place] = block
        return carry

    lax.fori_loop(0, src.shape[0], body, 0)


def run_unpack(slots, table, parts):
    count, _, width = slots.shape
    shapes = []
    for start, stop, joined in parts:
        shape = (count // 2, stop - start, 256) if joined else (count, stop - start, width)
        shapes.append(jax.ShapeDtypeStruct(shape, slots.dtype))
    return pl.pallas_call(
        functools.partial(unpack_kernel, parts=parts),
        in_specs=[
            pl.BlockSpec(memory_space=pltpu.SMEM),
            pl.BlockSpec(memory_space=pltpu.VMEM),
        ],
        out_specs=[pl.BlockSpec(memory_space=pltpu.VMEM)] * len(parts),
        out_shape=shapes,
        compiler_params=pltpu.CompilerParams(vmem_limit_bytes=VMEM_LIMIT),
    )(table, slots)


def pack_kernel(table, *refs, joined):
    ins = refs[: len(joined)]
    outs = refs[len(joined) :]

    def body(slot, carry):
        place = table[slot]
        for src, out, lanes_joined in zip(ins, outs, joined):
            if lanes_joined:
                lanes = pl.ds(pl.multiple_of((place & 1) * 128, 128), 128)
                out[slot] = src[place >> 1, :, lanes].astype(BF)
            else:
                out[slot] = src[place].astype(BF)
        return carry

    lax.fori_loop(0, outs[0].shape[0], body, 0)


def run_pack(arrays, table, joined):
    shapes = []
    for array, halves in zip(arrays, joined):
        count, rows, width = array.shape
        shape = (count * 2, rows, 128) if halves else (count, rows, width)
        shapes.append(jax.ShapeDtypeStruct(shape, BF))
    return pl.pallas_call(
        functools.partial(pack_kernel, joined=joined),
        in_specs=[pl.BlockSpec(memory_space=pltpu.SMEM)]
        + [pl.BlockSpec(memory_space=pltpu.VMEM)] * len(arrays),
        out_specs=[pl.BlockSpec(memory_space=pltpu.VMEM)] * len(arrays),
        out_shape=shapes,
        compiler_params=pltpu.CompilerParams(vmem_limit_bytes=VMEM_LIMIT),
    )(table, *arrays)


def group_total(s):
    lane = lax.broadcasted_iota(jnp.int32, s.shape, 1)
    width = s.shape[1]
    for k in (1, 2, 4):
        s = s + jnp.where((lane & k) == 0, pltpu.roll(s, width - k, 1), pltpu.roll(s, k, 1))
    return s


def rows_sum(z):
    return jnp.sum(z, axis=0, keepdims=True)


def stack_rows(rows):
    return rows[0] if len(rows) == 1 else jnp.concatenate(rows, axis=0)


def norm_stats(get, n, pixels):
    scale = 1.0 / (8 * pixels)
    mean = group_total(stack_rows([rows_sum(get(m)) for m in range(n)])) * scale
    spread = []
    for m in range(n):
        centered = get(m) - mean[m : m + 1, :]
        spread.append(rows_sum(centered * centered))
    inverse = lax.rsqrt(group_total(stack_rows(spread)) * scale + NORM_EPS)
    return mean, inverse


def sigmoid(v):
    return 1.0 / (1.0 + jnp.exp(-v))


def shift_store(dst, m, value, height, breadth, forward):
    pixels = height * breadth
    channels = value.shape[1]
    column = lax.broadcasted_iota(jnp.int32, value.shape, 0) & (breadth - 1)
    before = jnp.where(column == 0, 0.0, pltpu.roll(value, 1, 0)).astype(BF)
    after = jnp.where(column == breadth - 1, 0.0, pltpu.roll(value, pixels - 1, 0)).astype(BF)
    lo, hi = (before, after) if forward else (after, before)
    rows = slice(breadth, breadth + pixels)
    dst[m, rows, 0:channels] = lo
    dst[m, rows, channels : 2 * channels] = value.astype(BF)
    dst[m, rows, 2 * channels :] = hi


def zero_edges(dst, height, breadth):
    n, rows, width = dst.shape
    edge = jnp.zeros((n, breadth, width), BF)
    dst[:, 0:breadth, :] = edge
    dst[:, rows - breadth :, :] = edge


def join_halves(place, own, other, dst):
    rows = dst.shape[0]

    @pl.when(place == 0)
    def _():
        dst[:, 0:128] = own[...].reshape(rows, 128)
        dst[:, 128:256] = other[...].reshape(rows, 128)

    @pl.when(place != 0)
    def _():
        dst[:, 0:128] = other[...].reshape(rows, 128)
        dst[:, 128:256] = own[...].reshape(rows, 128)


def conv_forward(shifted, kt, n, height, breadth):
    pixels = height * breadth
    total = None
    for p in range(3):
        for q in range(3):
            tap = 3 * p + q
            window = shifted[:, p * breadth : p * breadth + pixels, q * 256 : (q + 1) * 256]
            part = dot(window.reshape(n * pixels, 256), kt[tap * 256 : (tap + 1) * 256, :], NT)
            total = part if total is None else total + part
    return total


def grad_window(shifted, p, n, height, breadth):
    pixels = height * breadth
    start = (2 - p) * breadth
    return shifted[:, start : start + pixels, :].reshape(n * pixels, 768)


def conv_back(shifted, kt, n, height, breadth):
    window = jnp.concatenate(
        [grad_window(shifted, p, n, height, breadth) for p in range(3)], axis=1
    )
    return dot(window, kt[...])


def conv_weight(shifted, act, acc, n, height, breadth):
    for p in range(3):
        window = grad_window(shifted, p, n, height, breadth)
        acc[p * 768 : (p + 1) * 768, :] += dot(window, act, TN)


def each_slot(places, low, high, body):
    count = low.shape[0]

    def step(i, carry):
        body(low, i, places[i])
        body(high, i, places[count + i])
        return carry

    lax.fori_loop(0, count, step, 0)


def lanes_of(place):
    return pl.ds(pl.multiple_of((place & 1) * 128, 128), 128)


def rows_of(index, count, unit):
    return pl.ds(pl.multiple_of(index * count, unit), count)


def first_kernel(sc, *refs, n, height, breadth, build, cols, vcols):
    pixels = height * breadth
    if build:
        (places, xa, xb, low, high, c1_o, u1_o, zh_o, inv_o, kt, vec, x_s, shifted, vt) = refs
    else:
        (xa, xb, kt, vec, c1_o, u1_o, zh_o, inv_o, x_s, shifted) = refs
    join_halves(sc[0], xa, xb, x_s)

    @pl.when(pl.program_id(0) == 0)
    def _():
        zero_edges(shifted, height, breadth)
        if build:

            def fill(ref, i, place):
                kt[rows_of(place >> 1, cols, 16), lanes_of(place)] = ref[i, 0:cols, :]
                extra = ref[i, cols : cols + 16, :].astype(F32)
                vt[rows_of(place, vcols, 8), :] = extra[0:vcols]

            each_slot(places, low, high, fill)
            vec[...] = vt[...].T[0:16, :]

    def get(m):
        return x_s[m * pixels : (m + 1) * pixels, :].astype(F32)

    mean, inverse = norm_stats(get, n, pixels)
    inv_o[0, 0:n, :] = inverse
    for m in range(n):
        rows = slice(m * pixels, (m + 1) * pixels)
        zh = (get(m) - mean[m : m + 1, :]) * inverse[m : m + 1, :]
        zh_o[rows, :] = zh.astype(BF)
        a1 = zh * vec[0:1, :] + vec[1:2, :]
        u1 = a1 * sigmoid(a1)
        u1_o[rows, :] = u1.astype(BF)
        shift_store(shifted, m, u1, height, breadth, True)
    c1_o[...] = conv_forward(shifted, kt, n, height, breadth)


def middle_kernel(
    sc, *refs, n, height, breadth, own, which, first_call, build, cols, time_rows, qcols, pcols,
    first_map,
):
    pixels = height * breadth
    step = pl.program_id(0)
    refs = list(refs)

    def take(count):
        taken = refs[:count]
        del refs[:count]
        return taken

    if build:
        (places,) = take(1)
    c1, xa, xb, ga, gb = take(5)
    if build:
        low, high, feats = take(3)
    else:
        te, kt, wqkv, wo = take(4)
    (vec,) = take(1)
    if not first_call:
        aq_i, ao_i, av_i = take(3)
    u2_o, zh2_o, inv2_o, gc2_o, mine_o, send_o, aq, ao, av = take(9)
    if build:
        te, kt, wqkv, wo = take(4)
    (x_s, gy_s, shifted, h_s, zh3_s, hn_s, qkv_s, o_s, go_s, j_s, gk_s, gv_s) = take(12)
    if build:
        wt_s, q_s, p_s = take(3)
    join_halves(sc[0], xa, xb, x_s)
    join_halves(sc[0], ga, gb, gy_s)

    @pl.when(step == 0)
    def _():
        zero_edges(shifted, height, breadth)
        aq[...] = jnp.zeros_like(aq) if first_call else aq_i[...]
        ao[...] = jnp.zeros_like(ao) if first_call else ao_i[...]
        av[...] = jnp.zeros_like(av) if first_call else av_i[...]
        if build:
            top = cols + time_rows
            both = qcols + pcols

            def fill(ref, i, place):
                kt[rows_of(place >> 1, cols, 16), lanes_of(place)] = ref[i, 0:cols, :]
                wt_s[rows_of(place >> 1, time_rows, 16), lanes_of(place)] = ref[i, cols:top, :]
                attn = ref[i, top : top + 2 * both, :].astype(F32)
                for part in range(2):
                    lanes = slice(part * 128, (part + 1) * 128)
                    start = part * both
                    q_s[rows_of(place, qcols, 8), lanes] = attn[start : start + qcols]
                    p_s[rows_of(place, pcols, 8), lanes] = attn[start + qcols : start + both]

            each_slot(places, low, high, fill)
            wqkv[...] = q_s[...].astype(BF)
            wo[...] = p_s[...].astype(BF)
            te[...] = dot(feats[...], wt_s[...]) + vec[6:7, :] + vec[7:8, :]

    live = []
    for m in range(n):
        rows = slice(m * pixels, (m + 1) * pixels)
        slot = sc[0] * own + step * n + m
        live.append((slot < sc[1 + which]).astype(F32))
        gy_s[rows, :] = (gy_s[rows, :].astype(F32) * live[m]).astype(BF)

    def get_c1(m):
        return c1[m * pixels : (m + 1) * pixels, :] + te[pl.ds(first_map + step * n + m, 1), :]

    mean, inverse = norm_stats(get_c1, n, pixels)
    inv2_o[0, 0:n, :] = inverse
    for m in range(n):
        rows = slice(m * pixels, (m + 1) * pixels)
        zh = (get_c1(m) - mean[m : m + 1, :]) * inverse[m : m + 1, :]
        zh2_o[rows, :] = zh.astype(BF)
        a2 = zh * vec[2:3, :] + vec[3:4, :]
        u2 = a2 * sigmoid(a2)
        u2_o[rows, :] = u2.astype(BF)
        shift_store(shifted, m, u2, height, breadth, True)
    h_s[...] = (
        conv_forward(shifted, kt, n, height, breadth) + vec[8:9, :] + x_s[...].astype(F32)
    )

    def get_h(m):
        return h_s[m * pixels : (m + 1) * pixels, :]

    mean, inverse3 = norm_stats(get_h, n, pixels)
    for m in range(n):
        rows = slice(m * pixels, (m + 1) * pixels)
        zh = (get_h(m) - mean[m : m + 1, :]) * inverse3[m : m + 1, :]
        zh3_s[rows, :] = zh
        hn_s[rows, :] = (zh * vec[4:5, :] + vec[5:6, :]).astype(BF)
    for part in range(3):
        lanes = slice(part * 256, (part + 1) * 256)
        projected = dot(hn_s[...], wqkv[lanes, :], NT)
        if part == 0:
            projected = projected + vec[9:10, :]
        if part == 2:
            projected = projected + vec[10:11, :]
        qkv_s[:, lanes] = projected.astype(BF)
    go_s[...] = dot(gy_s[...], wo[...]).astype(BF)

    chunk = min(pixels, 256)
    scale = 1.0 / math.sqrt(256)
    for m in range(n):
        rows = slice(m * pixels, (m + 1) * pixels)
        keys = qkv_s[rows, 256:512]
        values = qkv_s[rows, 512:768]
        for c in range(pixels // chunk):
            part = slice(m * pixels + c * chunk, m * pixels + (c + 1) * chunk)
            queries = qkv_s[part, 0:256]
            scores = dot(queries, keys, NT)
            top = jnp.max(scores, axis=1, keepdims=True)
            exponent = jnp.exp((scores - top) * scale)
            probs = exponent * (1.0 / jnp.sum(exponent, axis=1, keepdims=True))
            low = probs.astype(BF)
            o_s[part, :] = dot(low, values).astype(BF)
            grad_o = go_s[part, :]
            grad_p = dot(grad_o, values, NT)
            inner = jnp.sum(probs * grad_p, axis=1, keepdims=True)
            grad_s = (probs * (grad_p - inner)).astype(BF)
            j_s[part, 0:256] = (dot(grad_s, keys) * scale).astype(BF)
            grad_k = dot(grad_s, queries, TN)
            grad_v = dot(low, grad_o, TN)
            if c == 0:
                gk_s[...] = grad_k
                gv_s[...] = grad_v
            else:
                gk_s[...] += grad_k
                gv_s[...] += grad_v
        j_s[rows, 256:512] = (gk_s[...] * scale).astype(BF)
        j_s[rows, 512:768] = gv_s[...].astype(BF)

    branch = (dot(o_s[...], wo[...], NT) + vec[11:12, :]).astype(BF).astype(F32)
    for m in range(n):
        rows = slice(m * pixels, (m + 1) * pixels)
        out = ((h_s[rows, :] + branch[rows, :]) * live[m]).astype(BF)

        @pl.when(sc[0] == 0)
        def _(out=out, m=m):
            mine_o[m] = out[:, 0:128].reshape(height, breadth, 128)
            send_o[m] = out[:, 128:256].reshape(height, breadth, 128)

        @pl.when(sc[0] != 0)
        def _(out=out, m=m):
            mine_o[m] = out[:, 128:256].reshape(height, breadth, 128)
            send_o[m] = out[:, 0:128].reshape(height, breadth, 128)

    ao[...] += dot(gy_s[...], o_s[...], TN)
    aq[...] += dot(j_s[...], hn_s[...], TN)
    av[9:10, :] += rows_sum(j_s[:, 0:256].astype(F32))
    av[10:11, :] += rows_sum(j_s[:, 512:768].astype(F32))
    av[11:12, :] += rows_sum(gy_s[...].astype(F32))
    grad_hn = dot(j_s[...], wqkv[...]).astype(BF)

    gain = vec[4:5, :]
    one = []
    two = []
    for m in range(n):
        rows = slice(m * pixels, (m + 1) * pixels)
        d = grad_hn[rows, :].astype(F32)
        one.append(rows_sum(d))
        two.append(rows_sum(d * zh3_s[rows, :]))
    one = stack_rows(one)
    two = stack_rows(two)
    av[4:5, :] += rows_sum(two)
    av[5:6, :] += rows_sum(one)
    mean_one = group_total(one * gain) * (1.0 / (8 * pixels))
    mean_two = group_total(two * gain) * (1.0 / (8 * pixels))
    bias = jnp.zeros((1, 256), F32)
    for m in range(n):
        rows = slice(m * pixels, (m + 1) * pixels)
        d = grad_hn[rows, :].astype(F32)
        gz = inverse3[m : m + 1, :] * (
            d * gain - mean_one[m : m + 1, :] - zh3_s[rows, :] * mean_two[m : m + 1, :]
        )
        low = (gz + gy_s[rows, :].astype(F32)).astype(BF)
        gc2_o[rows, :] = low
        bias = bias + rows_sum(low.astype(F32))
    av[8:9, :] += bias


def norm_silu_back(grad_act, zh_ref, inv_ref, gain, shift, n, pixels):
    one = []
    two = []
    grads = []
    for m in range(n):
        rows = slice(m * pixels, (m + 1) * pixels)
        zh = zh_ref[rows, :].astype(F32)
        a = zh * gain + shift
        s = sigmoid(a)
        d = grad_act[rows, :] * (s * (1.0 + a * (1.0 - s)))
        grads.append(d)
        one.append(rows_sum(d))
        two.append(rows_sum(d * zh))
    one = stack_rows(one)
    two = stack_rows(two)
    mean_one = group_total(one * gain) * (1.0 / (8 * pixels))
    mean_two = group_total(two * gain) * (1.0 / (8 * pixels))
    result = []
    for m in range(n):
        rows = slice(m * pixels, (m + 1) * pixels)
        zh = zh_ref[rows, :].astype(F32)
        result.append(
            inv_ref[0, m : m + 1, :]
            * (grads[m] * gain - mean_one[m : m + 1, :] - zh * mean_two[m : m + 1, :])
        )
    return result, rows_sum(one), rows_sum(two)


def second_back_kernel(
    sc, *refs, n, height, breadth, first_call, pack, cols, time_rows, qcols, pcols
):
    pixels = height * breadth
    step = pl.program_id(0)
    refs = list(refs)

    def take(count):
        taken = refs[:count]
        del refs[:count]
        return taken

    if pack:
        (places,) = take(1)
    gc2, u2, zh2, inv2, kt, vec, av_i = take(7)
    if not first_call:
        (ak_i,) = take(1)
    if pack:
        aq, ao, feats, ge_i = take(4)
    gc1_o, av = take(2)
    if pack:
        keep, send = take(2)
    else:
        ge_o, ak = take(2)
    (shifted,) = take(1)
    if pack:
        ak, ge_o, wt_s = take(3)

    @pl.when(step == 0)
    def _():
        zero_edges(shifted, height, breadth)
        ak[...] = jnp.zeros_like(ak) if first_call else ak_i[...]
        av[...] = av_i[...]
        if pack:
            ge_o[...] = ge_i[...]
        else:
            ge_o[...] = jnp.zeros_like(ge_o)

    for m in range(n):
        rows = slice(m * pixels, (m + 1) * pixels)
        shift_store(shifted, m, gc2[rows, :].astype(F32), height, breadth, False)
    grad_act = conv_back(shifted, kt, n, height, breadth)
    conv_weight(shifted, u2[...], ak, n, height, breadth)
    grads, one, two = norm_silu_back(grad_act, zh2, inv2, vec[2:3, :], vec[3:4, :], n, pixels)
    av[2:3, :] += two
    av[3:4, :] += one
    base = 8 if pack else 0
    for m in range(n):
        rows = slice(m * pixels, (m + 1) * pixels)
        low = grads[m].astype(BF)
        gc1_o[rows, :] = low
        ge = rows_sum(low.astype(F32))
        ge_o[pl.ds(base + step * n + m, 1), :] = ge
        av[6:7, :] += ge
        av[7:8, :] += ge

    if pack:

        @pl.when(step == pl.num_programs(0) - 1)
        def _():
            wt_s[...] = lax.dot_general(
                feats[...].astype(F32), ge_o[...], TN, precision=PRECISE,
                preferred_element_type=F32,
            )
            top = cols + time_rows
            both = qcols + pcols

            def fill(ref, i, place):
                lanes = lanes_of(place)
                ref[i, 0:cols, :] = ak[rows_of(place >> 1, cols, 8), lanes].astype(BF)
                ref[i, cols:top, :] = wt_s[rows_of(place >> 1, time_rows, 8), lanes].astype(BF)
                for part in range(2):
                    half = slice(part * 128, (part + 1) * 128)
                    block = jnp.concatenate(
                        [
                            aq[rows_of(place, qcols, 8), half],
                            ao[rows_of(place, pcols, 8), half],
                        ],
                        axis=0,
                    )
                    ref[i, top + part * both : top + (part + 1) * both, :] = block.astype(BF)

            each_slot(places, keep, send, fill)


def first_weight_kernel(sc, *refs, n, height, breadth, first_call, pack, cols):
    pixels = height * breadth
    step = pl.program_id(0)
    if pack:
        places, gc1, u1, ak_i, keep, send, shifted, ak = refs
    elif first_call:
        gc1, u1, ak, shifted = refs
    else:
        gc1, u1, ak_i, ak, shifted = refs

    @pl.when(step == 0)
    def _():
        zero_edges(shifted, height, breadth)
        ak[...] = jnp.zeros_like(ak) if first_call else ak_i[...]

    for m in range(n):
        rows = slice(m * pixels, (m + 1) * pixels)
        shift_store(shifted, m, gc1[rows, :].astype(F32), height, breadth, False)
    conv_weight(shifted, u1[...], ak, n, height, breadth)

    if pack:

        @pl.when(step == pl.num_programs(0) - 1)
        def _():
            def fill(ref, i, place):
                ref[i] = ak[rows_of(place >> 1, cols, 8), lanes_of(place)].astype(BF)

            each_slot(places, keep, send, fill)


def first_back_kernel(
    sc, gc1, zh1, inv1, gc2, kt, vec, av_i, mine_o, send_o, av_o, shifted, *rest,
    n, height, breadth, last_call,
):
    pixels = height * breadth
    av = rest[0] if last_call else av_o

    @pl.when(pl.program_id(0) == 0)
    def _():
        zero_edges(shifted, height, breadth)
        av[...] = av_i[...]

    for m in range(n):
        rows = slice(m * pixels, (m + 1) * pixels)
        shift_store(shifted, m, gc1[rows, :].astype(F32), height, breadth, False)
    grad_act = conv_back(shifted, kt, n, height, breadth)
    grads, one, two = norm_silu_back(grad_act, zh1, inv1, vec[0:1, :], vec[1:2, :], n, pixels)
    av[0:1, :] += two
    av[1:2, :] += one
    for m in range(n):
        rows = slice(m * pixels, (m + 1) * pixels)
        grad = grads[m] + gc2[rows, :].astype(F32)

        @pl.when(sc[0] == 0)
        def _(grad=grad, m=m):
            mine_o[m] = grad[:, 0:128].reshape(height, breadth, 128)
            send_o[m] = grad[:, 128:256].astype(BF).reshape(height, breadth, 128)

        @pl.when(sc[0] != 0)
        def _(grad=grad, m=m):
            mine_o[m] = grad[:, 128:256].reshape(height, breadth, 128)
            send_o[m] = grad[:, 0:128].astype(BF).reshape(height, breadth, 128)


    if last_call:

        @pl.when(pl.program_id(0) == pl.num_programs(0) - 1)
        def _():
            padded = jnp.concatenate([av[...], jnp.zeros((112, 256), F32)], axis=0)
            av_o[...] = padded.T


class Group:
    def __init__(self, shape, which):
        self.maps, self.height, self.breadth, self.half = shape
        self.which = which
        self.own = self.maps // 2
        self.pixels = self.height * self.breadth
        self.n = max(1, min(self.own, BLOCK_ROWS // self.pixels))
        self.steps = self.own // self.n
        self.rows = self.n * self.pixels
        self.all_rows = self.own * self.pixels
        self.params = dict(n=self.n, height=self.height, breadth=self.breadth)

    def row_spec(self):
        return pl.BlockSpec((self.rows, 256), lambda i, sc, *_: (i, 0))

    def row_shape(self, dtype):
        return jax.ShapeDtypeStruct((self.all_rows, 256), dtype)

    def map_spec(self, placed):
        steps = self.steps
        shape = (self.n, self.height, self.breadth, 128)
        if placed:
            return pl.BlockSpec(shape, lambda i, sc, *_: (sc[0] * steps + i, 0, 0, 0))
        return pl.BlockSpec(shape, lambda i, sc, *_: (i, 0, 0, 0))

    def map_shape(self, placed, dtype):
        count = self.maps if placed else self.own
        return jax.ShapeDtypeStruct((count, self.height, self.breadth, 128), dtype)

    def stat_spec(self):
        return pl.BlockSpec((1, 8, 256), lambda i, sc, *_: (i, 0, 0))

    def stat_shape(self):
        return jax.ShapeDtypeStruct((self.steps, 8, 256), F32)

    def shifted(self):
        return pltpu.VMEM((self.n, (self.height + 2) * self.breadth, 768), BF)

    def call(self, body, in_specs, out_specs, out_shape, scratch, flops, prefetch=1):
        return pl.pallas_call(
            body,
            grid_spec=pltpu.PrefetchScalarGridSpec(
                num_scalar_prefetch=prefetch,
                grid=(self.steps,),
                in_specs=in_specs,
                out_specs=out_specs,
                scratch_shapes=scratch,
            ),
            out_shape=out_shape,
            compiler_params=pltpu.CompilerParams(vmem_limit_bytes=VMEM_LIMIT),
            cost_estimate=pl.CostEstimate(
                flops=flops, bytes_accessed=self.all_rows * 256 * 8, transcendentals=0
            ),
        )


def whole(shape):
    zeros = (0,) * len(shape)
    return pl.BlockSpec(shape, lambda i, sc, *_: zeros)


def run_first(g, sc, x, x_other, weights, dims):
    build = len(weights) == 3
    cols, vcols = dims["cols"], dims["vcols"]
    built = [whole((2304, 256)), whole((16, 256))]
    body = functools.partial(first_kernel, build=build, cols=cols, vcols=vcols, **g.params)
    outs = [g.row_spec(), g.row_spec(), g.row_spec(), g.stat_spec()]
    shapes = [g.row_shape(F32), g.row_shape(BF), g.row_shape(BF), g.stat_shape()]
    scratch = [pltpu.VMEM((g.rows, 256), BF), g.shifted()]
    flops = 2 * g.all_rows * 2304 * 256
    maps = [g.map_spec(True), g.map_spec(False)]
    if build:
        places, low, high = weights
        return g.call(
            body,
            maps + [whole(low.shape), whole(high.shape)],
            outs + built,
            shapes
            + [jax.ShapeDtypeStruct((2304, 256), BF), jax.ShapeDtypeStruct((16, 256), F32)],
            scratch + [pltpu.VMEM((256, 128), F32)],
            flops,
            2,
        )(sc, places, x, x_other, low, high)
    return g.call(body, maps + built, outs, shapes, scratch, flops)(sc, x, x_other, *weights)


def run_middle(g, sc, c1, x, x_other, gy, gy_other, weights, vec, acc, first_map, dims):
    build = len(weights) == 4 and weights[0].ndim == 1
    row = g.row_spec()
    big = pltpu.VMEM((g.rows, 256), F32)
    low16 = pltpu.VMEM((g.rows, 256), BF)
    wide = pltpu.VMEM((g.rows, 768), BF)
    body = functools.partial(
        middle_kernel, own=g.own, which=g.which, first_call=acc is None, build=build,
        first_map=first_map, cols=dims["cols"], time_rows=dims["time_rows"],
        qcols=dims["qcols"], pcols=dims["pcols"], **g.params,
    )
    acc_specs = [whole((768, 256)), whole((256, 256)), whole((16, 256))]
    built = [whole((16, 256)), whole((2304, 256)), whole((768, 256)), whole((256, 256))]
    maps = [g.map_spec(True), g.map_spec(False)] * 2
    ins = [row] + maps
    outs = [row, row, g.stat_spec(), row, g.map_spec(True), g.map_spec(False)] + acc_specs
    shapes = [
        g.row_shape(BF), g.row_shape(BF), g.stat_shape(), g.row_shape(BF),
        g.map_shape(True, BF), g.map_shape(False, BF),
        jax.ShapeDtypeStruct((768, 256), F32), jax.ShapeDtypeStruct((256, 256), F32),
        jax.ShapeDtypeStruct((16, 256), F32),
    ]
    scratch = [
        low16, low16, g.shifted(), big, big, low16, wide, low16, low16, wide,
        pltpu.VMEM((g.pixels, 256), F32), pltpu.VMEM((g.pixels, 256), F32),
    ]
    args = [c1, x, x_other, gy, gy_other]
    if build:
        places, low, high, feats = weights
        ins += [whole(low.shape), whole(high.shape), whole(feats.shape)]
        args = [places] + args + [low, high, feats]
        outs += built
        shapes += [
            jax.ShapeDtypeStruct((16, 256), F32), jax.ShapeDtypeStruct((2304, 256), BF),
            jax.ShapeDtypeStruct((768, 256), BF), jax.ShapeDtypeStruct((256, 256), BF),
        ]
        scratch += [
            pltpu.VMEM((feats.shape[1], 256), BF), pltpu.VMEM((768, 256), F32),
            pltpu.VMEM((256, 256), F32),
        ]
    else:
        ins += built
        args += list(weights)
    ins += [whole((16, 256))]
    args += [vec]
    if acc is not None:
        ins += acc_specs
        args += list(acc)
    flops = 2 * g.all_rows * 256 * (2304 + 256 * 12 + 6 * g.pixels)
    return g.call(body, ins, outs, shapes, scratch, flops, 2 if build else 1)(sc, *args)


def run_second_back(g, sc, gc2, u2, zh2, inv2, kt, vec, av, ak, packing, dims):
    row = g.row_spec()
    body = functools.partial(
        second_back_kernel, first_call=ak is None, pack=packing is not None,
        cols=dims["cols"], time_rows=dims["time_rows"], qcols=dims["qcols"],
        pcols=dims["pcols"], **g.params,
    )
    ins = [row, row, row, g.stat_spec(), whole((2304, 256)), whole((16, 256)), whole((16, 256))]
    args = [gc2, u2, zh2, inv2, kt, vec, av]
    outs = [row, whole((16, 256))]
    shapes = [g.row_shape(BF), jax.ShapeDtypeStruct((16, 256), F32)]
    scratch = [g.shifted()]
    if ak is not None:
        ins += [whole((2304, 256))]
        args += [ak]
    if packing is not None:
        places, aq, ao, feats, ge = packing
        ins += [whole((768, 256)), whole((256, 256)), whole(feats.shape), whole((16, 256))]
        args = [places] + args + [aq, ao, feats, ge]
        slots = (
            dims["places"] // 2,
            dims["cols"] + dims["time_rows"] + 2 * (dims["qcols"] + dims["pcols"]),
            128,
        )
        outs += [whole(slots)] * 2
        shapes += [jax.ShapeDtypeStruct(slots, BF)] * 2
        scratch += [
            pltpu.VMEM((2304, 256), F32), pltpu.VMEM((16, 256), F32),
            pltpu.VMEM((feats.shape[1], 256), F32),
        ]
    else:
        outs += [whole((16, 256)), whole((2304, 256))]
        shapes += [
            jax.ShapeDtypeStruct((16, 256), F32), jax.ShapeDtypeStruct((2304, 256), F32)
        ]
    return g.call(
        body, ins, outs, shapes, scratch, 4 * g.all_rows * 256 * 2304,
        1 if packing is None else 2,
    )(sc, *args)


def run_first_weight(g, sc, gc1, u1, ak, places, dims):
    row = g.row_spec()
    body = functools.partial(
        first_weight_kernel, first_call=ak is None, pack=places is not None,
        cols=dims["cols"], **g.params,
    )
    ins = [row, row]
    args = [gc1, u1]
    scratch = [g.shifted()]
    if ak is not None:
        ins += [whole((2304, 256))]
        args += [ak]
    if places is None:
        outs = whole((2304, 256))
        shapes = jax.ShapeDtypeStruct((2304, 256), F32)
    else:
        args = [places] + args
        slots = (dims["places"] // 2, dims["cols"], 128)
        outs = [whole(slots)] * 2
        shapes = [jax.ShapeDtypeStruct(slots, BF)] * 2
        scratch += [pltpu.VMEM((2304, 256), F32)]
    return g.call(
        body, ins, outs, shapes, scratch, 2 * g.all_rows * 256 * 2304,
        1 if places is None else 2,
    )(sc, *args)


def run_first_back(g, sc, gc1, zh1, inv1, gc2, kt, vec, av, last_call):
    row = g.row_spec()
    shape = (256, 128) if last_call else (16, 256)
    return g.call(
        functools.partial(first_back_kernel, last_call=last_call, **g.params),
        [row, row, g.stat_spec(), row, whole((2304, 256)), whole((16, 256)), whole((16, 256))],
        [g.map_spec(True), g.map_spec(False), whole(shape)],
        [g.map_shape(True, F32), g.map_shape(False, BF), jax.ShapeDtypeStruct(shape, F32)],
        [g.shifted()] + ([pltpu.VMEM((16, 256), F32)] if last_call else []),
        2 * g.all_rows * 256 * 2304,
    )(sc, gc1, zh1, inv1, gc2, kt, vec, av)


def features(steps, index, half_width):
    frequency = jnp.exp(
        (index % half_width).astype(F32) * (-LOG_PERIOD / (half_width - 1))
    )
    angles = steps.astype(F32)[:, None] * frequency[None, :]
    return jax.nn.silu(
        jnp.where(index[None, :] < half_width, jnp.sin(angles), jnp.cos(angles))
    ).astype(BF)


def adam_step(weight, grad, mean, square, rate, decay):
    mean_new = ADAM_ONE * mean + (1.0 - ADAM_ONE) * grad
    square_new = ADAM_TWO * square + (1.0 - ADAM_TWO) * grad * grad
    first_fix = mean_new / (1.0 - ADAM_ONE**STEP_NUMBER)
    second_fix = square_new / (1.0 - ADAM_TWO**STEP_NUMBER)
    weight_new = weight - rate * (first_fix / (jnp.sqrt(second_fix) + ADAM_EPS) + decay * weight)
    return (weight_new, mean_new, square_new)


def other_part(x, here, after=None):
    own = x.shape[0] // 2
    part = lax.dynamic_slice_in_dim(x, (1 - here) * own, own, 0)
    return swap_narrow(part if after is None else tie(part, after))


def put_part(full, arrived, here):
    own = arrived.shape[0]
    return lax.dynamic_update_slice_in_dim(
        full, arrived.astype(full.dtype), (1 - here) * own, 0
    )


def per_device(
    small_maps, large_maps, small_steps, large_steps, live_counts,
    small_cotangent, large_cotangent,
    first_conv, second_conv, time_dense, attn_qkv, attn_proj, vectors,
    first_conv_mean, first_conv_square, second_conv_mean, second_conv_square,
    time_dense_mean, time_dense_square, attn_qkv_mean, attn_qkv_square,
    attn_proj_mean, attn_proj_square, vectors_mean, vectors_square,
):
    n_wide = lax.axis_size("wide")
    here = lax.axis_index("narrow")
    channels = attn_qkv.shape[0]
    half = first_conv.shape[0]
    cols = first_conv.shape[1]
    time_rows = time_dense.shape[0]
    feature_width = time_rows * n_wide
    qcols = attn_qkv.shape[1]
    pcols = attn_proj.shape[1]
    vcols = vectors.shape[1]
    dims = dict(
        cols=cols, time_rows=time_rows, qcols=qcols, pcols=pcols, vcols=vcols, places=2 * n_wide
    )
    fits = not (cols % 16 or time_rows % 16 or qcols % 8 or pcols % 8 or vcols % 8)
    order = gather_order()
    devices = device_table(order)
    small = Group(small_maps.shape, 0)
    large = Group(large_maps.shape, 1)
    sc = jnp.concatenate([here[None].astype(jnp.int32), live_counts[0]])

    xs = other_part(small_maps, here)
    vec_rows = jnp.pad(
        vectors.astype(BF).T, ((0, 16 - vcols), (0, 128 - vectors.shape[0]))
    )
    block_one = jnp.concatenate([first_conv.astype(BF).T, vec_rows], axis=0)
    attn_rows = jnp.concatenate([attn_qkv.astype(BF).T, attn_proj.astype(BF).T], axis=0)
    block_two = jnp.concatenate(
        [
            second_conv.astype(BF).T, time_dense.astype(BF),
            attn_rows[:, :128], attn_rows[:, 128:],
        ],
        axis=0,
    )
    (pair_one, pair_two), log = gather_pairs([block_one, block_two], order)
    xl = other_part(large_maps, here, log[order.index("n")][0])
    gs = other_part(small_cotangent, here, xl)
    gl = other_part(large_cotangent, here, gs)

    own_small = lax.dynamic_slice_in_dim(small_steps, here * small.own, small.own, 0)
    own_large = lax.dynamic_slice_in_dim(large_steps, here * large.own, large.own, 0)
    own_steps = jnp.pad(
        jnp.concatenate([own_small, own_large]), (0, 16 - small.own - large.own)
    )
    feats = features(own_steps, jnp.arange(feature_width), feature_width // 2)
    if fits:
        weights_one = (devices, *pair_one)
        weights_two = (devices, *pair_two, feats)
    else:
        table = slot_table(order)
        top = cols + time_rows
        both = qcols + pcols
        kt_one, vec = run_unpack(
            jnp.concatenate(pair_one), table, ((0, cols, True), (cols, cols + 16, False))
        )
        vec = vec[:, :vcols, :16].reshape(channels, 16).T.astype(F32)
        kt_two, wt, attn = run_unpack(
            jnp.concatenate(pair_two), table,
            ((0, cols, True), (cols, top, True), (top, top + 2 * both, False)),
        )
        wt = wt.reshape(feature_width, 2 * half)
        attn = jnp.concatenate([attn[:, :both], attn[:, both:]], axis=2)
        te = jnp.dot(feats, wt, preferred_element_type=F32) + vec[7] + vec[6]
        weights_one = (kt_one.reshape(n_wide * cols, 2 * half), vec)
        weights_two = (
            te, kt_two.reshape(n_wide * cols, 2 * half),
            attn[:, :qcols].reshape(3 * channels, channels),
            attn[:, qcols:].reshape(channels, channels),
        )

    s_c1, s_u1, s_zh1, s_inv1, *built = run_first(
        small, sc, small_maps, xs, weights_one, dims
    )
    weights_one = built if fits else weights_one
    kt_one, vec = weights_one
    l_c1, l_u1, l_zh1, l_inv1 = run_first(large, sc, large_maps, xl, weights_one, dims)
    (s_u2, s_zh2, s_inv2, s_gc2, s_mine, s_send, aq, ao, av, *built) = run_middle(
        small, sc, s_c1, small_maps, xs, small_cotangent, gs, weights_two, vec, None, 0, dims
    )
    small_out = put_part(s_mine, swap_narrow(s_send), here)
    weights_two = built if fits else weights_two
    kt_two = weights_two[1]
    (l_u2, l_zh2, l_inv2, l_gc2, l_mine, l_send, aq, ao, av) = run_middle(
        large, sc, l_c1, large_maps, xl, large_cotangent, gl, weights_two, vec, (aq, ao, av),
        small.own, dims,
    )
    large_out = put_part(l_mine, swap_narrow(l_send), here)

    s_gc1, av, ge, ak = run_second_back(
        small, sc, s_gc2, s_u2, s_zh2, s_inv2, kt_two, vec, av, None, None, dims
    )
    if fits:
        l_gc1, av, keep, send = run_second_back(
            large, sc, l_gc2, l_u2, l_zh2, l_inv2, kt_two, vec, av, ak,
            (devices, aq, ao, feats, ge), dims,
        )
    else:
        l_gc1, av, l_ge, ak = run_second_back(
            large, sc, l_gc2, l_u2, l_zh2, l_inv2, kt_two, vec, av, ak, None, dims
        )
        ge = jnp.concatenate([ge[:8], l_ge[:8]])
        gwt = jnp.dot(feats.astype(F32).T, ge, precision=PRECISE)
        packed = run_pack(
            (
                ak.reshape(n_wide, cols, 256), gwt.reshape(n_wide, time_rows, 256),
                aq.reshape(-1, qcols, 256), ao.reshape(-1, pcols, 256),
            ),
            devices, (True, True, False, False),
        )
        attn = jnp.concatenate(packed[2:], axis=1)
        slots = jnp.concatenate(
            [packed[0], packed[1], attn[:, :, :128], attn[:, :, 128:]], axis=1
        )
        keep, send = slots[:n_wide], slots[n_wide:]
    sum_two = scatter_pair(keep, send, order)

    ak = run_first_weight(small, sc, s_gc1, s_u1, None, None, dims)
    if fits:
        keep, send = run_first_weight(large, sc, l_gc1, l_u1, ak, devices, dims)
    else:
        ak = run_first_weight(large, sc, l_gc1, l_u1, ak, None, dims)
        slots = run_pack((ak.reshape(n_wide, cols, 256),), devices, (True,))[0]
        keep, send = slots[:n_wide], slots[n_wide:]
    sum_one = scatter_pair(keep, send, order)
    s_mine, s_send, av = run_first_back(
        small, sc, s_gc1, s_zh1, s_inv1, s_gc2, kt_one, vec, av, False
    )
    small_grad = put_part(s_mine, swap_narrow(s_send), here)
    l_mine, l_send, av = run_first_back(
        large, sc, l_gc1, l_zh1, l_inv1, l_gc2, kt_one, vec, av, True
    )
    large_grad = put_part(l_mine, swap_narrow(l_send), here)
    arrived = lax.all_to_all(
        av.reshape(2 * n_wide, vcols, 128), ("wide", "narrow"), split_axis=0, concat_axis=0,
        tiled=True,
    )
    sum_vec = arrived.sum(axis=0)[:, :12].T

    top = cols + time_rows
    both = qcols + pcols
    time_sum = sum_two[cols:top]
    attn_sum = jnp.concatenate([sum_two[top : top + both], sum_two[top + both :]], axis=1)
    one_new = adam_step(
        first_conv, sum_one.T, first_conv_mean, first_conv_square, RATE_CONV, DECAY
    )
    two_new = adam_step(
        second_conv, sum_two[:cols].T, second_conv_mean, second_conv_square, RATE_CONV, DECAY
    )
    time_new = adam_step(
        time_dense, time_sum, time_dense_mean, time_dense_square, RATE_TIME, DECAY
    )
    qkv_new = adam_step(
        attn_qkv, attn_sum[:qcols].T, attn_qkv_mean, attn_qkv_square, RATE_QKV, DECAY
    )
    proj_new = adam_step(
        attn_proj, attn_sum[qcols:].T, attn_proj_mean, attn_proj_square, RATE_PROJ, DECAY
    )
    vec_new = adam_step(vectors, sum_vec, vectors_mean, vectors_square, RATE_VECTOR, 0.0)
    return (
        small_out, large_out, small_grad, large_grad,
        *one_new, *two_new, *time_new, *qkv_new, *proj_new, *vec_new,
    )


def solution(mesh):
    maps = P("wide", None, None, "narrow")
    conv = P("narrow", "wide")
    dense = P("wide", "narrow")
    attn = P(None, ("wide", "narrow"))
    return jax.shard_map(
        per_device,
        mesh=mesh,
        in_specs=(
            maps, maps, P("wide"), P("wide"), P("wide", None), maps, maps,
            conv, conv, dense, attn, attn, attn,
            conv, conv, conv, conv, dense, dense, attn, attn, attn, attn, attn, attn,
        ),
        out_specs=(maps,) * 4 + (conv,) * 6 + (dense,) * 3 + (attn,) * 9,
        check_vma=False,
    )
```

```python
import functools
import math

import jax
import jax.numpy as jnp
from jax import lax
from jax.experimental import pallas as pl
from jax.experimental.pallas import tpu as pltpu
from jax.sharding import PartitionSpec as P

GROUPS = 32
STEP_NUMBER = 10
NORM_EPS = 1e-05
ADAM_ONE = 0.9
ADAM_TWO = 0.999
ADAM_EPS = 1e-08
DECAY = 0.01
RATE_CONV = 0.08
RATE_TIME = 0.1
RATE_QKV = 0.2
RATE_PROJ = 1.0
RATE_VECTOR = 1.5
LOG_PERIOD = math.log(10000.0)
PRECISE = lax.Precision.HIGHEST
BF = jnp.bfloat16
F32 = jnp.float32
BLOCK_ROWS = 1024
VMEM_LIMIT = 28 * 2**20
NT = (((1,), (1,)), ((), ()))
TN = (((0,), (0,)), ((), ()))


def dot(a, b, dims=(((1,), (0,)), ((), ()))):
    return lax.dot_general(a, b, dims, preferred_element_type=F32)


def swap_narrow(x):
    return lax.ppermute(x, "narrow", [(0, 1), (1, 0)])


def swap_wide(x, bit):
    count = lax.axis_size("wide")
    return lax.ppermute(x, "wide", [(i, i ^ (1 << bit)) for i in range(count)])


def swap(x, step):
    return swap_narrow(x) if step == "n" else swap_wide(x, step)


def tie(x, after):
    return lax.optimization_barrier((x, after))[0]


def gather_order():
    bits = (lax.axis_size("wide") - 1).bit_length()
    return ["n"] + list(range(bits - 1, -1, -1))


def gather_step(slots, log, order, after=None):
    if log:
        last = log[-1]
        if after is not None:
            last = tie(last, after)
        slots = jnp.concatenate([slots, last], axis=0)
    elif after is not None:
        slots = tie(slots, after)
    return slots, log + [swap(slots, order[len(log)])]


def scatter_step(pair, step, last=False):
    keep, send = pair
    keep = keep.astype(F32) + swap(send, step).astype(F32)
    if last:
        return keep[0]
    half = keep.shape[0] // 2
    return keep[:half], keep[half:].astype(BF)


def slot_of(order, delta_wide, delta_narrow):
    slot = 0
    for i, step in enumerate(order):
        bit = delta_narrow if step == "n" else (delta_wide >> step) & 1
        slot = slot + (bit << i)
    return slot


def slot_table(order):
    here_wide = lax.axis_index("wide")
    here_narrow = lax.axis_index("narrow")
    wide = jnp.arange(lax.axis_size("wide"), dtype=jnp.int32)[:, None] ^ here_wide
    narrow = jnp.arange(lax.axis_size("narrow"), dtype=jnp.int32)[None, :] ^ here_narrow
    return slot_of(order, wide, narrow).reshape(-1)


def device_table(order):
    here_wide = lax.axis_index("wide")
    here_narrow = lax.axis_index("narrow")
    slots = jnp.arange(lax.axis_size("wide") * lax.axis_size("narrow"), dtype=jnp.int32)
    wide = jnp.zeros_like(slots)
    narrow = jnp.zeros_like(slots)
    for i, step in enumerate(order):
        bit = (slots >> i) & 1
        if step == "n":
            narrow = narrow + bit
        else:
            wide = wide + (bit << step)
    return (wide ^ here_wide) * 2 + (narrow ^ here_narrow)


def prepare_kernel(first, second, dense, qkv, proj, vectors, one, two, attn_s, vec_s):
    cols = first.shape[0]
    top = cols + dense.shape[0]
    qcols, pcols = qkv.shape[0], proj.shape[0]
    both = qcols + pcols
    one[0:cols, :] = first[...].astype(BF)
    two[0:cols, :] = second[...].astype(BF)
    two[cols:top, :] = dense[...].astype(BF)
    attn_s[0:qcols, :] = qkv[...]
    attn_s[qcols:both, :] = proj[...]
    two[top : top + both, :] = attn_s[:, 0:128].astype(BF)
    two[top + both : top + 2 * both, :] = attn_s[:, 128:256].astype(BF)
    vec_s[...] = jnp.zeros_like(vec_s)
    vec_s[0 : vectors.shape[0], 0 : vectors.shape[1]] = vectors[...]
    one[cols : cols + 16, :] = vec_s[...].astype(BF)


def run_prepare(first, second, dense, qkv, proj, vectors):
    cols = first.shape[0]
    both = qkv.shape[0] + proj.shape[0]
    rows = cols + dense.shape[0] + 2 * both
    args = (first, second, dense, qkv, proj, vectors)

    def spec(shape):
        return pl.BlockSpec(shape, lambda i: (0, 0))

    return pl.pallas_call(
        prepare_kernel,
        grid=(1,),
        in_specs=[spec(x.shape) for x in args],
        out_specs=[spec((cols + 16, 128)), spec((rows, 128))],
        out_shape=[
            jax.ShapeDtypeStruct((cols + 16, 128), BF), jax.ShapeDtypeStruct((rows, 128), BF)
        ],
        scratch_shapes=[pltpu.VMEM((both, 256), F32), pltpu.VMEM((16, 128), F32)],
        compiler_params=pltpu.CompilerParams(vmem_limit_bytes=60 * 2**20),
    )(*args)


def unpack_kernel(table, src, *outs, parts):
    def body(place, carry):
        slot = table[place]
        for out, (start, stop, joined) in zip(outs, parts):
            block = src[slot, start:stop, :]
            if joined:
                lanes = pl.ds(pl.multiple_of((place & 1) * 128, 128), 128)
                out[place >> 1, :, lanes] = block
            else:
                out[place] = block
        return carry

    lax.fori_loop(0, src.shape[0], body, 0)


def run_unpack(slots, table, parts):
    count, _, width = slots.shape
    shapes = []
    for start, stop, joined in parts:
        shape = (count // 2, stop - start, 256) if joined else (count, stop - start, width)
        shapes.append(jax.ShapeDtypeStruct(shape, slots.dtype))
    return pl.pallas_call(
        functools.partial(unpack_kernel, parts=parts),
        in_specs=[
            pl.BlockSpec(memory_space=pltpu.SMEM),
            pl.BlockSpec(memory_space=pltpu.VMEM),
        ],
        out_specs=[pl.BlockSpec(memory_space=pltpu.VMEM)] * len(parts),
        out_shape=shapes,
        compiler_params=pltpu.CompilerParams(vmem_limit_bytes=VMEM_LIMIT),
    )(table, slots)


def pack_kernel(table, *refs, joined):
    ins = refs[: len(joined)]
    outs = refs[len(joined) :]

    def body(slot, carry):
        place = table[slot]
        for src, out, lanes_joined in zip(ins, outs, joined):
            if lanes_joined:
                lanes = pl.ds(pl.multiple_of((place & 1) * 128, 128), 128)
                out[slot] = src[place >> 1, :, lanes].astype(BF)
            else:
                out[slot] = src[place].astype(BF)
        return carry

    lax.fori_loop(0, outs[0].shape[0], body, 0)


def run_pack(arrays, table, joined):
    shapes = []
    for array, halves in zip(arrays, joined):
        count, rows, width = array.shape
        shape = (count * 2, rows, 128) if halves else (count, rows, width)
        shapes.append(jax.ShapeDtypeStruct(shape, BF))
    return pl.pallas_call(
        functools.partial(pack_kernel, joined=joined),
        in_specs=[pl.BlockSpec(memory_space=pltpu.SMEM)]
        + [pl.BlockSpec(memory_space=pltpu.VMEM)] * len(arrays),
        out_specs=[pl.BlockSpec(memory_space=pltpu.VMEM)] * len(arrays),
        out_shape=shapes,
        compiler_params=pltpu.CompilerParams(vmem_limit_bytes=VMEM_LIMIT),
    )(table, *arrays)


def group_total(s):
    lane = lax.broadcasted_iota(jnp.int32, s.shape, 1)
    width = s.shape[1]
    for k in (1, 2, 4):
        s = s + jnp.where((lane & k) == 0, pltpu.roll(s, width - k, 1), pltpu.roll(s, k, 1))
    return s


def rows_sum(z):
    return jnp.sum(z, axis=0, keepdims=True)


def stack_rows(rows):
    return rows[0] if len(rows) == 1 else jnp.concatenate(rows, axis=0)


def norm_stats(get, n, pixels):
    scale = 1.0 / (8 * pixels)
    mean = group_total(stack_rows([rows_sum(get(m)) for m in range(n)])) * scale
    spread = []
    for m in range(n):
        centered = get(m) - mean[m : m + 1, :]
        spread.append(rows_sum(centered * centered))
    inverse = lax.rsqrt(group_total(stack_rows(spread)) * scale + NORM_EPS)
    return mean, inverse


def sigmoid(v):
    return 1.0 / (1.0 + jnp.exp(-v))


def shift_store(dst, m, value, height, breadth, forward):
    pixels = height * breadth
    channels = value.shape[1]
    column = lax.broadcasted_iota(jnp.int32, value.shape, 0) & (breadth - 1)
    before = jnp.where(column == 0, 0.0, pltpu.roll(value, 1, 0)).astype(BF)
    after = jnp.where(column == breadth - 1, 0.0, pltpu.roll(value, pixels - 1, 0)).astype(BF)
    lo, hi = (before, after) if forward else (after, before)
    rows = slice(breadth, breadth + pixels)
    dst[m, rows, 0:channels] = lo
    dst[m, rows, channels : 2 * channels] = value.astype(BF)
    dst[m, rows, 2 * channels :] = hi


def zero_edges(dst, height, breadth):
    n, rows, width = dst.shape
    edge = jnp.zeros((n, breadth, width), BF)
    dst[:, 0:breadth, :] = edge
    dst[:, rows - breadth :, :] = edge


def join_halves(place, own, other, dst):
    rows = dst.shape[0]

    @pl.when(place == 0)
    def _():
        dst[:, 0:128] = own[...].reshape(rows, 128)
        dst[:, 128:256] = other[...]

    @pl.when(place != 0)
    def _():
        dst[:, 0:128] = other[...]
        dst[:, 128:256] = own[...].reshape(rows, 128)


def conv_forward(shifted, kt, n, height, breadth):
    pixels = height * breadth
    total = None
    for p in range(3):
        for q in range(3):
            tap = 3 * p + q
            window = shifted[:, p * breadth : p * breadth + pixels, q * 256 : (q + 1) * 256]
            part = dot(window.reshape(n * pixels, 256), kt[tap * 256 : (tap + 1) * 256, :], NT)
            total = part if total is None else total + part
    return total


def grad_window(shifted, p, n, height, breadth):
    pixels = height * breadth
    start = (2 - p) * breadth
    return shifted[:, start : start + pixels, :].reshape(n * pixels, 768)


def conv_back(shifted, kt, n, height, breadth):
    window = jnp.concatenate(
        [grad_window(shifted, p, n, height, breadth) for p in range(3)], axis=1
    )
    return dot(window, kt[...])


def conv_weight(shifted, act, acc, n, height, breadth):
    for p in range(3):
        window = grad_window(shifted, p, n, height, breadth)
        acc[p * 768 : (p + 1) * 768, :] += dot(window, act, TN)


def each_slot(places, low, high, body):
    count = low.shape[0]

    def step(i, carry):
        body(low, i, places[i])
        body(high, i, places[count + i])
        return carry

    lax.fori_loop(0, count, step, 0)


def lanes_of(place):
    return pl.ds(pl.multiple_of((place & 1) * 128, 128), 128)


def rows_of(index, count, unit):
    return pl.ds(pl.multiple_of(index * count, unit), count)


def first_kernel(sc, *refs, n, height, breadth, build, cols, vcols):
    pixels = height * breadth
    if build:
        (places, xa, xb, low, high, c1_o, u1_o, zh_o, inv_o, kt, vec, x_s, shifted, vt) = refs
    else:
        (xa, xb, kt, vec, c1_o, u1_o, zh_o, inv_o, x_s, shifted) = refs
    join_halves(sc[0], xa, xb, x_s)

    @pl.when(pl.program_id(0) == 0)
    def _():
        zero_edges(shifted, height, breadth)
        if build:

            def fill(ref, i, place):
                kt[rows_of(place >> 1, cols, 16), lanes_of(place)] = ref[i, 0:cols, :]
                extra = ref[i, cols : cols + 16, :].astype(F32)
                vt[rows_of(place, vcols, 8), :] = extra[0:vcols]

            each_slot(places, low, high, fill)
            vec[...] = vt[...].T[0:16, :]

    def get(m):
        return x_s[m * pixels : (m + 1) * pixels, :].astype(F32)

    mean, inverse = norm_stats(get, n, pixels)
    inv_o[0, 0:n, :] = inverse
    for m in range(n):
        rows = slice(m * pixels, (m + 1) * pixels)
        zh = (get(m) - mean[m : m + 1, :]) * inverse[m : m + 1, :]
        zh_o[rows, :] = zh.astype(BF)
        a1 = zh * vec[0:1, :] + vec[1:2, :]
        u1 = a1 * sigmoid(a1)
        u1_o[rows, :] = u1.astype(BF)
        shift_store(shifted, m, u1, height, breadth, True)
    c1_o[...] = conv_forward(shifted, kt, n, height, breadth)


def middle_kernel(
    sc, *refs, n, height, breadth, own, which, first_call, build, cols, time_rows, qcols, pcols,
    first_map,
):
    pixels = height * breadth
    step = pl.program_id(0)
    refs = list(refs)

    def take(count):
        taken = refs[:count]
        del refs[:count]
        return taken

    if build:
        (places,) = take(1)
    c1, xa, xb, ga, gb = take(5)
    if build:
        low, high, feats = take(3)
    else:
        te, kt, wqkv, wo = take(4)
    (vec,) = take(1)
    if not first_call:
        aq_i, ao_i, av_i = take(3)
    u2_o, zh2_o, inv2_o, gc2_o, mine_o, send_o, aq, ao, av = take(9)
    if build:
        te, kt, wqkv, wo = take(4)
    (x_s, gy_s, shifted, h_s, zh3_s, hn_s, qkv_s, o_s, go_s, j_s, gk_s, gv_s) = take(12)
    if build:
        wt_s, q_s, p_s = take(3)
    join_halves(sc[0], xa, xb, x_s)
    join_halves(sc[0], ga, gb, gy_s)

    @pl.when(step == 0)
    def _():
        zero_edges(shifted, height, breadth)
        aq[...] = jnp.zeros_like(aq) if first_call else aq_i[...]
        ao[...] = jnp.zeros_like(ao) if first_call else ao_i[...]
        av[...] = jnp.zeros_like(av) if first_call else av_i[...]
        if build:
            top = cols + time_rows
            both = qcols + pcols

            def fill(ref, i, place):
                kt[rows_of(place >> 1, cols, 16), lanes_of(place)] = ref[i, 0:cols, :]
                wt_s[rows_of(place >> 1, time_rows, 16), lanes_of(place)] = ref[i, cols:top, :]
                attn = ref[i, top : top + 2 * both, :].astype(F32)
                for part in range(2):
                    lanes = slice(part * 128, (part + 1) * 128)
                    start = part * both
                    q_s[rows_of(place, qcols, 8), lanes] = attn[start : start + qcols]
                    p_s[rows_of(place, pcols, 8), lanes] = attn[start + qcols : start + both]

            each_slot(places, low, high, fill)
            wqkv[...] = q_s[...].astype(BF)
            wo[...] = p_s[...].astype(BF)
            te[...] = dot(feats[...], wt_s[...]) + vec[6:7, :] + vec[7:8, :]

    live = []
    for m in range(n):
        rows = slice(m * pixels, (m + 1) * pixels)
        slot = sc[0] * own + step * n + m
        live.append((slot < sc[1 + which]).astype(F32))
        gy_s[rows, :] = (gy_s[rows, :].astype(F32) * live[m]).astype(BF)

    def get_c1(m):
        return c1[m * pixels : (m + 1) * pixels, :] + te[pl.ds(first_map + step * n + m, 1), :]

    mean, inverse = norm_stats(get_c1, n, pixels)
    inv2_o[0, 0:n, :] = inverse
    for m in range(n):
        rows = slice(m * pixels, (m + 1) * pixels)
        zh = (get_c1(m) - mean[m : m + 1, :]) * inverse[m : m + 1, :]
        zh2_o[rows, :] = zh.astype(BF)
        a2 = zh * vec[2:3, :] + vec[3:4, :]
        u2 = a2 * sigmoid(a2)
        u2_o[rows, :] = u2.astype(BF)
        shift_store(shifted, m, u2, height, breadth, True)
    h_s[...] = (
        conv_forward(shifted, kt, n, height, breadth) + vec[8:9, :] + x_s[...].astype(F32)
    )

    def get_h(m):
        return h_s[m * pixels : (m + 1) * pixels, :]

    mean, inverse3 = norm_stats(get_h, n, pixels)
    for m in range(n):
        rows = slice(m * pixels, (m + 1) * pixels)
        zh = (get_h(m) - mean[m : m + 1, :]) * inverse3[m : m + 1, :]
        zh3_s[rows, :] = zh
        hn_s[rows, :] = (zh * vec[4:5, :] + vec[5:6, :]).astype(BF)
    for part in range(3):
        lanes = slice(part * 256, (part + 1) * 256)
        projected = dot(hn_s[...], wqkv[lanes, :], NT)
        if part == 0:
            projected = projected + vec[9:10, :]
        if part == 2:
            projected = projected + vec[10:11, :]
        qkv_s[:, lanes] = projected.astype(BF)
    go_s[...] = dot(gy_s[...], wo[...]).astype(BF)

    chunk = min(pixels, 256)
    scale = 1.0 / math.sqrt(256)
    for m in range(n):
        rows = slice(m * pixels, (m + 1) * pixels)
        keys = qkv_s[rows, 256:512]
        values = qkv_s[rows, 512:768]
        for c in range(pixels // chunk):
            part = slice(m * pixels + c * chunk, m * pixels + (c + 1) * chunk)
            queries = qkv_s[part, 0:256]
            scores = dot(queries, keys, NT)
            top = jnp.max(scores, axis=1, keepdims=True)
            exponent = jnp.exp((scores - top) * scale)
            probs = exponent * (1.0 / jnp.sum(exponent, axis=1, keepdims=True))
            low = probs.astype(BF)
            o_s[part, :] = dot(low, values).astype(BF)
            grad_o = go_s[part, :]
            grad_p = dot(grad_o, values, NT)
            inner = jnp.sum(probs * grad_p, axis=1, keepdims=True)
            grad_s = (probs * (grad_p - inner)).astype(BF)
            j_s[part, 0:256] = (dot(grad_s, keys) * scale).astype(BF)
            grad_k = dot(grad_s, queries, TN)
            grad_v = dot(low, grad_o, TN)
            if c == 0:
                gk_s[...] = grad_k
                gv_s[...] = grad_v
            else:
                gk_s[...] += grad_k
                gv_s[...] += grad_v
        j_s[rows, 256:512] = (gk_s[...] * scale).astype(BF)
        j_s[rows, 512:768] = gv_s[...].astype(BF)

    branch = (dot(o_s[...], wo[...], NT) + vec[11:12, :]).astype(BF).astype(F32)
    for m in range(n):
        rows = slice(m * pixels, (m + 1) * pixels)
        out = ((h_s[rows, :] + branch[rows, :]) * live[m]).astype(BF)

        @pl.when(sc[0] == 0)
        def _(out=out, m=m):
            mine_o[m] = out[:, 0:128].reshape(height, breadth, 128)
            send_o[m] = out[:, 128:256].reshape(height, breadth, 128)

        @pl.when(sc[0] != 0)
        def _(out=out, m=m):
            mine_o[m] = out[:, 128:256].reshape(height, breadth, 128)
            send_o[m] = out[:, 0:128].reshape(height, breadth, 128)

    ao[...] += dot(gy_s[...], o_s[...], TN)
    aq[...] += dot(j_s[...], hn_s[...], TN)
    av[9:10, :] += rows_sum(j_s[:, 0:256].astype(F32))
    av[10:11, :] += rows_sum(j_s[:, 512:768].astype(F32))
    av[11:12, :] += rows_sum(gy_s[...].astype(F32))
    grad_hn = dot(j_s[...], wqkv[...]).astype(BF)

    gain = vec[4:5, :]
    one = []
    two = []
    for m in range(n):
        rows = slice(m * pixels, (m + 1) * pixels)
        d = grad_hn[rows, :].astype(F32)
        one.append(rows_sum(d))
        two.append(rows_sum(d * zh3_s[rows, :]))
    one = stack_rows(one)
    two = stack_rows(two)
    av[4:5, :] += rows_sum(two)
    av[5:6, :] += rows_sum(one)
    mean_one = group_total(one * gain) * (1.0 / (8 * pixels))
    mean_two = group_total(two * gain) * (1.0 / (8 * pixels))
    bias = jnp.zeros((1, 256), F32)
    for m in range(n):
        rows = slice(m * pixels, (m + 1) * pixels)
        d = grad_hn[rows, :].astype(F32)
        gz = inverse3[m : m + 1, :] * (
            d * gain - mean_one[m : m + 1, :] - zh3_s[rows, :] * mean_two[m : m + 1, :]
        )
        low = (gz + gy_s[rows, :].astype(F32)).astype(BF)
        gc2_o[rows, :] = low
        bias = bias + rows_sum(low.astype(F32))
    av[8:9, :] += bias


def norm_silu_back(grad_act, zh_ref, inv_ref, gain, shift, n, pixels):
    one = []
    two = []
    grads = []
    for m in range(n):
        rows = slice(m * pixels, (m + 1) * pixels)
        zh = zh_ref[rows, :].astype(F32)
        a = zh * gain + shift
        s = sigmoid(a)
        d = grad_act[rows, :] * (s * (1.0 + a * (1.0 - s)))
        grads.append(d)
        one.append(rows_sum(d))
        two.append(rows_sum(d * zh))
    one = stack_rows(one)
    two = stack_rows(two)
    mean_one = group_total(one * gain) * (1.0 / (8 * pixels))
    mean_two = group_total(two * gain) * (1.0 / (8 * pixels))
    result = []
    for m in range(n):
        rows = slice(m * pixels, (m + 1) * pixels)
        zh = zh_ref[rows, :].astype(F32)
        result.append(
            inv_ref[0, m : m + 1, :]
            * (grads[m] * gain - mean_one[m : m + 1, :] - zh * mean_two[m : m + 1, :])
        )
    return result, rows_sum(one), rows_sum(two)


def second_back_kernel(
    sc, *refs, n, height, breadth, first_call, pack, cols, time_rows, qcols, pcols
):
    pixels = height * breadth
    step = pl.program_id(0)
    refs = list(refs)

    def take(count):
        taken = refs[:count]
        del refs[:count]
        return taken

    if pack:
        (places,) = take(1)
    gc2, u2, zh2, inv2, kt, vec, av_i = take(7)
    if not first_call:
        (ak_i,) = take(1)
    if pack:
        aq, ao, feats, ge_i = take(4)
    gc1_o, av = take(2)
    if pack:
        keep, send = take(2)
    else:
        ge_o, ak = take(2)
    (shifted,) = take(1)
    if pack:
        ak, ge_o, wt_s = take(3)

    @pl.when(step == 0)
    def _():
        zero_edges(shifted, height, breadth)
        ak[...] = jnp.zeros_like(ak) if first_call else ak_i[...]
        av[...] = av_i[...]
        if pack:
            ge_o[...] = ge_i[...]
        else:
            ge_o[...] = jnp.zeros_like(ge_o)

    for m in range(n):
        rows = slice(m * pixels, (m + 1) * pixels)
        shift_store(shifted, m, gc2[rows, :].astype(F32), height, breadth, False)
    grad_act = conv_back(shifted, kt, n, height, breadth)
    conv_weight(shifted, u2[...], ak, n, height, breadth)
    grads, one, two = norm_silu_back(grad_act, zh2, inv2, vec[2:3, :], vec[3:4, :], n, pixels)
    av[2:3, :] += two
    av[3:4, :] += one
    base = 8 if pack else 0
    for m in range(n):
        rows = slice(m * pixels, (m + 1) * pixels)
        low = grads[m].astype(BF)
        gc1_o[rows, :] = low
        ge = rows_sum(low.astype(F32))
        ge_o[pl.ds(base + step * n + m, 1), :] = ge
        av[6:7, :] += ge
        av[7:8, :] += ge

    if pack:

        @pl.when(step == pl.num_programs(0) - 1)
        def _():
            wt_s[...] = lax.dot_general(
                feats[...].astype(F32), ge_o[...], TN, precision=PRECISE,
                preferred_element_type=F32,
            )
            top = cols + time_rows
            both = qcols + pcols

            def fill(ref, i, place):
                lanes = lanes_of(place)
                ref[i, 0:cols, :] = ak[rows_of(place >> 1, cols, 8), lanes].astype(BF)
                ref[i, cols:top, :] = wt_s[rows_of(place >> 1, time_rows, 8), lanes].astype(BF)
                for part in range(2):
                    half = slice(part * 128, (part + 1) * 128)
                    block = jnp.concatenate(
                        [
                            aq[rows_of(place, qcols, 8), half],
                            ao[rows_of(place, pcols, 8), half],
                        ],
                        axis=0,
                    )
                    ref[i, top + part * both : top + (part + 1) * both, :] = block.astype(BF)

            each_slot(places, keep, send, fill)


def first_weight_kernel(sc, *refs, n, height, breadth, first_call, pack, cols):
    pixels = height * breadth
    step = pl.program_id(0)
    if pack:
        places, gc1, u1, ak_i, keep, send, shifted, ak = refs
    elif first_call:
        gc1, u1, ak, shifted = refs
    else:
        gc1, u1, ak_i, ak, shifted = refs

    @pl.when(step == 0)
    def _():
        zero_edges(shifted, height, breadth)
        ak[...] = jnp.zeros_like(ak) if first_call else ak_i[...]

    for m in range(n):
        rows = slice(m * pixels, (m + 1) * pixels)
        shift_store(shifted, m, gc1[rows, :].astype(F32), height, breadth, False)
    conv_weight(shifted, u1[...], ak, n, height, breadth)

    if pack:

        @pl.when(step == pl.num_programs(0) - 1)
        def _():
            def fill(ref, i, place):
                ref[i] = ak[rows_of(place >> 1, cols, 8), lanes_of(place)].astype(BF)

            each_slot(places, keep, send, fill)


def first_back_kernel(
    sc, gc1, zh1, inv1, gc2, kt, vec, av_i, mine_o, send_o, av_o, shifted, *rest,
    n, height, breadth, last_call,
):
    pixels = height * breadth
    av = rest[0] if last_call else av_o

    @pl.when(pl.program_id(0) == 0)
    def _():
        zero_edges(shifted, height, breadth)
        av[...] = av_i[...]

    for m in range(n):
        rows = slice(m * pixels, (m + 1) * pixels)
        shift_store(shifted, m, gc1[rows, :].astype(F32), height, breadth, False)
    grad_act = conv_back(shifted, kt, n, height, breadth)
    grads, one, two = norm_silu_back(grad_act, zh1, inv1, vec[0:1, :], vec[1:2, :], n, pixels)
    av[0:1, :] += two
    av[1:2, :] += one
    for m in range(n):
        rows = slice(m * pixels, (m + 1) * pixels)
        grad = grads[m] + gc2[rows, :].astype(F32)

        @pl.when(sc[0] == 0)
        def _(grad=grad, m=m):
            mine_o[m] = grad[:, 0:128].reshape(height, breadth, 128)
            send_o[m] = grad[:, 128:256].astype(BF).reshape(height, breadth, 128)

        @pl.when(sc[0] != 0)
        def _(grad=grad, m=m):
            mine_o[m] = grad[:, 128:256].reshape(height, breadth, 128)
            send_o[m] = grad[:, 0:128].astype(BF).reshape(height, breadth, 128)


    if last_call:

        @pl.when(pl.program_id(0) == pl.num_programs(0) - 1)
        def _():
            padded = jnp.concatenate([av[...], jnp.zeros((112, 256), F32)], axis=0)
            av_o[...] = padded.T


class Group:
    def __init__(self, shape, which):
        self.maps, self.height, self.breadth, self.half = shape
        self.which = which
        self.own = self.maps // 2
        self.pixels = self.height * self.breadth
        self.n = max(1, min(self.own, BLOCK_ROWS // self.pixels))
        self.steps = self.own // self.n
        self.rows = self.n * self.pixels
        self.all_rows = self.own * self.pixels
        self.params = dict(n=self.n, height=self.height, breadth=self.breadth)

    def row_spec(self):
        return pl.BlockSpec((self.rows, 256), lambda i, sc, *_: (i, 0))

    def row_shape(self, dtype):
        return jax.ShapeDtypeStruct((self.all_rows, 256), dtype)

    def map_spec(self, placed):
        steps = self.steps
        shape = (self.n, self.height, self.breadth, 128)
        if placed:
            return pl.BlockSpec(shape, lambda i, sc, *_: (sc[0] * steps + i, 0, 0, 0))
        return pl.BlockSpec(shape, lambda i, sc, *_: (i, 0, 0, 0))

    def flat_spec(self, first):
        first = first // self.rows
        return pl.BlockSpec((self.rows, 128), lambda i, sc, *_: (first + i, 0))

    def map_shape(self, placed, dtype):
        count = self.maps if placed else self.own
        return jax.ShapeDtypeStruct((count, self.height, self.breadth, 128), dtype)

    def stat_spec(self):
        return pl.BlockSpec((1, 8, 256), lambda i, sc, *_: (i, 0, 0))

    def stat_shape(self):
        return jax.ShapeDtypeStruct((self.steps, 8, 256), F32)

    def shifted(self):
        return pltpu.VMEM((self.n, (self.height + 2) * self.breadth, 768), BF)

    def call(self, body, in_specs, out_specs, out_shape, scratch, flops, prefetch=1):
        return pl.pallas_call(
            body,
            grid_spec=pltpu.PrefetchScalarGridSpec(
                num_scalar_prefetch=prefetch,
                grid=(self.steps,),
                in_specs=in_specs,
                out_specs=out_specs,
                scratch_shapes=scratch,
            ),
            out_shape=out_shape,
            compiler_params=pltpu.CompilerParams(vmem_limit_bytes=VMEM_LIMIT),
            cost_estimate=pl.CostEstimate(
                flops=4 * flops, bytes_accessed=self.all_rows * 256 * 8, transcendentals=0
            ),
        )


def whole(shape):
    zeros = (0,) * len(shape)
    return pl.BlockSpec(shape, lambda i, sc, *_: zeros)


def run_first(g, sc, x, x_other, first_row, weights, dims):
    build = len(weights) == 3
    cols, vcols = dims["cols"], dims["vcols"]
    built = [whole((2304, 256)), whole((16, 256))]
    body = functools.partial(first_kernel, build=build, cols=cols, vcols=vcols, **g.params)
    outs = [g.row_spec(), g.row_spec(), g.row_spec(), g.stat_spec()]
    shapes = [g.row_shape(F32), g.row_shape(BF), g.row_shape(BF), g.stat_shape()]
    scratch = [pltpu.VMEM((g.rows, 256), BF), g.shifted()]
    flops = 2 * g.all_rows * 2304 * 256
    maps = [g.map_spec(True), g.flat_spec(first_row)]
    if build:
        places, low, high = weights
        return g.call(
            body,
            maps + [whole(low.shape), whole(high.shape)],
            outs + built,
            shapes
            + [jax.ShapeDtypeStruct((2304, 256), BF), jax.ShapeDtypeStruct((16, 256), F32)],
            scratch + [pltpu.VMEM((256, 128), F32)],
            flops,
            2,
        )(sc, places, x, x_other, low, high)
    return g.call(body, maps + built, outs, shapes, scratch, flops)(sc, x, x_other, *weights)


def run_middle(
    g, sc, c1, x, x_other, first_row, gy, gy_other, weights, vec, acc, first_map, dims
):
    build = len(weights) == 4 and weights[0].ndim == 1
    row = g.row_spec()
    big = pltpu.VMEM((g.rows, 256), F32)
    low16 = pltpu.VMEM((g.rows, 256), BF)
    wide = pltpu.VMEM((g.rows, 768), BF)
    body = functools.partial(
        middle_kernel, own=g.own, which=g.which, first_call=acc is None, build=build,
        first_map=first_map, cols=dims["cols"], time_rows=dims["time_rows"],
        qcols=dims["qcols"], pcols=dims["pcols"], **g.params,
    )
    acc_specs = [whole((768, 256)), whole((256, 256)), whole((16, 256))]
    built = [whole((16, 256)), whole((2304, 256)), whole((768, 256)), whole((256, 256))]
    maps = [
        g.map_spec(True), g.flat_spec(first_row), g.map_spec(True), g.flat_spec(0),
    ]
    ins = [row] + maps
    outs = [row, row, g.stat_spec(), row, g.map_spec(True), g.map_spec(False)] + acc_specs
    shapes = [
        g.row_shape(BF), g.row_shape(BF), g.stat_shape(), g.row_shape(BF),
        g.map_shape(True, BF), g.map_shape(False, BF),
        jax.ShapeDtypeStruct((768, 256), F32), jax.ShapeDtypeStruct((256, 256), F32),
        jax.ShapeDtypeStruct((16, 256), F32),
    ]
    scratch = [
        low16, low16, g.shifted(), big, big, low16, wide, low16, low16, wide,
        pltpu.VMEM((g.pixels, 256), F32), pltpu.VMEM((g.pixels, 256), F32),
    ]
    args = [c1, x, x_other, gy, gy_other]
    if build:
        places, low, high, feats = weights
        ins += [whole(low.shape), whole(high.shape), whole(feats.shape)]
        args = [places] + args + [low, high, feats]
        outs += built
        shapes += [
            jax.ShapeDtypeStruct((16, 256), F32), jax.ShapeDtypeStruct((2304, 256), BF),
            jax.ShapeDtypeStruct((768, 256), BF), jax.ShapeDtypeStruct((256, 256), BF),
        ]
        scratch += [
            pltpu.VMEM((feats.shape[1], 256), BF), pltpu.VMEM((768, 256), F32),
            pltpu.VMEM((256, 256), F32),
        ]
    else:
        ins += built
        args += list(weights)
    ins += [whole((16, 256))]
    args += [vec]
    if acc is not None:
        ins += acc_specs
        args += list(acc)
    flops = 2 * g.all_rows * 256 * (2304 + 256 * 12 + 6 * g.pixels)
    return g.call(body, ins, outs, shapes, scratch, flops, 2 if build else 1)(sc, *args)


def run_second_back(g, sc, gc2, u2, zh2, inv2, kt, vec, av, ak, packing, dims):
    row = g.row_spec()
    body = functools.partial(
        second_back_kernel, first_call=ak is None, pack=packing is not None,
        cols=dims["cols"], time_rows=dims["time_rows"], qcols=dims["qcols"],
        pcols=dims["pcols"], **g.params,
    )
    ins = [row, row, row, g.stat_spec(), whole((2304, 256)), whole((16, 256)), whole((16, 256))]
    args = [gc2, u2, zh2, inv2, kt, vec, av]
    outs = [row, whole((16, 256))]
    shapes = [g.row_shape(BF), jax.ShapeDtypeStruct((16, 256), F32)]
    scratch = [g.shifted()]
    if ak is not None:
        ins += [whole((2304, 256))]
        args += [ak]
    if packing is not None:
        places, aq, ao, feats, ge = packing
        ins += [whole((768, 256)), whole((256, 256)), whole(feats.shape), whole((16, 256))]
        args = [places] + args + [aq, ao, feats, ge]
        slots = (
            dims["places"] // 2,
            dims["cols"] + dims["time_rows"] + 2 * (dims["qcols"] + dims["pcols"]),
            128,
        )
        outs += [whole(slots)] * 2
        shapes += [jax.ShapeDtypeStruct(slots, BF)] * 2
        scratch += [
            pltpu.VMEM((2304, 256), F32), pltpu.VMEM((16, 256), F32),
            pltpu.VMEM((feats.shape[1], 256), F32),
        ]
    else:
        outs += [whole((16, 256)), whole((2304, 256))]
        shapes += [
            jax.ShapeDtypeStruct((16, 256), F32), jax.ShapeDtypeStruct((2304, 256), F32)
        ]
    return g.call(
        body, ins, outs, shapes, scratch, 4 * g.all_rows * 256 * 2304,
        1 if packing is None else 2,
    )(sc, *args)


def run_first_weight(g, sc, gc1, u1, ak, places, dims):
    row = g.row_spec()
    body = functools.partial(
        first_weight_kernel, first_call=ak is None, pack=places is not None,
        cols=dims["cols"], **g.params,
    )
    ins = [row, row]
    args = [gc1, u1]
    scratch = [g.shifted()]
    if ak is not None:
        ins += [whole((2304, 256))]
        args += [ak]
    if places is None:
        outs = whole((2304, 256))
        shapes = jax.ShapeDtypeStruct((2304, 256), F32)
    else:
        args = [places] + args
        slots = (dims["places"] // 2, dims["cols"], 128)
        outs = [whole(slots)] * 2
        shapes = [jax.ShapeDtypeStruct(slots, BF)] * 2
        scratch += [pltpu.VMEM((2304, 256), F32)]
    return g.call(
        body, ins, outs, shapes, scratch, 2 * g.all_rows * 256 * 2304,
        1 if places is None else 2,
    )(sc, *args)


def run_first_back(g, sc, gc1, zh1, inv1, gc2, kt, vec, av, last_call):
    row = g.row_spec()
    shape = (256, 128) if last_call else (16, 256)
    return g.call(
        functools.partial(first_back_kernel, last_call=last_call, **g.params),
        [row, row, g.stat_spec(), row, whole((2304, 256)), whole((16, 256)), whole((16, 256))],
        [g.map_spec(True), g.map_spec(False), whole(shape)],
        [g.map_shape(True, F32), g.map_shape(False, BF), jax.ShapeDtypeStruct(shape, F32)],
        [g.shifted()] + ([pltpu.VMEM((16, 256), F32)] if last_call else []),
        2 * g.all_rows * 256 * 2304,
    )(sc, gc1, zh1, inv1, gc2, kt, vec, av)


def features(steps, index, half_width):
    frequency = jnp.exp(
        (index % half_width).astype(F32) * (-LOG_PERIOD / (half_width - 1))
    )
    angles = steps.astype(F32)[:, None] * frequency[None, :]
    return jax.nn.silu(
        jnp.where(index[None, :] < half_width, jnp.sin(angles), jnp.cos(angles))
    ).astype(BF)


def adam_step(weight, grad, mean, square, rate, decay):
    mean_new = ADAM_ONE * mean + (1.0 - ADAM_ONE) * grad
    square_new = ADAM_TWO * square + (1.0 - ADAM_TWO) * grad * grad
    first_fix = mean_new / (1.0 - ADAM_ONE**STEP_NUMBER)
    second_fix = square_new / (1.0 - ADAM_TWO**STEP_NUMBER)
    weight_new = weight - rate * (first_fix / (jnp.sqrt(second_fix) + ADAM_EPS) + decay * weight)
    return (weight_new, mean_new, square_new)


def other_rows(x, here):
    own = x.shape[0] // 2
    return lax.dynamic_slice_in_dim(x, (1 - here) * own, own, 0).reshape(-1, x.shape[3])


def put_part(full, arrived, here):
    own = arrived.shape[0]
    return lax.dynamic_update_slice_in_dim(
        full, arrived.astype(full.dtype), (1 - here) * own, 0
    )


def per_device(
    small_maps, large_maps, small_steps, large_steps, live_counts,
    small_cotangent, large_cotangent,
    first_conv, second_conv, time_dense, attn_qkv, attn_proj, vectors,
    first_conv_mean, first_conv_square, second_conv_mean, second_conv_square,
    time_dense_mean, time_dense_square, attn_qkv_mean, attn_qkv_square,
    attn_proj_mean, attn_proj_square, vectors_mean, vectors_square,
):
    n_wide = lax.axis_size("wide")
    here = lax.axis_index("narrow")
    channels = attn_qkv.shape[0]
    half = first_conv.shape[0]
    cols = first_conv.shape[1]
    time_rows = time_dense.shape[0]
    feature_width = time_rows * n_wide
    qcols = attn_qkv.shape[1]
    pcols = attn_proj.shape[1]
    vcols = vectors.shape[1]
    dims = dict(
        cols=cols, time_rows=time_rows, qcols=qcols, pcols=pcols, vcols=vcols, places=2 * n_wide
    )
    fits = not (cols % 16 or time_rows % 16 or qcols % 8 or pcols % 8 or vcols % 8)
    order = gather_order()
    devices = device_table(order)
    small = Group(small_maps.shape, 0)
    large = Group(large_maps.shape, 1)

    if fits:
        block_one, block_two = run_prepare(
            first_conv.T, second_conv.T, time_dense, attn_qkv.T, attn_proj.T, vectors.T
        )
    else:
        vec_rows = jnp.pad(
            vectors.astype(BF).T, ((0, 16 - vcols), (0, 128 - vectors.shape[0]))
        )
        block_one = jnp.concatenate([first_conv.astype(BF).T, vec_rows], axis=0)
        attn_rows = jnp.concatenate([attn_qkv.astype(BF).T, attn_proj.astype(BF).T], axis=0)
        block_two = jnp.concatenate(
            [
                second_conv.astype(BF).T, time_dense.astype(BF),
                attn_rows[:, :128], attn_rows[:, 128:],
            ],
            axis=0,
        )
    one, log = block_one[None], []
    for _ in order:
        one, log = gather_step(one, log, order)
    two, log_two = block_two[None], []
    for i in range(len(order) - 1):
        two, log_two = gather_step(two, log_two, order, log[(0, 1, 2)[min(i, 2)]])
    xs = swap_narrow(other_rows(tie(small_maps, (log[0], log_two[0])), here))
    xl = swap_narrow(other_rows(tie(large_maps, (log[1], log_two[0])), here))
    pair_one = (one, log[-1])
    small_steps, large_steps, live_counts = tie((small_steps, large_steps, live_counts), log[2])
    sc = jnp.concatenate([here[None].astype(jnp.int32), live_counts[0]])

    own_small = lax.dynamic_slice_in_dim(small_steps, here * small.own, small.own, 0)
    own_large = lax.dynamic_slice_in_dim(large_steps, here * large.own, large.own, 0)
    own_steps = jnp.pad(
        jnp.concatenate([own_small, own_large]), (0, 16 - small.own - large.own)
    )
    feats = features(own_steps, jnp.arange(feature_width), feature_width // 2)
    if fits:
        weights_one = (devices, *pair_one)
    else:
        table = slot_table(order)
        kt_one, vec = run_unpack(
            jnp.concatenate(pair_one), table, ((0, cols, True), (cols, cols + 16, False))
        )
        vec = vec[:, :vcols, :16].reshape(channels, 16).T.astype(F32)
        weights_one = (kt_one.reshape(n_wide * cols, 2 * half), vec)

    s_c1, s_u1, s_zh1, s_inv1, *built = run_first(
        small, sc, small_maps, xs, 0, weights_one, dims
    )
    weights_one = built if fits else weights_one
    kt_one, vec = weights_one
    gs = swap_narrow(other_rows(tie(small_cotangent, pair_one[1]), here))
    two, log_two = gather_step(two, log_two, order, s_c1)
    pair_two = (two, log_two[-1])
    xl = tie(xl, (s_c1, log_two[-2], gs))
    l_c1, l_u1, l_zh1, l_inv1 = run_first(
        large, sc, large_maps, xl, 0, weights_one, dims
    )
    gl = swap_narrow(other_rows(tie(large_cotangent, s_c1), here))
    if fits:
        weights_two = (devices, *pair_two, feats)
    else:
        top = cols + time_rows
        both = qcols + pcols
        kt_two, wt, attn = run_unpack(
            jnp.concatenate(pair_two), table,
            ((0, cols, True), (cols, top, True), (top, top + 2 * both, False)),
        )
        wt = wt.reshape(feature_width, 2 * half)
        attn = jnp.concatenate([attn[:, :both], attn[:, both:]], axis=2)
        te = jnp.dot(feats, wt, preferred_element_type=F32) + vec[7] + vec[6]
        weights_two = (
            te, kt_two.reshape(n_wide * cols, 2 * half),
            attn[:, :qcols].reshape(3 * channels, channels),
            attn[:, qcols:].reshape(channels, channels),
        )

    (s_u2, s_zh2, s_inv2, s_gc2, s_mine, s_send, aq, ao, av, *built) = run_middle(
        small, sc, s_c1, small_maps, xs, 0, small_cotangent, gs, weights_two, vec, None, 0,
        dims
    )
    out_arrived = swap_narrow(s_send)
    small_out = put_part(s_mine, out_arrived, here)
    weights_two = built if fits else weights_two
    kt_two = weights_two[1]
    (l_u2, l_zh2, l_inv2, l_gc2, l_mine, l_send, aq, ao, av) = run_middle(
        large, sc, l_c1, large_maps, xl, 0, large_cotangent, gl, weights_two,
        vec, (aq, ao, av), small.own, dims,
    )
    s_gc2 = tie(s_gc2, (out_arrived, l_gc2))
    out_arrived = swap_narrow(l_send)
    large_out = put_part(l_mine, out_arrived, here)

    s_gc1, av, ge, ak = run_second_back(
        small, sc, s_gc2, s_u2, s_zh2, s_inv2, kt_two, vec, av, None, None, dims
    )
    if fits:
        l_gc1, av, keep, send = run_second_back(
            large, sc, l_gc2, l_u2, l_zh2, l_inv2, kt_two, vec, av, ak,
            (devices, aq, ao, feats, ge), dims,
        )
    else:
        l_gc1, av, l_ge, ak = run_second_back(
            large, sc, l_gc2, l_u2, l_zh2, l_inv2, kt_two, vec, av, ak, None, dims
        )
        ge = jnp.concatenate([ge[:8], l_ge[:8]])
        gwt = jnp.dot(feats.astype(F32).T, ge, precision=PRECISE)
        packed = run_pack(
            (
                ak.reshape(n_wide, cols, 256), gwt.reshape(n_wide, time_rows, 256),
                aq.reshape(-1, qcols, 256), ao.reshape(-1, pcols, 256),
            ),
            devices, (True, True, False, False),
        )
        attn = jnp.concatenate(packed[2:], axis=1)
        slots = jnp.concatenate(
            [packed[0], packed[1], attn[:, :, :128], attn[:, :, 128:]], axis=1
        )
        keep, send = slots[:n_wide], slots[n_wide:]
    back = list(reversed(order))
    two = scatter_step((keep, send), back[0])
    s_gc1 = tie(s_gc1, (out_arrived, l_gc1))
    s_mine, s_send, av = run_first_back(
        small, sc, s_gc1, s_zh1, s_inv1, s_gc2, kt_one, vec, av, False
    )
    grad_arrived = swap_narrow(s_send)
    s_gc1 = tie(s_gc1, (av, two))
    two = scatter_step(two, back[1])
    ak = run_first_weight(small, sc, s_gc1, s_u1, None, None, dims)
    if fits:
        one = run_first_weight(large, sc, l_gc1, l_u1, ak, devices, dims)
    else:
        ak = run_first_weight(large, sc, l_gc1, l_u1, ak, None, dims)
        slots = run_pack((ak.reshape(n_wide, cols, 256),), devices, (True,))[0]
        one = (slots[:n_wide], slots[n_wide:])
    one = scatter_step(one, back[0])
    l_gc1 = tie(l_gc1, one)
    two = scatter_step(two, back[2])
    l_mine, l_send, av = run_first_back(
        large, sc, l_gc1, l_zh1, l_inv1, l_gc2, kt_one, vec, av, True
    )
    large_arrived = swap_narrow(l_send)
    two = tie(two, av)
    arrived = None
    last = len(back) - 1
    for i in range(1, last + 1):
        one = scatter_step(one, back[i], i == last)
        if i == 1:
            arrived = lax.all_to_all(
                tie(av, one).reshape(2 * n_wide, vcols, 128), ("wide", "narrow"), split_axis=0,
                concat_axis=0, tiled=True,
            )
        if i > 2:
            two = scatter_step(two, back[i], i == last)
        if i == last - 1:
            late = one
    small_grad = put_part(s_mine, tie(grad_arrived, late), here)
    large_grad = put_part(l_mine, tie(large_arrived, late), here)
    arrived = tie(arrived, late)
    sum_one, sum_two = one, two
    sum_vec = arrived.sum(axis=0)[:, :12].T

    top = cols + time_rows
    both = qcols + pcols
    time_sum = sum_two[cols:top]
    attn_sum = jnp.concatenate([sum_two[top : top + both], sum_two[top + both :]], axis=1)
    one_new = adam_step(
        first_conv, sum_one.T, first_conv_mean, first_conv_square, RATE_CONV, DECAY
    )
    two_new = adam_step(
        second_conv, sum_two[:cols].T, second_conv_mean, second_conv_square, RATE_CONV, DECAY
    )
    time_new = adam_step(
        time_dense, time_sum, time_dense_mean, time_dense_square, RATE_TIME, DECAY
    )
    qkv_new = adam_step(
        attn_qkv, attn_sum[:qcols].T, attn_qkv_mean, attn_qkv_square, RATE_QKV, DECAY
    )
    proj_new = adam_step(
        attn_proj, attn_sum[qcols:].T, attn_proj_mean, attn_proj_square, RATE_PROJ, DECAY
    )
    vec_new = adam_step(vectors, sum_vec, vectors_mean, vectors_square, RATE_VECTOR, 0.0)
    return (
        small_out, large_out, small_grad, large_grad,
        *one_new, *two_new, *time_new, *qkv_new, *proj_new, *vec_new,
    )


def solution(mesh):
    maps = P("wide", None, None, "narrow")
    conv = P("narrow", "wide")
    dense = P("wide", "narrow")
    attn = P(None, ("wide", "narrow"))
    return jax.shard_map(
        per_device,
        mesh=mesh,
        in_specs=(
            maps, maps, P("wide"), P("wide"), P("wide", None), maps, maps,
            conv, conv, dense, attn, attn, attn,
            conv, conv, conv, conv, dense, dense, attn, attn, attn, attn, attn, attn,
        ),
        out_specs=(maps,) * 4 + (conv,) * 6 + (dense,) * 3 + (attn,) * 9,
        check_vma=False,
    )
```

```python
import functools
import math

import jax
import jax.numpy as jnp
from jax import lax
from jax.experimental import pallas as pl
from jax.experimental.pallas import tpu as pltpu
from jax.sharding import PartitionSpec as P

GROUPS = 32
STEP_NUMBER = 10
NORM_EPS = 1e-05
ADAM_ONE = 0.9
ADAM_TWO = 0.999
ADAM_EPS = 1e-08
DECAY = 0.01
RATE_CONV = 0.08
RATE_TIME = 0.1
RATE_QKV = 0.2
RATE_PROJ = 1.0
RATE_VECTOR = 1.5
LOG_PERIOD = math.log(10000.0)
PRECISE = lax.Precision.HIGHEST
BF = jnp.bfloat16
F32 = jnp.float32
BLOCK_ROWS = 1024
PASS_ROWS = 64
PART_ROWS = 256
SOFT_ROWS = 16
VMEM_LIMIT = 28 * 2**20
NT = (((1,), (1,)), ((), ()))
TN = (((0,), (0,)), ((), ()))


def dot(a, b, dims=(((1,), (0,)), ((), ()))):
    return lax.dot_general(a, b, dims, preferred_element_type=F32)


def swap_narrow(x):
    return lax.ppermute(x, "narrow", [(0, 1), (1, 0)])


def swap_wide(x, bit):
    count = lax.axis_size("wide")
    return lax.ppermute(x, "wide", [(i, i ^ (1 << bit)) for i in range(count)])


def swap(x, step):
    return swap_narrow(x) if step == "n" else swap_wide(x, step)


def tie(x, after):
    return lax.optimization_barrier((x, after))[0]


def gather_order():
    bits = (lax.axis_size("wide") - 1).bit_length()
    return ["n"] + list(range(bits - 1, -1, -1))


def gather_step(slots, log, order, after=None):
    if log:
        last = log[-1]
        if after is not None:
            last = tie(last, after)
        slots = jnp.concatenate([slots, last], axis=0)
    elif after is not None:
        slots = tie(slots, after)
    return slots, log + [swap(slots, order[len(log)])]


def scatter_step(pair, step, last=False, hold=None):
    keep, send = pair
    arrived = swap(send, step)
    if hold is not None:
        arrived = tie(arrived, hold)
    keep = keep.astype(F32) + arrived.astype(F32)
    if last:
        return keep[0]
    half = keep.shape[0] // 2
    return keep[:half], keep[half:].astype(BF)


def slot_of(order, delta_wide, delta_narrow):
    slot = 0
    for i, step in enumerate(order):
        bit = delta_narrow if step == "n" else (delta_wide >> step) & 1
        slot = slot + (bit << i)
    return slot


def slot_table(order):
    here_wide = lax.axis_index("wide")
    here_narrow = lax.axis_index("narrow")
    wide = jnp.arange(lax.axis_size("wide"), dtype=jnp.int32)[:, None] ^ here_wide
    narrow = jnp.arange(lax.axis_size("narrow"), dtype=jnp.int32)[None, :] ^ here_narrow
    return slot_of(order, wide, narrow).reshape(-1)


def device_table(order):
    here_wide = lax.axis_index("wide")
    here_narrow = lax.axis_index("narrow")
    slots = jnp.arange(lax.axis_size("wide") * lax.axis_size("narrow"), dtype=jnp.int32)
    wide = jnp.zeros_like(slots)
    narrow = jnp.zeros_like(slots)
    for i, step in enumerate(order):
        bit = (slots >> i) & 1
        if step == "n":
            narrow = narrow + bit
        else:
            wide = wide + (bit << step)
    return (wide ^ here_wide) * 2 + (narrow ^ here_narrow)


def prepare_kernel(first, second, dense, qkv, proj, vectors, one, two, attn_s, vec_s):
    cols = first.shape[0]
    top = cols + dense.shape[0]
    qcols, pcols = qkv.shape[0], proj.shape[0]
    both = qcols + pcols
    one[0:cols, :] = first[...].astype(BF)
    two[0:cols, :] = second[...].astype(BF)
    two[cols:top, :] = dense[...].astype(BF)
    attn_s[0:qcols, :] = qkv[...]
    attn_s[qcols:both, :] = proj[...]
    two[top : top + both, :] = attn_s[:, 0:128].astype(BF)
    two[top + both : top + 2 * both, :] = attn_s[:, 128:256].astype(BF)
    vec_s[...] = jnp.zeros_like(vec_s)
    vec_s[0 : vectors.shape[0], 0 : vectors.shape[1]] = vectors[...]
    one[cols : cols + 16, :] = vec_s[...].astype(BF)


def run_prepare(first, second, dense, qkv, proj, vectors):
    cols = first.shape[0]
    both = qkv.shape[0] + proj.shape[0]
    rows = cols + dense.shape[0] + 2 * both
    args = (first, second, dense, qkv, proj, vectors)

    def spec(shape):
        return pl.BlockSpec(shape, lambda i: (0, 0))

    return pl.pallas_call(
        prepare_kernel,
        grid=(1,),
        in_specs=[spec(x.shape) for x in args],
        out_specs=[spec((cols + 16, 128)), spec((rows, 128))],
        out_shape=[
            jax.ShapeDtypeStruct((cols + 16, 128), BF), jax.ShapeDtypeStruct((rows, 128), BF)
        ],
        scratch_shapes=[pltpu.VMEM((both, 256), F32), pltpu.VMEM((16, 128), F32)],
        compiler_params=pltpu.CompilerParams(vmem_limit_bytes=60 * 2**20),
    )(*args)


def unpack_kernel(table, src, *outs, parts):
    def body(place, carry):
        slot = table[place]
        for out, (start, stop, joined) in zip(outs, parts):
            block = src[slot, start:stop, :]
            if joined:
                lanes = pl.ds(pl.multiple_of((place & 1) * 128, 128), 128)
                out[place >> 1, :, lanes] = block
            else:
                out[place] = block
        return carry

    lax.fori_loop(0, src.shape[0], body, 0)


def run_unpack(slots, table, parts):
    count, _, width = slots.shape
    shapes = []
    for start, stop, joined in parts:
        shape = (count // 2, stop - start, 256) if joined else (count, stop - start, width)
        shapes.append(jax.ShapeDtypeStruct(shape, slots.dtype))
    return pl.pallas_call(
        functools.partial(unpack_kernel, parts=parts),
        in_specs=[
            pl.BlockSpec(memory_space=pltpu.SMEM),
            pl.BlockSpec(memory_space=pltpu.VMEM),
        ],
        out_specs=[pl.BlockSpec(memory_space=pltpu.VMEM)] * len(parts),
        out_shape=shapes,
        compiler_params=pltpu.CompilerParams(vmem_limit_bytes=VMEM_LIMIT),
    )(table, slots)


def pack_kernel(table, *refs, joined):
    ins = refs[: len(joined)]
    outs = refs[len(joined) :]

    def body(slot, carry):
        place = table[slot]
        for src, out, lanes_joined in zip(ins, outs, joined):
            if lanes_joined:
                lanes = pl.ds(pl.multiple_of((place & 1) * 128, 128), 128)
                out[slot] = src[place >> 1, :, lanes].astype(BF)
            else:
                out[slot] = src[place].astype(BF)
        return carry

    lax.fori_loop(0, outs[0].shape[0], body, 0)


def run_pack(arrays, table, joined):
    shapes = []
    for array, halves in zip(arrays, joined):
        count, rows, width = array.shape
        shape = (count * 2, rows, 128) if halves else (count, rows, width)
        shapes.append(jax.ShapeDtypeStruct(shape, BF))
    return pl.pallas_call(
        functools.partial(pack_kernel, joined=joined),
        in_specs=[pl.BlockSpec(memory_space=pltpu.SMEM)]
        + [pl.BlockSpec(memory_space=pltpu.VMEM)] * len(arrays),
        out_specs=[pl.BlockSpec(memory_space=pltpu.VMEM)] * len(arrays),
        out_shape=shapes,
        compiler_params=pltpu.CompilerParams(vmem_limit_bytes=VMEM_LIMIT),
    )(table, *arrays)


def group_total(s):
    lane = lax.broadcasted_iota(jnp.int32, s.shape, 1)
    width = s.shape[1]
    for k in (1, 2, 4):
        s = s + jnp.where((lane & k) == 0, pltpu.roll(s, width - k, 1), pltpu.roll(s, k, 1))
    return s


def rows_sum(z):
    return jnp.sum(z, axis=0, keepdims=True)


def eight_sum(z):
    return jnp.sum(z.reshape(z.shape[0] // 8, 8, z.shape[1]), axis=0)


def stack_rows(rows):
    return rows[0] if len(rows) == 1 else jnp.concatenate(rows, axis=0)


def add_to(total, part):
    return part if total is None else total + part


def norm_from_sums(base, one, two, pixels):
    own = one * (1.0 / pixels)
    center = base + own
    mean = group_total(center) * 0.125
    off = center - mean
    spread = group_total(two - one * own + off * off * pixels) * (1.0 / (8 * pixels))
    return mean, lax.rsqrt(spread + NORM_EPS)


def norm_stats(get, n, pixels):
    base, one, two = [], [], []
    for m in range(n):
        first = get(m, 0, 8)[0:1]
        base.append(first)
        s1 = s2 = None
        for r in range(0, pixels, PASS_ROWS):
            d = get(m, r, PASS_ROWS) - first
            s1 = add_to(s1, eight_sum(d))
            s2 = add_to(s2, eight_sum(d * d))
        one.append(rows_sum(s1))
        two.append(rows_sum(s2))
    return norm_from_sums(stack_rows(base), stack_rows(one), stack_rows(two), pixels)


def sigmoid(v):
    return 0.5 * jnp.tanh(0.5 * v) + 0.5


def shift_store(dst, m, start, value, breadth, forward):
    pixels, channels = value.shape
    column = lax.broadcasted_iota(jnp.int32, value.shape, 0) & (breadth - 1)
    before = jnp.where(column == 0, 0.0, pltpu.roll(value, 1, 0)).astype(BF)
    after = jnp.where(column == breadth - 1, 0.0, pltpu.roll(value, pixels - 1, 0)).astype(BF)
    lo, hi = (before, after) if forward else (after, before)
    rows = slice(breadth + start, breadth + start + pixels)
    dst[m, rows, 0:channels] = lo
    dst[m, rows, channels : 2 * channels] = value.astype(BF)
    dst[m, rows, 2 * channels :] = hi


def shift_all(dst, src, n, pixels, breadth):
    for m in range(n):
        for r in range(0, pixels, PASS_ROWS):
            at = m * pixels + r
            shift_store(dst, m, r, src[at : at + PASS_ROWS, :].astype(F32), breadth, False)


def zero_edges(dst, breadth):
    n, rows, width = dst.shape
    edge = jnp.zeros((n, breadth, width), BF)
    dst[:, 0:breadth, :] = edge
    dst[:, rows - breadth :, :] = edge


def half_lanes(place):
    return pl.ds(pl.multiple_of(place * 128, 128), 128)


def join_halves(place, own, other, dst):
    dst[:, half_lanes(place)] = own[...].reshape(dst.shape[0], 128)
    dst[:, half_lanes(1 - place)] = other[...]


def conv_part(shifted, kt, m, start, count, breadth):
    total = None
    for p in range(3):
        for q in range(3):
            tap = 3 * p + q
            first = p * breadth + start
            window = shifted[m, first : first + count, q * 256 : (q + 1) * 256]
            total = add_to(total, dot(window, kt[tap * 256 : (tap + 1) * 256, :], NT))
    return total


def back_part(shifted, kt, m, start, count, breadth):
    parts = []
    for p in range(3):
        first = (2 - p) * breadth + start
        parts.append(shifted[m, first : first + count, :])
    return dot(jnp.concatenate(parts, axis=1), kt[...])


def conv_weight(shifted, act, acc, n, pixels, breadth):
    for p in range(3):
        start = (2 - p) * breadth
        window = shifted[:, start : start + pixels, :].reshape(n * pixels, 768)
        acc[p * 768 : (p + 1) * 768, :] += dot(window, act, TN)


def activate(get, mean, inverse, gain, shift, n, pixels, breadth, zh_o, u_o, shifted):
    for m in range(n):
        scale = inverse[m : m + 1, :]
        offset = -mean[m : m + 1, :] * scale
        for r in range(0, pixels, PASS_ROWS):
            rows = slice(m * pixels + r, m * pixels + r + PASS_ROWS)
            zh = get(m, r, PASS_ROWS) * scale + offset
            zh_o[rows, :] = zh.astype(BF)
            a = zh * gain + shift
            u = a * sigmoid(a)
            u_o[rows, :] = u.astype(BF)
            shift_store(shifted, m, r, u, breadth, True)


def each_slot(places, low, high, body):
    count = low.shape[0]

    def step(i, carry):
        body(low, i, places[i])
        body(high, i, places[count + i])
        return carry

    lax.fori_loop(0, count, step, 0)


def lanes_of(place):
    return pl.ds(pl.multiple_of((place & 1) * 128, 128), 128)


def rows_of(index, count, unit):
    return pl.ds(pl.multiple_of(index * count, unit), count)


def first_kernel(sc, *refs, n, height, breadth, build, cols, vcols):
    pixels = height * breadth
    if build:
        (places, xa, xb, low, high, c1_o, u1_o, zh_o, inv_o, kt, vec, x_s, shifted, vt) = refs
    else:
        (xa, xb, kt, vec, c1_o, u1_o, zh_o, inv_o, x_s, shifted) = refs
    join_halves(sc[0], xa, xb, x_s)

    @pl.when(pl.program_id(0) == 0)
    def _():
        zero_edges(shifted, breadth)
        if build:

            def fill(ref, i, place):
                kt[rows_of(place >> 1, cols, 16), lanes_of(place)] = ref[i, 0:cols, :]
                extra = ref[i, cols : cols + 16, :].astype(F32)
                vt[rows_of(place, vcols, 8), :] = extra[0:vcols]

            each_slot(places, low, high, fill)
            vec[...] = vt[...].T[0:16, :]

    def get(m, r, count):
        return x_s[m * pixels + r : m * pixels + r + count, :].astype(F32)

    mean, inverse = norm_stats(get, n, pixels)
    inv_o[0, 0:n, :] = inverse
    activate(
        get, mean, inverse, vec[0:1, :], vec[1:2, :], n, pixels, breadth, zh_o, u1_o, shifted
    )
    for m in range(n):
        first = s1 = s2 = None
        for r in range(0, pixels, PART_ROWS):
            part = conv_part(shifted, kt, m, r, PART_ROWS, breadth)
            c1_o[m * pixels + r : m * pixels + r + PART_ROWS, :] = part
            first = part[0:1] if first is None else first
            d = part - first
            s1 = add_to(s1, eight_sum(d))
            s2 = add_to(s2, eight_sum(d * d))
        inv_o[0, 8 + m : 9 + m, :] = first
        inv_o[0, 16 + m : 17 + m, :] = rows_sum(s1)
        inv_o[0, 24 + m : 25 + m, :] = rows_sum(s2)


def middle_kernel(
    sc, *refs, n, height, breadth, own, which, first_call, build, cols, time_rows, qcols, pcols,
    first_map,
):
    pixels = height * breadth
    step = pl.program_id(0)
    refs = list(refs)

    def take(count):
        taken = refs[:count]
        del refs[:count]
        return taken

    if build:
        (places,) = take(1)
    c1, st, xa, xb, ga, gb = take(6)
    if build:
        low, high, feats = take(3)
    else:
        te, kt, wqkv, wo = take(4)
    (vec,) = take(1)
    if not first_call:
        aq_i, ao_i, av_i = take(3)
    u2_o, zh2_o, inv2_o, gc2_o, mine_o, send_o, aq, ao, av = take(9)
    if build:
        te, kt, wqkv, wo = take(4)
    (x_s, gy_s, shifted, h_s, zh3_s, hn_s, qkv_s, o_s, go_s, j_s, gk_s, gv_s) = take(12)
    s_s, gp_s, p_s16, gs_s16 = take(4)
    if build:
        wt_s, q_s, p_s = take(3)
    join_halves(sc[0], xa, xb, x_s)
    join_halves(sc[0], ga, gb, gy_s)

    @pl.when(step == 0)
    def _():
        zero_edges(shifted, breadth)
        aq[...] = jnp.zeros_like(aq) if first_call else aq_i[...]
        ao[...] = jnp.zeros_like(ao) if first_call else ao_i[...]
        av[...] = jnp.zeros_like(av) if first_call else av_i[...]
        if build:
            top = cols + time_rows
            both = qcols + pcols

            def fill(ref, i, place):
                kt[rows_of(place >> 1, cols, 16), lanes_of(place)] = ref[i, 0:cols, :]
                wt_s[rows_of(place >> 1, time_rows, 16), lanes_of(place)] = ref[i, cols:top, :]
                attn = ref[i, top : top + 2 * both, :].astype(F32)
                for part in range(2):
                    lanes = slice(part * 128, (part + 1) * 128)
                    start = part * both
                    q_s[rows_of(place, qcols, 8), lanes] = attn[start : start + qcols]
                    p_s[rows_of(place, pcols, 8), lanes] = attn[start + qcols : start + both]

            each_slot(places, low, high, fill)
            wqkv[...] = q_s[...].astype(BF)
            wo[...] = p_s[...].astype(BF)
            te[...] = dot(feats[...], wt_s[...]) + vec[6:7, :] + vec[7:8, :]

    items = [(m, r) for m in range(n) for r in range(0, pixels, PART_ROWS)]

    def at(m, r, count=PART_ROWS):
        return slice(m * pixels + r, m * pixels + r + count)

    live = []
    sum_gy = None
    for m in range(n):
        slot = sc[0] * own + step * n + m
        live.append((slot < sc[1 + which]).astype(F32))
        for r in range(0, pixels, PASS_ROWS):
            gy = gy_s[at(m, r, PASS_ROWS), :].astype(F32) * live[m]
            sum_gy = add_to(sum_gy, eight_sum(gy))
            gy_s[at(m, r, PASS_ROWS), :] = gy.astype(BF)

    extra = stack_rows([te[pl.ds(first_map + step * n + m, 1), :] for m in range(n)])
    mean, inverse = norm_from_sums(
        st[0, 8 : 8 + n, :] + extra, st[0, 16 : 16 + n, :], st[0, 24 : 24 + n, :], pixels
    )
    inv2_o[0, 0:n, :] = inverse

    def get_c1(m, r, count):
        return c1[at(m, r, count), :]

    activate(
        get_c1, mean - extra, inverse, vec[2:3, :], vec[3:4, :], n, pixels, breadth,
        zh2_o, u2_o, shifted,
    )
    for m, r in items:
        go_s[at(m, r), :] = dot(gy_s[at(m, r), :], wo[...]).astype(BF)
    base, one, two = [], [], []
    for m in range(n):
        first = s1 = s2 = None
        for r in range(0, pixels, PART_ROWS):
            part = conv_part(shifted, kt, m, r, PART_ROWS, breadth)
            part = part + vec[8:9, :] + x_s[at(m, r), :].astype(F32)
            h_s[at(m, r), :] = part
            first = part[0:1] if first is None else first
            d = part - first
            s1 = add_to(s1, eight_sum(d))
            s2 = add_to(s2, eight_sum(d * d))
        base.append(first)
        one.append(rows_sum(s1))
        two.append(rows_sum(s2))

    mean, inverse3 = norm_from_sums(stack_rows(base), stack_rows(one), stack_rows(two), pixels)
    for m, r in items:
        scale = inverse3[m : m + 1, :]
        offset = -mean[m : m + 1, :] * scale
        for k in range(r, r + PART_ROWS, PASS_ROWS):
            zh = h_s[at(m, k, PASS_ROWS), :] * scale + offset
            zh3_s[at(m, k, PASS_ROWS), :] = zh.astype(BF)
            hn_s[at(m, k, PASS_ROWS), :] = (zh * vec[4:5, :] + vec[5:6, :]).astype(BF)
        for part in range(3):
            lanes = slice(part * 256, (part + 1) * 256)
            projected = dot(hn_s[at(m, r), :], wqkv[lanes, :], NT)
            if part == 0:
                projected = projected + vec[9:10, :]
            if part == 2:
                projected = projected + vec[10:11, :]
            qkv_s[at(m, r), lanes] = projected.astype(BF)

    scale = 1.0 / math.sqrt(256)

    def map_rows(m):
        return slice(m * pixels, (m + 1) * pixels)

    def scores_of(i):
        m, r = items[i]
        s_s[i % 2] = dot(qkv_s[at(m, r), 0:256], qkv_s[map_rows(m), 256:512], NT)
        gp_s[i % 2] = dot(go_s[at(m, r), :], qkv_s[map_rows(m), 512:768], NT)

    sum_q = None
    sum_v = None
    scores_of(0)
    for i, (m, r) in enumerate(items):
        if i + 1 < len(items):
            scores_of(i + 1)
        for k in range(0, PART_ROWS, SOFT_ROWS):
            rows = slice(k, k + SOFT_ROWS)
            scores = s_s[i % 2, rows, :]
            top = jnp.max(scores, axis=1, keepdims=True)
            exponent = jnp.exp((scores - top) * scale)
            probs = exponent * (1.0 / jnp.sum(exponent, axis=1, keepdims=True))
            p_s16[i % 2, rows, :] = probs.astype(BF)
            weighted = probs * gp_s[i % 2, rows, :]
            inner = jnp.sum(weighted, axis=1, keepdims=True)
            gs_s16[i % 2, rows, :] = (weighted - probs * inner).astype(BF)
        keys = qkv_s[map_rows(m), 256:512]
        values = qkv_s[map_rows(m), 512:768]
        low = p_s16[i % 2]
        grad_s = gs_s16[i % 2]
        o_s[at(m, r), :] = dot(low, values).astype(BF)
        grad_q = dot(grad_s, keys) * scale
        sum_q = add_to(sum_q, eight_sum(grad_q))
        j_s[at(m, r), 0:256] = grad_q.astype(BF)
        grad_k = dot(grad_s, qkv_s[at(m, r), 0:256], TN)
        grad_v = dot(low, go_s[at(m, r), :], TN)
        if r > 0:
            grad_k = grad_k + gk_s[...]
            grad_v = grad_v + gv_s[...]
        if r + PART_ROWS < pixels:
            gk_s[...] = grad_k
            gv_s[...] = grad_v
        else:
            j_s[map_rows(m), 256:512] = (grad_k * scale).astype(BF)
            sum_v = add_to(sum_v, eight_sum(grad_v))
            j_s[map_rows(m), 512:768] = grad_v.astype(BF)

    gain = vec[4:5, :]
    one, two = [], []
    for m in range(n):
        s1 = s2 = None
        for r in range(0, pixels, PART_ROWS):
            low = dot(j_s[at(m, r), :], wqkv[...]).astype(BF)
            hn_grad = low.astype(F32)
            go_s[at(m, r), :] = low
            s1 = add_to(s1, eight_sum(hn_grad))
            s2 = add_to(s2, eight_sum(hn_grad * zh3_s[at(m, r), :].astype(F32)))
        one.append(rows_sum(s1))
        two.append(rows_sum(s2))
    one = stack_rows(one)
    two = stack_rows(two)
    mean_one = group_total(one * gain) * (1.0 / (8 * pixels))
    mean_two = group_total(two * gain) * (1.0 / (8 * pixels))

    ao[...] += dot(gy_s[...], o_s[...], TN)
    aq[...] += dot(j_s[...], hn_s[...], TN)

    for m, r in items:
        branch = (dot(o_s[at(m, r), :], wo[...], NT) + vec[11:12, :]).astype(BF).astype(F32)
        x_s[at(m, r), :] = ((h_s[at(m, r), :] + branch) * live[m]).astype(BF)
    for m in range(n):
        own_half = x_s[map_rows(m), half_lanes(sc[0])]
        other_half = x_s[map_rows(m), half_lanes(1 - sc[0])]
        mine_o[m] = own_half.reshape(height, breadth, 128)
        send_o[m] = other_half.reshape(height, breadth, 128)

    bias = None
    for m in range(n):
        scale_d = inverse3[m : m + 1, :] * gain
        offset = inverse3[m : m + 1, :] * mean_one[m : m + 1, :]
        scale_z = inverse3[m : m + 1, :] * mean_two[m : m + 1, :]
        for r in range(0, pixels, PASS_ROWS):
            rows = at(m, r, PASS_ROWS)
            gz = (
                go_s[rows, :].astype(F32) * scale_d - offset - zh3_s[rows, :].astype(F32) * scale_z
            )
            low = (gz + gy_s[rows, :].astype(F32)).astype(BF)
            gc2_o[rows, :] = low
            bias = add_to(bias, eight_sum(low.astype(F32)))
    av[4:5, :] += rows_sum(two)
    av[5:6, :] += rows_sum(one)
    av[8:9, :] += rows_sum(bias)
    av[9:10, :] += rows_sum(sum_q)
    av[10:11, :] += rows_sum(sum_v)
    av[11:12, :] += rows_sum(sum_gy)


def conv_norm_back(
    shifted, kt, d_s, zh_ref, inv_ref, gain, shift, n, pixels, breadth, between, emit
):
    one, two = [], []
    for m in range(n):
        s1 = s2 = None
        for r in range(0, pixels, PART_ROWS):
            rows = slice(m * pixels + r, m * pixels + r + PART_ROWS)
            grad_act = back_part(shifted, kt, m, r, PART_ROWS, breadth)
            zh = zh_ref[rows, :].astype(F32)
            a = zh * gain + shift
            s = sigmoid(a)
            d = grad_act * (s * (1.0 + a * (1.0 - s)))
            d_s[rows, :] = d
            s1 = add_to(s1, eight_sum(d))
            s2 = add_to(s2, eight_sum(d * zh))
        one.append(rows_sum(s1))
        two.append(rows_sum(s2))
    one = stack_rows(one)
    two = stack_rows(two)
    mean_one = group_total(one * gain) * (1.0 / (8 * pixels))
    mean_two = group_total(two * gain) * (1.0 / (8 * pixels))
    between()
    for m in range(n):
        inverse = inv_ref[0, m : m + 1, :]
        scale_d = inverse * gain
        offset = inverse * mean_one[m : m + 1, :]
        scale_z = inverse * mean_two[m : m + 1, :]
        for r in range(0, pixels, PASS_ROWS):
            rows = slice(m * pixels + r, m * pixels + r + PASS_ROWS)
            zh = zh_ref[rows, :].astype(F32)
            emit(m, r, rows, d_s[rows, :] * scale_d - offset - zh * scale_z)
    return rows_sum(one), rows_sum(two)


def second_back_kernel(
    sc, *refs, n, height, breadth, first_call, pack, cols, time_rows, qcols, pcols
):
    pixels = height * breadth
    step = pl.program_id(0)
    refs = list(refs)

    def take(count):
        taken = refs[:count]
        del refs[:count]
        return taken

    if pack:
        (places,) = take(1)
    gc2, u2, zh2, inv2, kt, vec, av_i = take(7)
    if not first_call:
        (ak_i,) = take(1)
    if pack:
        aq, ao, feats, ge_i = take(4)
    gc1_o, av = take(2)
    if pack:
        keep, send = take(2)
    else:
        ge_o, ak = take(2)
    shifted, d_s = take(2)
    if pack:
        ak, ge_o, wt_s = take(3)

    @pl.when(step == 0)
    def _():
        zero_edges(shifted, breadth)
        ak[...] = jnp.zeros_like(ak) if first_call else ak_i[...]
        av[...] = av_i[...]
        if pack:
            ge_o[...] = ge_i[...]
        else:
            ge_o[...] = jnp.zeros_like(ge_o)

    shift_all(shifted, gc2, n, pixels, breadth)
    sums = [None] * n

    def emit(m, r, rows, grad):
        low = grad.astype(BF)
        gc1_o[rows, :] = low
        sums[m] = add_to(sums[m], eight_sum(low.astype(F32)))

    def between():
        conv_weight(shifted, u2[...], ak, n, pixels, breadth)

    one, two = conv_norm_back(
        shifted, kt, d_s, zh2, inv2, vec[2:3, :], vec[3:4, :], n, pixels, breadth, between, emit
    )
    av[2:3, :] += two
    av[3:4, :] += one
    base = 8 if pack else 0
    for m in range(n):
        ge = rows_sum(sums[m])
        ge_o[pl.ds(base + step * n + m, 1), :] = ge
        av[6:7, :] += ge
        av[7:8, :] += ge

    if pack:

        @pl.when(step == pl.num_programs(0) - 1)
        def _():
            wt_s[...] = lax.dot_general(
                feats[...].astype(F32), ge_o[...], TN, precision=PRECISE,
                preferred_element_type=F32,
            )
            top = cols + time_rows
            both = qcols + pcols

            def fill(ref, i, place):
                lanes = lanes_of(place)
                ref[i, 0:cols, :] = ak[rows_of(place >> 1, cols, 8), lanes].astype(BF)
                ref[i, cols:top, :] = wt_s[rows_of(place >> 1, time_rows, 8), lanes].astype(BF)
                for part in range(2):
                    half = slice(part * 128, (part + 1) * 128)
                    block = jnp.concatenate(
                        [
                            aq[rows_of(place, qcols, 8), half],
                            ao[rows_of(place, pcols, 8), half],
                        ],
                        axis=0,
                    )
                    ref[i, top + part * both : top + (part + 1) * both, :] = block.astype(BF)

            each_slot(places, keep, send, fill)


def first_weight_kernel(sc, *refs, n, height, breadth, first_call, pack, cols):
    pixels = height * breadth
    step = pl.program_id(0)
    if pack:
        places, gc1, u1, ak_i, keep, send, shifted, ak = refs
    elif first_call:
        gc1, u1, ak, shifted = refs
    else:
        gc1, u1, ak_i, ak, shifted = refs

    @pl.when(step == 0)
    def _():
        zero_edges(shifted, breadth)
        ak[...] = jnp.zeros_like(ak) if first_call else ak_i[...]

    shift_all(shifted, gc1, n, pixels, breadth)
    conv_weight(shifted, u1[...], ak, n, pixels, breadth)

    if pack:

        @pl.when(step == pl.num_programs(0) - 1)
        def _():
            def fill(ref, i, place):
                ref[i] = ak[rows_of(place >> 1, cols, 8), lanes_of(place)].astype(BF)

            each_slot(places, keep, send, fill)


def first_back_kernel(
    sc, gc1, zh1, inv1, gc2, kt, vec, av_i, mine_o, send_o, av_o, shifted, d_s, *rest,
    n, height, breadth, last_call,
):
    pixels = height * breadth
    av = rest[0] if last_call else av_o

    @pl.when(pl.program_id(0) == 0)
    def _():
        zero_edges(shifted, breadth)
        av[...] = av_i[...]

    shift_all(shifted, gc1, n, pixels, breadth)

    def emit(m, r, rows, grad):
        d_s[rows, :] = grad + gc2[rows, :].astype(F32)
        lines = slice(r // breadth, (r + PASS_ROWS) // breadth)
        shape = (PASS_ROWS // breadth, breadth, 128)
        mine_o[m, lines] = d_s[rows, half_lanes(sc[0])].reshape(shape)
        send_o[m, lines] = d_s[rows, half_lanes(1 - sc[0])].astype(BF).reshape(shape)

    one, two = conv_norm_back(
        shifted, kt, d_s, zh1, inv1, vec[0:1, :], vec[1:2, :], n, pixels, breadth,
        lambda: None, emit,
    )
    av[0:1, :] += two
    av[1:2, :] += one

    if last_call:

        @pl.when(pl.program_id(0) == pl.num_programs(0) - 1)
        def _():
            padded = jnp.concatenate([av[...], jnp.zeros((112, 256), F32)], axis=0)
            av_o[...] = padded.T


class Group:
    def __init__(self, shape, which):
        self.maps, self.height, self.breadth, self.half = shape
        self.which = which
        self.own = self.maps // 2
        self.pixels = self.height * self.breadth
        self.n = max(1, min(self.own, BLOCK_ROWS // self.pixels))
        self.steps = self.own // self.n
        self.rows = self.n * self.pixels
        self.all_rows = self.own * self.pixels
        self.params = dict(n=self.n, height=self.height, breadth=self.breadth)

    def row_spec(self):
        return pl.BlockSpec((self.rows, 256), lambda i, sc, *_: (i, 0))

    def row_shape(self, dtype):
        return jax.ShapeDtypeStruct((self.all_rows, 256), dtype)

    def map_spec(self, placed):
        steps = self.steps
        shape = (self.n, self.height, self.breadth, 128)
        if placed:
            return pl.BlockSpec(shape, lambda i, sc, *_: (sc[0] * steps + i, 0, 0, 0))
        return pl.BlockSpec(shape, lambda i, sc, *_: (i, 0, 0, 0))

    def flat_spec(self, first):
        first = first // self.rows
        return pl.BlockSpec((self.rows, 128), lambda i, sc, *_: (first + i, 0))

    def map_shape(self, placed, dtype):
        count = self.maps if placed else self.own
        return jax.ShapeDtypeStruct((count, self.height, self.breadth, 128), dtype)

    def stat_spec(self):
        return pl.BlockSpec((1, 32, 256), lambda i, sc, *_: (i, 0, 0))

    def stat_shape(self):
        return jax.ShapeDtypeStruct((self.steps, 32, 256), F32)

    def shifted(self):
        return pltpu.VMEM((self.n, (self.height + 2) * self.breadth, 768), BF)

    def call(self, body, in_specs, out_specs, out_shape, scratch, flops, prefetch=1):
        return pl.pallas_call(
            body,
            grid_spec=pltpu.PrefetchScalarGridSpec(
                num_scalar_prefetch=prefetch,
                grid=(self.steps,),
                in_specs=in_specs,
                out_specs=out_specs,
                scratch_shapes=scratch,
            ),
            out_shape=out_shape,
            compiler_params=pltpu.CompilerParams(vmem_limit_bytes=VMEM_LIMIT),
            cost_estimate=pl.CostEstimate(
                flops=4 * flops, bytes_accessed=self.all_rows * 256 * 8, transcendentals=0
            ),
        )


def whole(shape):
    zeros = (0,) * len(shape)
    return pl.BlockSpec(shape, lambda i, sc, *_: zeros)


def run_first(g, sc, x, x_other, first_row, weights, dims):
    build = len(weights) == 3
    cols, vcols = dims["cols"], dims["vcols"]
    built = [whole((2304, 256)), whole((16, 256))]
    body = functools.partial(first_kernel, build=build, cols=cols, vcols=vcols, **g.params)
    outs = [g.row_spec(), g.row_spec(), g.row_spec(), g.stat_spec()]
    shapes = [g.row_shape(F32), g.row_shape(BF), g.row_shape(BF), g.stat_shape()]
    scratch = [pltpu.VMEM((g.rows, 256), BF), g.shifted()]
    flops = 2 * g.all_rows * 2304 * 256
    maps = [g.map_spec(True), g.flat_spec(first_row)]
    if build:
        places, low, high = weights
        return g.call(
            body,
            maps + [whole(low.shape), whole(high.shape)],
            outs + built,
            shapes
            + [jax.ShapeDtypeStruct((2304, 256), BF), jax.ShapeDtypeStruct((16, 256), F32)],
            scratch + [pltpu.VMEM((256, 128), F32)],
            flops,
            2,
        )(sc, places, x, x_other, low, high)
    return g.call(body, maps + built, outs, shapes, scratch, flops)(sc, x, x_other, *weights)


def run_middle(
    g, sc, c1, st, x, x_other, first_row, gy, gy_other, weights, vec, acc, first_map, dims
):
    build = len(weights) == 4 and weights[0].ndim == 1
    row = g.row_spec()
    big = pltpu.VMEM((g.rows, 256), F32)
    low16 = pltpu.VMEM((g.rows, 256), BF)
    wide = pltpu.VMEM((g.rows, 768), BF)
    body = functools.partial(
        middle_kernel, own=g.own, which=g.which, first_call=acc is None, build=build,
        first_map=first_map, cols=dims["cols"], time_rows=dims["time_rows"],
        qcols=dims["qcols"], pcols=dims["pcols"], **g.params,
    )
    acc_specs = [whole((768, 256)), whole((256, 256)), whole((16, 256))]
    built = [whole((16, 256)), whole((2304, 256)), whole((768, 256)), whole((256, 256))]
    maps = [
        g.map_spec(True), g.flat_spec(first_row), g.map_spec(True), g.flat_spec(0),
    ]
    ins = [row, g.stat_spec()] + maps
    outs = [row, row, g.stat_spec(), row, g.map_spec(True), g.map_spec(False)] + acc_specs
    shapes = [
        g.row_shape(BF), g.row_shape(BF), g.stat_shape(), g.row_shape(BF),
        g.map_shape(True, BF), g.map_shape(False, BF),
        jax.ShapeDtypeStruct((768, 256), F32), jax.ShapeDtypeStruct((256, 256), F32),
        jax.ShapeDtypeStruct((16, 256), F32),
    ]
    scratch = [
        low16, low16, g.shifted(), big, low16, low16, wide, low16, low16, wide,
        pltpu.VMEM((g.pixels, 256), F32), pltpu.VMEM((g.pixels, 256), F32),
        pltpu.VMEM((2, PART_ROWS, g.pixels), F32), pltpu.VMEM((2, PART_ROWS, g.pixels), F32),
        pltpu.VMEM((2, PART_ROWS, g.pixels), BF), pltpu.VMEM((2, PART_ROWS, g.pixels), BF),
    ]
    args = [c1, st, x, x_other, gy, gy_other]
    if build:
        places, low, high, feats = weights
        ins += [whole(low.shape), whole(high.shape), whole(feats.shape)]
        args = [places] + args + [low, high, feats]
        outs += built
        shapes += [
            jax.ShapeDtypeStruct((16, 256), F32), jax.ShapeDtypeStruct((2304, 256), BF),
            jax.ShapeDtypeStruct((768, 256), BF), jax.ShapeDtypeStruct((256, 256), BF),
        ]
        scratch += [
            pltpu.VMEM((feats.shape[1], 256), BF), pltpu.VMEM((768, 256), F32),
            pltpu.VMEM((256, 256), F32),
        ]
    else:
        ins += built
        args += list(weights)
    ins += [whole((16, 256))]
    args += [vec]
    if acc is not None:
        ins += acc_specs
        args += list(acc)
    flops = 2 * g.all_rows * 256 * (2304 + 256 * 12 + 6 * g.pixels)
    return g.call(body, ins, outs, shapes, scratch, flops, 2 if build else 1)(sc, *args)


def run_second_back(g, sc, gc2, u2, zh2, inv2, kt, vec, av, ak, packing, dims):
    row = g.row_spec()
    body = functools.partial(
        second_back_kernel, first_call=ak is None, pack=packing is not None,
        cols=dims["cols"], time_rows=dims["time_rows"], qcols=dims["qcols"],
        pcols=dims["pcols"], **g.params,
    )
    ins = [row, row, row, g.stat_spec(), whole((2304, 256)), whole((16, 256)), whole((16, 256))]
    args = [gc2, u2, zh2, inv2, kt, vec, av]
    outs = [row, whole((16, 256))]
    shapes = [g.row_shape(BF), jax.ShapeDtypeStruct((16, 256), F32)]
    scratch = [g.shifted(), pltpu.VMEM((g.rows, 256), F32)]
    if ak is not None:
        ins += [whole((2304, 256))]
        args += [ak]
    if packing is not None:
        places, aq, ao, feats, ge = packing
        ins += [whole((768, 256)), whole((256, 256)), whole(feats.shape), whole((16, 256))]
        args = [places] + args + [aq, ao, feats, ge]
        slots = (
            dims["places"] // 2,
            dims["cols"] + dims["time_rows"] + 2 * (dims["qcols"] + dims["pcols"]),
            128,
        )
        outs += [whole(slots)] * 2
        shapes += [jax.ShapeDtypeStruct(slots, BF)] * 2
        scratch += [
            pltpu.VMEM((2304, 256), F32), pltpu.VMEM((16, 256), F32),
            pltpu.VMEM((feats.shape[1], 256), F32),
        ]
    else:
        outs += [whole((16, 256)), whole((2304, 256))]
        shapes += [
            jax.ShapeDtypeStruct((16, 256), F32), jax.ShapeDtypeStruct((2304, 256), F32)
        ]
    return g.call(
        body, ins, outs, shapes, scratch, 4 * g.all_rows * 256 * 2304,
        1 if packing is None else 2,
    )(sc, *args)


def run_first_weight(g, sc, gc1, u1, ak, places, dims):
    row = g.row_spec()
    body = functools.partial(
        first_weight_kernel, first_call=ak is None, pack=places is not None,
        cols=dims["cols"], **g.params,
    )
    ins = [row, row]
    args = [gc1, u1]
    scratch = [g.shifted()]
    if ak is not None:
        ins += [whole((2304, 256))]
        args += [ak]
    if places is None:
        outs = whole((2304, 256))
        shapes = jax.ShapeDtypeStruct((2304, 256), F32)
    else:
        args = [places] + args
        slots = (dims["places"] // 2, dims["cols"], 128)
        outs = [whole(slots)] * 2
        shapes = [jax.ShapeDtypeStruct(slots, BF)] * 2
        scratch += [pltpu.VMEM((2304, 256), F32)]
    return g.call(
        body, ins, outs, shapes, scratch, 2 * g.all_rows * 256 * 2304,
        1 if places is None else 2,
    )(sc, *args)


def run_first_back(g, sc, gc1, zh1, inv1, gc2, kt, vec, av, last_call):
    row = g.row_spec()
    shape = (256, 128) if last_call else (16, 256)
    return g.call(
        functools.partial(first_back_kernel, last_call=last_call, **g.params),
        [row, row, g.stat_spec(), row, whole((2304, 256)), whole((16, 256)), whole((16, 256))],
        [g.map_spec(True), g.map_spec(False), whole(shape)],
        [g.map_shape(True, F32), g.map_shape(False, BF), jax.ShapeDtypeStruct(shape, F32)],
        [g.shifted(), pltpu.VMEM((g.rows, 256), F32)]
        + ([pltpu.VMEM((16, 256), F32)] if last_call else []),
        2 * g.all_rows * 256 * 2304,
    )(sc, gc1, zh1, inv1, gc2, kt, vec, av)


def features(steps, index, half_width):
    frequency = jnp.exp(
        (index % half_width).astype(F32) * (-LOG_PERIOD / (half_width - 1))
    )
    angles = steps.astype(F32)[:, None] * frequency[None, :]
    return jax.nn.silu(
        jnp.where(index[None, :] < half_width, jnp.sin(angles), jnp.cos(angles))
    ).astype(BF)


def adam_step(weight, grad, mean, square, rate, decay):
    mean_new = ADAM_ONE * mean + (1.0 - ADAM_ONE) * grad
    square_new = ADAM_TWO * square + (1.0 - ADAM_TWO) * grad * grad
    first_fix = mean_new / (1.0 - ADAM_ONE**STEP_NUMBER)
    second_fix = square_new / (1.0 - ADAM_TWO**STEP_NUMBER)
    weight_new = weight - rate * (first_fix / (jnp.sqrt(second_fix) + ADAM_EPS) + decay * weight)
    return (weight_new, mean_new, square_new)


def other_rows(x, here):
    own = x.shape[0] // 2
    return lax.dynamic_slice_in_dim(x, (1 - here) * own, own, 0).reshape(-1, x.shape[3])


def put_part(full, arrived, here):
    own = arrived.shape[0]
    return lax.dynamic_update_slice_in_dim(
        full, arrived.astype(full.dtype), (1 - here) * own, 0
    )


def per_device(
    small_maps, large_maps, small_steps, large_steps, live_counts,
    small_cotangent, large_cotangent,
    first_conv, second_conv, time_dense, attn_qkv, attn_proj, vectors,
    first_conv_mean, first_conv_square, second_conv_mean, second_conv_square,
    time_dense_mean, time_dense_square, attn_qkv_mean, attn_qkv_square,
    attn_proj_mean, attn_proj_square, vectors_mean, vectors_square,
):
    n_wide = lax.axis_size("wide")
    here = lax.axis_index("narrow")
    channels = attn_qkv.shape[0]
    half = first_conv.shape[0]
    cols = first_conv.shape[1]
    time_rows = time_dense.shape[0]
    feature_width = time_rows * n_wide
    qcols = attn_qkv.shape[1]
    pcols = attn_proj.shape[1]
    vcols = vectors.shape[1]
    dims = dict(
        cols=cols, time_rows=time_rows, qcols=qcols, pcols=pcols, vcols=vcols, places=2 * n_wide
    )
    fits = not (cols % 16 or time_rows % 16 or qcols % 8 or pcols % 8 or vcols % 8)
    order = gather_order()
    devices = device_table(order)
    small = Group(small_maps.shape, 0)
    large = Group(large_maps.shape, 1)

    if fits:
        block_one, block_two = run_prepare(
            first_conv.T, second_conv.T, time_dense, attn_qkv.T, attn_proj.T, vectors.T
        )
    else:
        vec_rows = jnp.pad(
            vectors.astype(BF).T, ((0, 16 - vcols), (0, 128 - vectors.shape[0]))
        )
        block_one = jnp.concatenate([first_conv.astype(BF).T, vec_rows], axis=0)
        attn_rows = jnp.concatenate([attn_qkv.astype(BF).T, attn_proj.astype(BF).T], axis=0)
        block_two = jnp.concatenate(
            [
                second_conv.astype(BF).T, time_dense.astype(BF),
                attn_rows[:, :128], attn_rows[:, 128:],
            ],
            axis=0,
        )
    one, log = block_one[None], []
    for _ in order:
        one, log = gather_step(one, log, order)
    two, log_two = block_two[None], []
    for i in range(len(order) - 1):
        two, log_two = gather_step(two, log_two, order, log[(0, 1, 2)[min(i, 2)]])
    xs = swap_narrow(other_rows(tie(small_maps, (log[0], log_two[0])), here))
    xl = swap_narrow(other_rows(tie(large_maps, (log[1], log_two[0])), here))
    pair_one = (one, log[-1])
    small_steps, large_steps, live_counts = tie((small_steps, large_steps, live_counts), log[2])
    sc = jnp.concatenate([here[None].astype(jnp.int32), live_counts[0]])

    own_small = lax.dynamic_slice_in_dim(small_steps, here * small.own, small.own, 0)
    own_large = lax.dynamic_slice_in_dim(large_steps, here * large.own, large.own, 0)
    own_steps = jnp.pad(
        jnp.concatenate([own_small, own_large]), (0, 16 - small.own - large.own)
    )
    feats = features(own_steps, jnp.arange(feature_width), feature_width // 2)
    if fits:
        weights_one = (devices, *pair_one)
    else:
        table = slot_table(order)
        kt_one, vec = run_unpack(
            jnp.concatenate(pair_one), table, ((0, cols, True), (cols, cols + 16, False))
        )
        vec = vec[:, :vcols, :16].reshape(channels, 16).T.astype(F32)
        weights_one = (kt_one.reshape(n_wide * cols, 2 * half), vec)

    s_c1, s_u1, s_zh1, s_inv1, *built = run_first(
        small, sc, small_maps, xs, 0, weights_one, dims
    )
    weights_one = built if fits else weights_one
    kt_one, vec = weights_one
    gs = swap_narrow(other_rows(tie(small_cotangent, pair_one[1]), here))
    two, log_two = gather_step(two, log_two, order, s_c1)
    pair_two = (two, log_two[-1])
    xl = tie(xl, (s_c1, log_two[-2], gs))
    l_c1, l_u1, l_zh1, l_inv1 = run_first(
        large, sc, large_maps, xl, 0, weights_one, dims
    )
    gl = swap_narrow(other_rows(tie(large_cotangent, s_c1), here))
    if fits:
        weights_two = (devices, *pair_two, feats)
    else:
        top = cols + time_rows
        both = qcols + pcols
        kt_two, wt, attn = run_unpack(
            jnp.concatenate(pair_two), table,
            ((0, cols, True), (cols, top, True), (top, top + 2 * both, False)),
        )
        wt = wt.reshape(feature_width, 2 * half)
        attn = jnp.concatenate([attn[:, :both], attn[:, both:]], axis=2)
        te = jnp.dot(feats, wt, preferred_element_type=F32) + vec[7] + vec[6]
        weights_two = (
            te, kt_two.reshape(n_wide * cols, 2 * half),
            attn[:, :qcols].reshape(3 * channels, channels),
            attn[:, qcols:].reshape(channels, channels),
        )

    (s_u2, s_zh2, s_inv2, s_gc2, s_mine, s_send, aq, ao, av, *built) = run_middle(
        small, sc, s_c1, s_inv1, small_maps, xs, 0, small_cotangent, gs, weights_two, vec, None, 0,
        dims
    )
    out_arrived = swap_narrow(s_send)
    small_out = put_part(s_mine, out_arrived, here)
    weights_two = built if fits else weights_two
    kt_two = weights_two[1]
    (l_u2, l_zh2, l_inv2, l_gc2, l_mine, l_send, aq, ao, av) = run_middle(
        large, sc, l_c1, l_inv1, large_maps, xl, 0, large_cotangent, gl, weights_two,
        vec, (aq, ao, av), small.own, dims,
    )
    s_gc2 = tie(s_gc2, (out_arrived, l_gc2))
    out_arrived = swap_narrow(l_send)
    large_out = put_part(l_mine, out_arrived, here)

    s_gc1, av, ge, ak = run_second_back(
        small, sc, s_gc2, s_u2, s_zh2, s_inv2, kt_two, vec, av, None, None, dims
    )
    if fits:
        l_gc1, av, keep, send = run_second_back(
            large, sc, l_gc2, l_u2, l_zh2, l_inv2, kt_two, vec, av, ak,
            (devices, aq, ao, feats, ge), dims,
        )
    else:
        l_gc1, av, l_ge, ak = run_second_back(
            large, sc, l_gc2, l_u2, l_zh2, l_inv2, kt_two, vec, av, ak, None, dims
        )
        ge = jnp.concatenate([ge[:8], l_ge[:8]])
        gwt = jnp.dot(feats.astype(F32).T, ge, precision=PRECISE)
        packed = run_pack(
            (
                ak.reshape(n_wide, cols, 256), gwt.reshape(n_wide, time_rows, 256),
                aq.reshape(-1, qcols, 256), ao.reshape(-1, pcols, 256),
            ),
            devices, (True, True, False, False),
        )
        attn = jnp.concatenate(packed[2:], axis=1)
        slots = jnp.concatenate(
            [packed[0], packed[1], attn[:, :, :128], attn[:, :, 128:]], axis=1
        )
        keep, send = slots[:n_wide], slots[n_wide:]
    back = list(reversed(order))
    two = scatter_step((keep, send), back[0])
    s_gc1 = tie(s_gc1, (out_arrived, l_gc1))
    ak = run_first_weight(small, sc, s_gc1, s_u1, None, None, dims)
    l_gc1 = tie(l_gc1, (ak, two))
    two = scatter_step(two, back[1])
    if fits:
        one = run_first_weight(large, sc, l_gc1, l_u1, ak, devices, dims)
    else:
        ak = run_first_weight(large, sc, l_gc1, l_u1, ak, None, dims)
        slots = run_pack((ak.reshape(n_wide, cols, 256),), devices, (True,))[0]
        one = (slots[:n_wide], slots[n_wide:])
    s_gc1 = tie(s_gc1, one)
    one = scatter_step(one, back[0])
    s_mine, s_send, av = run_first_back(
        small, sc, s_gc1, s_zh1, s_inv1, s_gc2, kt_one, vec, av, False
    )
    grad_arrived = swap_narrow(s_send)
    l_gc1 = tie(l_gc1, (av, one, two))
    two = scatter_step(two, back[2])
    l_mine, l_send, av = run_first_back(
        large, sc, l_gc1, l_zh1, l_inv1, l_gc2, kt_one, vec, av, True
    )
    large_arrived = swap_narrow(l_send)
    arrived = None
    last = len(back) - 1
    trail = []
    for i in range(1, last + 1):
        one = scatter_step(one, back[i], i == last)
        trail.append(one)
        if i == 1:
            arrived = lax.all_to_all(
                tie(av, one).reshape(2 * n_wide, vcols, 128), ("wide", "narrow"), split_axis=0,
                concat_axis=0, tiled=True,
            )
    late = trail[-2]
    two = tie(two, av)
    for i in range(3, last + 1):
        two = scatter_step(two, back[i], i == last, trail[-3] if i == last else None)
    small_grad = put_part(s_mine, tie(grad_arrived, trail[-3]), here)
    large_grad = put_part(l_mine, tie(large_arrived, late), here)
    arrived = tie(arrived, late)
    sum_one, sum_two = one, two
    sum_vec = arrived.sum(axis=0)[:, :12].T

    top = cols + time_rows
    both = qcols + pcols
    time_sum = sum_two[cols:top]
    attn_sum = jnp.concatenate([sum_two[top : top + both], sum_two[top + both :]], axis=1)
    one_new = adam_step(
        first_conv, sum_one.T, first_conv_mean, first_conv_square, RATE_CONV, DECAY
    )
    two_new = adam_step(
        second_conv, sum_two[:cols].T, second_conv_mean, second_conv_square, RATE_CONV, DECAY
    )
    time_new = adam_step(
        time_dense, time_sum, time_dense_mean, time_dense_square, RATE_TIME, DECAY
    )
    qkv_new = adam_step(
        attn_qkv, attn_sum[:qcols].T, attn_qkv_mean, attn_qkv_square, RATE_QKV, DECAY
    )
    proj_new = adam_step(
        attn_proj, attn_sum[qcols:].T, attn_proj_mean, attn_proj_square, RATE_PROJ, DECAY
    )
    vec_new = adam_step(vectors, sum_vec, vectors_mean, vectors_square, RATE_VECTOR, 0.0)
    return (
        small_out, large_out, small_grad, large_grad,
        *one_new, *two_new, *time_new, *qkv_new, *proj_new, *vec_new,
    )


def solution(mesh):
    maps = P("wide", None, None, "narrow")
    conv = P("narrow", "wide")
    dense = P("wide", "narrow")
    attn = P(None, ("wide", "narrow"))
    return jax.shard_map(
        per_device,
        mesh=mesh,
        in_specs=(
            maps, maps, P("wide"), P("wide"), P("wide", None), maps, maps,
            conv, conv, dense, attn, attn, attn,
            conv, conv, conv, conv, dense, dense, attn, attn, attn, attn, attn, attn,
        ),
        out_specs=(maps,) * 4 + (conv,) * 6 + (dense,) * 3 + (attn,) * 9,
        check_vma=False,
    )
```

```python
import functools
import math

import jax
import jax.numpy as jnp
from jax import lax
from jax.experimental import pallas as pl
from jax.experimental.pallas import tpu as pltpu
from jax.sharding import PartitionSpec as P

GROUPS = 32
STEP_NUMBER = 10
NORM_EPS = 1e-05
ADAM_ONE = 0.9
ADAM_TWO = 0.999
ADAM_EPS = 1e-08
DECAY = 0.01
RATE_CONV = 0.08
RATE_TIME = 0.1
RATE_QKV = 0.2
RATE_PROJ = 1.0
RATE_VECTOR = 1.5
LOG_PERIOD = math.log(10000.0)
PRECISE = lax.Precision.HIGHEST
BF = jnp.bfloat16
F32 = jnp.float32
BLOCK_ROWS = 1024
PASS_ROWS = 64
PART_ROWS = 256
SOFT_ROWS = 16
VMEM_LIMIT = 28 * 2**20
NT = (((1,), (1,)), ((), ()))
TN = (((0,), (0,)), ((), ()))


def dot(a, b, dims=(((1,), (0,)), ((), ()))):
    return lax.dot_general(a, b, dims, preferred_element_type=F32)


def swap_narrow(x):
    return lax.ppermute(x, "narrow", [(0, 1), (1, 0)])


def swap_wide(x, bit):
    count = lax.axis_size("wide")
    return lax.ppermute(x, "wide", [(i, i ^ (1 << bit)) for i in range(count)])


def swap(x, step):
    return swap_narrow(x) if step == "n" else swap_wide(x, step)


def tie(x, after):
    return lax.optimization_barrier((x, after))[0]


def gather_order():
    bits = (lax.axis_size("wide") - 1).bit_length()
    return ["n"] + list(range(bits - 1, -1, -1))


def gather_step(slots, log, order, after=None):
    if log:
        last = log[-1]
        if after is not None:
            last = tie(last, after)
        slots = jnp.concatenate([slots, last], axis=0)
    elif after is not None:
        slots = tie(slots, after)
    return slots, log + [swap(slots, order[len(log)])]


def scatter_step(pair, step, last=False, hold=None):
    keep, send = pair
    arrived = swap(send, step)
    if hold is not None:
        arrived = tie(arrived, hold)
    keep = keep.astype(F32) + arrived.astype(F32)
    if last:
        return keep[0]
    half = keep.shape[0] // 2
    return keep[:half], keep[half:].astype(BF)


def slot_of(order, delta_wide, delta_narrow):
    slot = 0
    for i, step in enumerate(order):
        bit = delta_narrow if step == "n" else (delta_wide >> step) & 1
        slot = slot + (bit << i)
    return slot


def slot_table(order):
    here_wide = lax.axis_index("wide")
    here_narrow = lax.axis_index("narrow")
    wide = jnp.arange(lax.axis_size("wide"), dtype=jnp.int32)[:, None] ^ here_wide
    narrow = jnp.arange(lax.axis_size("narrow"), dtype=jnp.int32)[None, :] ^ here_narrow
    return slot_of(order, wide, narrow).reshape(-1)


def device_table(order):
    here_wide = lax.axis_index("wide")
    here_narrow = lax.axis_index("narrow")
    slots = jnp.arange(lax.axis_size("wide") * lax.axis_size("narrow"), dtype=jnp.int32)
    wide = jnp.zeros_like(slots)
    narrow = jnp.zeros_like(slots)
    for i, step in enumerate(order):
        bit = (slots >> i) & 1
        if step == "n":
            narrow = narrow + bit
        else:
            wide = wide + (bit << step)
    return (wide ^ here_wide) * 2 + (narrow ^ here_narrow)


def prepare_kernel(first, second, dense, qkv, proj, vectors, one, two, attn_s, vec_s):
    cols = first.shape[0]
    top = cols + dense.shape[0]
    qcols, pcols = qkv.shape[0], proj.shape[0]
    both = qcols + pcols
    one[0:cols, :] = first[...].astype(BF)
    two[0:cols, :] = second[...].astype(BF)
    two[cols:top, :] = dense[...].astype(BF)
    attn_s[0:qcols, :] = qkv[...]
    attn_s[qcols:both, :] = proj[...]
    two[top : top + both, :] = attn_s[:, 0:128].astype(BF)
    two[top + both : top + 2 * both, :] = attn_s[:, 128:256].astype(BF)
    vec_s[...] = jnp.zeros_like(vec_s)
    vec_s[0 : vectors.shape[0], 0 : vectors.shape[1]] = vectors[...]
    one[cols : cols + 16, :] = vec_s[...].astype(BF)


def run_prepare(first, second, dense, qkv, proj, vectors):
    cols = first.shape[0]
    both = qkv.shape[0] + proj.shape[0]
    rows = cols + dense.shape[0] + 2 * both
    args = (first, second, dense, qkv, proj, vectors)

    def spec(shape):
        return pl.BlockSpec(shape, lambda i: (0, 0))

    return pl.pallas_call(
        prepare_kernel,
        grid=(1,),
        in_specs=[spec(x.shape) for x in args],
        out_specs=[spec((cols + 16, 128)), spec((rows, 128))],
        out_shape=[
            jax.ShapeDtypeStruct((cols + 16, 128), BF), jax.ShapeDtypeStruct((rows, 128), BF)
        ],
        scratch_shapes=[pltpu.VMEM((both, 256), F32), pltpu.VMEM((16, 128), F32)],
        compiler_params=pltpu.CompilerParams(vmem_limit_bytes=60 * 2**20),
    )(*args)


def unpack_kernel(table, src, *outs, parts):
    def body(place, carry):
        slot = table[place]
        for out, (start, stop, joined) in zip(outs, parts):
            block = src[slot, start:stop, :]
            if joined:
                lanes = pl.ds(pl.multiple_of((place & 1) * 128, 128), 128)
                out[place >> 1, :, lanes] = block
            else:
                out[place] = block
        return carry

    lax.fori_loop(0, src.shape[0], body, 0)


def run_unpack(slots, table, parts):
    count, _, width = slots.shape
    shapes = []
    for start, stop, joined in parts:
        shape = (count // 2, stop - start, 256) if joined else (count, stop - start, width)
        shapes.append(jax.ShapeDtypeStruct(shape, slots.dtype))
    return pl.pallas_call(
        functools.partial(unpack_kernel, parts=parts),
        in_specs=[
            pl.BlockSpec(memory_space=pltpu.SMEM),
            pl.BlockSpec(memory_space=pltpu.VMEM),
        ],
        out_specs=[pl.BlockSpec(memory_space=pltpu.VMEM)] * len(parts),
        out_shape=shapes,
        compiler_params=pltpu.CompilerParams(vmem_limit_bytes=VMEM_LIMIT),
    )(table, slots)


def pack_kernel(table, *refs, joined):
    ins = refs[: len(joined)]
    outs = refs[len(joined) :]

    def body(slot, carry):
        place = table[slot]
        for src, out, lanes_joined in zip(ins, outs, joined):
            if lanes_joined:
                lanes = pl.ds(pl.multiple_of((place & 1) * 128, 128), 128)
                out[slot] = src[place >> 1, :, lanes].astype(BF)
            else:
                out[slot] = src[place].astype(BF)
        return carry

    lax.fori_loop(0, outs[0].shape[0], body, 0)


def run_pack(arrays, table, joined):
    shapes = []
    for array, halves in zip(arrays, joined):
        count, rows, width = array.shape
        shape = (count * 2, rows, 128) if halves else (count, rows, width)
        shapes.append(jax.ShapeDtypeStruct(shape, BF))
    return pl.pallas_call(
        functools.partial(pack_kernel, joined=joined),
        in_specs=[pl.BlockSpec(memory_space=pltpu.SMEM)]
        + [pl.BlockSpec(memory_space=pltpu.VMEM)] * len(arrays),
        out_specs=[pl.BlockSpec(memory_space=pltpu.VMEM)] * len(arrays),
        out_shape=shapes,
        compiler_params=pltpu.CompilerParams(vmem_limit_bytes=VMEM_LIMIT),
    )(table, *arrays)


def group_total(s):
    lane = lax.broadcasted_iota(jnp.int32, s.shape, 1)
    width = s.shape[1]
    for k in (1, 2, 4):
        s = s + jnp.where((lane & k) == 0, pltpu.roll(s, width - k, 1), pltpu.roll(s, k, 1))
    return s


def rows_sum(z):
    return jnp.sum(z, axis=0, keepdims=True)


def eight_sum(z):
    return jnp.sum(z.reshape(z.shape[0] // 8, 8, z.shape[1]), axis=0)


def stack_rows(rows):
    return rows[0] if len(rows) == 1 else jnp.concatenate(rows, axis=0)


def add_to(total, part):
    return part if total is None else total + part


def norm_from_sums(base, one, two, pixels):
    own = one * (1.0 / pixels)
    center = base + own
    mean = group_total(center) * 0.125
    off = center - mean
    spread = group_total(two - one * own + off * off * pixels) * (1.0 / (8 * pixels))
    return mean, lax.rsqrt(spread + NORM_EPS)


def norm_stats(get, n, pixels):
    base, one, two = [], [], []
    for m in range(n):
        first = get(m, 0, 8)[0:1]
        base.append(first)
        s1 = s2 = None
        for r in range(0, pixels, PASS_ROWS):
            d = get(m, r, PASS_ROWS) - first
            s1 = add_to(s1, eight_sum(d))
            s2 = add_to(s2, eight_sum(d * d))
        one.append(rows_sum(s1))
        two.append(rows_sum(s2))
    return norm_from_sums(stack_rows(base), stack_rows(one), stack_rows(two), pixels)


def sigmoid(v):
    return 0.5 * jnp.tanh(0.5 * v) + 0.5


def shift_store(dst, m, start, value, breadth, forward):
    pixels, channels = value.shape
    column = lax.broadcasted_iota(jnp.int32, value.shape, 0) & (breadth - 1)
    before = jnp.where(column == 0, 0.0, pltpu.roll(value, 1, 0)).astype(BF)
    after = jnp.where(column == breadth - 1, 0.0, pltpu.roll(value, pixels - 1, 0)).astype(BF)
    lo, hi = (before, after) if forward else (after, before)
    rows = slice(breadth + start, breadth + start + pixels)
    dst[m, rows, 0:channels] = lo
    dst[m, rows, channels : 2 * channels] = value.astype(BF)
    dst[m, rows, 2 * channels :] = hi


def shift_all(dst, src, n, pixels, breadth):
    for m in range(n):
        for r in range(0, pixels, PASS_ROWS):
            at = m * pixels + r
            shift_store(dst, m, r, src[at : at + PASS_ROWS, :].astype(F32), breadth, False)


def zero_edges(dst, breadth):
    n, rows, width = dst.shape
    edge = jnp.zeros((n, breadth, width), BF)
    dst[:, 0:breadth, :] = edge
    dst[:, rows - breadth :, :] = edge


def half_lanes(place):
    return pl.ds(pl.multiple_of(place * 128, 128), 128)


def join_halves(place, own, other, dst):
    dst[:, half_lanes(place)] = own[...].reshape(dst.shape[0], 128)
    dst[:, half_lanes(1 - place)] = other[...]


def conv_part(shifted, kt, m, start, count, breadth):
    total = None
    for p in range(3):
        for q in range(3):
            tap = 3 * p + q
            first = p * breadth + start
            window = shifted[m, first : first + count, q * 256 : (q + 1) * 256]
            total = add_to(total, dot(window, kt[tap * 256 : (tap + 1) * 256, :], NT))
    return total


def back_part(shifted, kt, m, start, count, breadth):
    parts = []
    for p in range(3):
        first = (2 - p) * breadth + start
        parts.append(shifted[m, first : first + count, :])
    return dot(jnp.concatenate(parts, axis=1), kt[...])


def conv_weight(shifted, act, acc, n, pixels, breadth):
    for p in range(3):
        start = (2 - p) * breadth
        window = shifted[:, start : start + pixels, :].reshape(n * pixels, 768)
        acc[p * 768 : (p + 1) * 768, :] += dot(window, act, TN)


def activate(get, mean, inverse, gain, shift, n, pixels, breadth, zh_o, u_o, shifted):
    for m in range(n):
        scale = inverse[m : m + 1, :]
        offset = -mean[m : m + 1, :] * scale
        for r in range(0, pixels, PASS_ROWS):
            rows = slice(m * pixels + r, m * pixels + r + PASS_ROWS)
            zh = get(m, r, PASS_ROWS) * scale + offset
            zh_o[rows, :] = zh.astype(BF)
            a = zh * gain + shift
            u = a * sigmoid(a)
            u_o[rows, :] = u.astype(BF)
            shift_store(shifted, m, r, u, breadth, True)


def each_slot(places, low, high, body):
    count = low.shape[0]

    def step(i, carry):
        body(low, i, places[i])
        body(high, i, places[count + i])
        return carry

    lax.fori_loop(0, count, step, 0)


def lanes_of(place):
    return pl.ds(pl.multiple_of((place & 1) * 128, 128), 128)


def rows_of(index, count, unit):
    return pl.ds(pl.multiple_of(index * count, unit), count)


def first_kernel(sc, *refs, n, height, breadth, build, cols, vcols):
    pixels = height * breadth
    if build:
        (places, xa, xb, low, high, c1_o, u1_o, zh_o, inv_o, kt, vec, x_s, shifted, vt) = refs
    else:
        (xa, xb, kt, vec, c1_o, u1_o, zh_o, inv_o, x_s, shifted) = refs
    join_halves(sc[0], xa, xb, x_s)

    @pl.when(pl.program_id(0) == 0)
    def _():
        zero_edges(shifted, breadth)
        if build:

            def fill(ref, i, place):
                kt[rows_of(place >> 1, cols, 16), lanes_of(place)] = ref[i, 0:cols, :]
                extra = ref[i, cols : cols + 16, :].astype(F32)
                vt[rows_of(place, vcols, 8), :] = extra[0:vcols]

            each_slot(places, low, high, fill)
            vec[...] = vt[...].T[0:16, :]

    def get(m, r, count):
        return x_s[m * pixels + r : m * pixels + r + count, :].astype(F32)

    mean, inverse = norm_stats(get, n, pixels)
    inv_o[0, 0:n, :] = inverse
    activate(
        get, mean, inverse, vec[0:1, :], vec[1:2, :], n, pixels, breadth, zh_o, u1_o, shifted
    )
    for m in range(n):
        first = s1 = s2 = None
        for r in range(0, pixels, PART_ROWS):
            part = conv_part(shifted, kt, m, r, PART_ROWS, breadth)
            c1_o[m * pixels + r : m * pixels + r + PART_ROWS, :] = part
            first = part[0:1] if first is None else first
            d = part - first
            s1 = add_to(s1, eight_sum(d))
            s2 = add_to(s2, eight_sum(d * d))
        inv_o[0, 8 + m : 9 + m, :] = first
        inv_o[0, 16 + m : 17 + m, :] = rows_sum(s1)
        inv_o[0, 24 + m : 25 + m, :] = rows_sum(s2)


def middle_kernel(
    sc, *refs, n, height, breadth, own, which, first_call, build, cols, time_rows, qcols, pcols,
    first_map,
):
    pixels = height * breadth
    step = pl.program_id(0)
    refs = list(refs)

    def take(count):
        taken = refs[:count]
        del refs[:count]
        return taken

    if build:
        (places,) = take(1)
    c1, st, xa, xb, ga, gb = take(6)
    if build:
        low, high, feats = take(3)
    else:
        te, kt, wqkv, wo = take(4)
    (vec,) = take(1)
    if not first_call:
        aq_i, ao_i, av_i = take(3)
    u2_o, zh2_o, inv2_o, gc2_o, mine_o, send_o, aq, ao, av = take(9)
    if build:
        te, kt, wqkv, wo = take(4)
    (x_s, gy_s, shifted, h_s, zh3_s, hn_s, qkv_s, o_s, go_s, j_s, gk_s, gv_s) = take(12)
    s_s, gp_s, p_s16, gs_s16 = take(4)
    if build:
        wt_s, q_s, p_s = take(3)
    join_halves(sc[0], xa, xb, x_s)
    join_halves(sc[0], ga, gb, gy_s)

    @pl.when(step == 0)
    def _():
        zero_edges(shifted, breadth)
        aq[...] = jnp.zeros_like(aq) if first_call else aq_i[...]
        ao[...] = jnp.zeros_like(ao) if first_call else ao_i[...]
        av[...] = jnp.zeros_like(av) if first_call else av_i[...]
        if build:
            top = cols + time_rows
            both = qcols + pcols

            def fill(ref, i, place):
                kt[rows_of(place >> 1, cols, 16), lanes_of(place)] = ref[i, 0:cols, :]
                wt_s[rows_of(place >> 1, time_rows, 16), lanes_of(place)] = ref[i, cols:top, :]
                attn = ref[i, top : top + 2 * both, :].astype(F32)
                for part in range(2):
                    lanes = slice(part * 128, (part + 1) * 128)
                    start = part * both
                    q_s[rows_of(place, qcols, 8), lanes] = attn[start : start + qcols]
                    p_s[rows_of(place, pcols, 8), lanes] = attn[start + qcols : start + both]

            each_slot(places, low, high, fill)
            wqkv[...] = q_s[...].astype(BF)
            wo[...] = p_s[...].astype(BF)
            te[...] = dot(feats[...], wt_s[...]) + vec[6:7, :] + vec[7:8, :]

    items = [(m, r) for m in range(n) for r in range(0, pixels, PART_ROWS)]

    def at(m, r, count=PART_ROWS):
        return slice(m * pixels + r, m * pixels + r + count)

    live = []
    sum_gy = None
    for m in range(n):
        slot = sc[0] * own + step * n + m
        live.append((slot < sc[1 + which]).astype(F32))
        for r in range(0, pixels, PASS_ROWS):
            gy = gy_s[at(m, r, PASS_ROWS), :].astype(F32) * live[m]
            sum_gy = add_to(sum_gy, eight_sum(gy))
            gy_s[at(m, r, PASS_ROWS), :] = gy.astype(BF)

    extra = stack_rows([te[pl.ds(first_map + step * n + m, 1), :] for m in range(n)])
    mean, inverse = norm_from_sums(
        st[0, 8 : 8 + n, :] + extra, st[0, 16 : 16 + n, :], st[0, 24 : 24 + n, :], pixels
    )
    inv2_o[0, 0:n, :] = inverse

    def get_c1(m, r, count):
        return c1[at(m, r, count), :]

    activate(
        get_c1, mean - extra, inverse, vec[2:3, :], vec[3:4, :], n, pixels, breadth,
        zh2_o, u2_o, shifted,
    )
    for m, r in items:
        go_s[at(m, r), :] = dot(gy_s[at(m, r), :], wo[...]).astype(BF)
    base, one, two = [], [], []
    for m in range(n):
        first = s1 = s2 = None
        for r in range(0, pixels, PART_ROWS):
            part = conv_part(shifted, kt, m, r, PART_ROWS, breadth)
            part = part + vec[8:9, :] + x_s[at(m, r), :].astype(F32)
            h_s[at(m, r), :] = part
            first = part[0:1] if first is None else first
            d = part - first
            s1 = add_to(s1, eight_sum(d))
            s2 = add_to(s2, eight_sum(d * d))
        base.append(first)
        one.append(rows_sum(s1))
        two.append(rows_sum(s2))

    mean, inverse3 = norm_from_sums(stack_rows(base), stack_rows(one), stack_rows(two), pixels)
    for m, r in items:
        scale = inverse3[m : m + 1, :]
        offset = -mean[m : m + 1, :] * scale
        for k in range(r, r + PART_ROWS, PASS_ROWS):
            zh = h_s[at(m, k, PASS_ROWS), :] * scale + offset
            zh3_s[at(m, k, PASS_ROWS), :] = zh.astype(BF)
            hn_s[at(m, k, PASS_ROWS), :] = (zh * vec[4:5, :] + vec[5:6, :]).astype(BF)
        for part in range(3):
            lanes = slice(part * 256, (part + 1) * 256)
            projected = dot(hn_s[at(m, r), :], wqkv[lanes, :], NT)
            if part == 0:
                projected = projected + vec[9:10, :]
            if part == 2:
                projected = projected + vec[10:11, :]
            qkv_s[at(m, r), lanes] = projected.astype(BF)

    scale = 1.0 / math.sqrt(256)

    def map_rows(m):
        return slice(m * pixels, (m + 1) * pixels)

    def scores_of(i):
        m, r = items[i]
        s_s[i % 2] = dot(qkv_s[at(m, r), 0:256], qkv_s[map_rows(m), 256:512], NT)
        gp_s[i % 2] = dot(go_s[at(m, r), :], qkv_s[map_rows(m), 512:768], NT)

    sum_q = None
    sum_v = None
    scores_of(0)
    for i, (m, r) in enumerate(items):
        if i + 1 < len(items):
            scores_of(i + 1)
        for k in range(0, PART_ROWS, SOFT_ROWS):
            rows = slice(k, k + SOFT_ROWS)
            scores = s_s[i % 2, rows, :]
            top = jnp.max(scores, axis=1, keepdims=True)
            exponent = jnp.exp((scores - top) * scale)
            probs = exponent * (1.0 / jnp.sum(exponent, axis=1, keepdims=True))
            p_s16[i % 2, rows, :] = probs.astype(BF)
            weighted = probs * gp_s[i % 2, rows, :]
            inner = jnp.sum(weighted, axis=1, keepdims=True)
            gs_s16[i % 2, rows, :] = (weighted - probs * inner).astype(BF)
        keys = qkv_s[map_rows(m), 256:512]
        values = qkv_s[map_rows(m), 512:768]
        low = p_s16[i % 2]
        grad_s = gs_s16[i % 2]
        o_s[at(m, r), :] = dot(low, values).astype(BF)
        grad_q = dot(grad_s, keys) * scale
        sum_q = add_to(sum_q, eight_sum(grad_q))
        j_s[at(m, r), 0:256] = grad_q.astype(BF)
        grad_k = dot(grad_s, qkv_s[at(m, r), 0:256], TN)
        grad_v = dot(low, go_s[at(m, r), :], TN)
        if r > 0:
            grad_k = grad_k + gk_s[...]
            grad_v = grad_v + gv_s[...]
        if r + PART_ROWS < pixels:
            gk_s[...] = grad_k
            gv_s[...] = grad_v
        else:
            j_s[map_rows(m), 256:512] = (grad_k * scale).astype(BF)
            sum_v = add_to(sum_v, eight_sum(grad_v))
            j_s[map_rows(m), 512:768] = grad_v.astype(BF)

    gain = vec[4:5, :]
    one, two = [], []
    for m in range(n):
        s1 = s2 = None
        for r in range(0, pixels, PART_ROWS):
            low = dot(j_s[at(m, r), :], wqkv[...]).astype(BF)
            hn_grad = low.astype(F32)
            go_s[at(m, r), :] = low
            s1 = add_to(s1, eight_sum(hn_grad))
            s2 = add_to(s2, eight_sum(hn_grad * zh3_s[at(m, r), :].astype(F32)))
        one.append(rows_sum(s1))
        two.append(rows_sum(s2))
    one = stack_rows(one)
    two = stack_rows(two)
    mean_one = group_total(one * gain) * (1.0 / (8 * pixels))
    mean_two = group_total(two * gain) * (1.0 / (8 * pixels))

    ao[...] += dot(gy_s[...], o_s[...], TN)
    aq[...] += dot(j_s[...], hn_s[...], TN)

    for m, r in items:
        branch = (dot(o_s[at(m, r), :], wo[...], NT) + vec[11:12, :]).astype(BF).astype(F32)
        x_s[at(m, r), :] = ((h_s[at(m, r), :] + branch) * live[m]).astype(BF)
    for m in range(n):
        own_half = x_s[map_rows(m), half_lanes(sc[0])]
        other_half = x_s[map_rows(m), half_lanes(1 - sc[0])]
        mine_o[m] = own_half.reshape(height, breadth, 128)
        send_o[m] = other_half.reshape(height, breadth, 128)

    bias = None
    for m in range(n):
        scale_d = inverse3[m : m + 1, :] * gain
        offset = inverse3[m : m + 1, :] * mean_one[m : m + 1, :]
        scale_z = inverse3[m : m + 1, :] * mean_two[m : m + 1, :]
        for r in range(0, pixels, PASS_ROWS):
            rows = at(m, r, PASS_ROWS)
            gz = (
                go_s[rows, :].astype(F32) * scale_d - offset - zh3_s[rows, :].astype(F32) * scale_z
            )
            low = (gz + gy_s[rows, :].astype(F32)).astype(BF)
            gc2_o[rows, :] = low
            bias = add_to(bias, eight_sum(low.astype(F32)))
    av[4:5, :] += rows_sum(two)
    av[5:6, :] += rows_sum(one)
    av[8:9, :] += rows_sum(bias)
    av[9:10, :] += rows_sum(sum_q)
    av[10:11, :] += rows_sum(sum_v)
    av[11:12, :] += rows_sum(sum_gy)


def conv_norm_back(
    shifted, kt, d_s, zh_ref, inv_ref, gain, shift, n, pixels, breadth, between, emit
):
    one, two = [], []
    for m in range(n):
        s1 = s2 = None
        for r in range(0, pixels, PART_ROWS):
            rows = slice(m * pixels + r, m * pixels + r + PART_ROWS)
            grad_act = back_part(shifted, kt, m, r, PART_ROWS, breadth)
            zh = zh_ref[rows, :].astype(F32)
            a = zh * gain + shift
            s = sigmoid(a)
            d = grad_act * (s * (1.0 + a * (1.0 - s)))
            d_s[rows, :] = d
            s1 = add_to(s1, eight_sum(d))
            s2 = add_to(s2, eight_sum(d * zh))
        one.append(rows_sum(s1))
        two.append(rows_sum(s2))
    one = stack_rows(one)
    two = stack_rows(two)
    mean_one = group_total(one * gain) * (1.0 / (8 * pixels))
    mean_two = group_total(two * gain) * (1.0 / (8 * pixels))
    between()
    for m in range(n):
        inverse = inv_ref[0, m : m + 1, :]
        scale_d = inverse * gain
        offset = inverse * mean_one[m : m + 1, :]
        scale_z = inverse * mean_two[m : m + 1, :]
        for r in range(0, pixels, PASS_ROWS):
            rows = slice(m * pixels + r, m * pixels + r + PASS_ROWS)
            zh = zh_ref[rows, :].astype(F32)
            emit(m, r, rows, d_s[rows, :] * scale_d - offset - zh * scale_z)
    return rows_sum(one), rows_sum(two)


def second_back_kernel(
    sc, *refs, n, height, breadth, first_call, pack, cols, time_rows, qcols, pcols
):
    pixels = height * breadth
    step = pl.program_id(0)
    refs = list(refs)

    def take(count):
        taken = refs[:count]
        del refs[:count]
        return taken

    if pack:
        (places,) = take(1)
    gc2, u2, zh2, inv2, kt, vec, av_i = take(7)
    if not first_call:
        (ak_i,) = take(1)
    if pack:
        aq, ao, feats, ge_i = take(4)
    gc1_o, av = take(2)
    if pack:
        keep, send = take(2)
    else:
        ge_o, ak = take(2)
    shifted, d_s = take(2)
    if pack:
        ak, ge_o, wt_s = take(3)

    @pl.when(step == 0)
    def _():
        zero_edges(shifted, breadth)
        ak[...] = jnp.zeros_like(ak) if first_call else ak_i[...]
        av[...] = av_i[...]
        if pack:
            ge_o[...] = ge_i[...]
        else:
            ge_o[...] = jnp.zeros_like(ge_o)

    shift_all(shifted, gc2, n, pixels, breadth)
    sums = [None] * n

    def emit(m, r, rows, grad):
        low = grad.astype(BF)
        gc1_o[rows, :] = low
        sums[m] = add_to(sums[m], eight_sum(low.astype(F32)))

    def between():
        conv_weight(shifted, u2[...], ak, n, pixels, breadth)

    one, two = conv_norm_back(
        shifted, kt, d_s, zh2, inv2, vec[2:3, :], vec[3:4, :], n, pixels, breadth, between, emit
    )
    av[2:3, :] += two
    av[3:4, :] += one
    base = 8 if pack else 0
    for m in range(n):
        ge = rows_sum(sums[m])
        ge_o[pl.ds(base + step * n + m, 1), :] = ge
        av[6:7, :] += ge
        av[7:8, :] += ge

    if pack:

        @pl.when(step == pl.num_programs(0) - 1)
        def _():
            wt_s[...] = lax.dot_general(
                feats[...].astype(F32), ge_o[...], TN, precision=PRECISE,
                preferred_element_type=F32,
            )
            top = cols + time_rows
            both = qcols + pcols

            def fill(ref, i, place):
                lanes = lanes_of(place)
                ref[i, 0:cols, :] = ak[rows_of(place >> 1, cols, 8), lanes].astype(BF)
                ref[i, cols:top, :] = wt_s[rows_of(place >> 1, time_rows, 8), lanes].astype(BF)
                for part in range(2):
                    half = slice(part * 128, (part + 1) * 128)
                    block = jnp.concatenate(
                        [
                            aq[rows_of(place, qcols, 8), half],
                            ao[rows_of(place, pcols, 8), half],
                        ],
                        axis=0,
                    )
                    ref[i, top + part * both : top + (part + 1) * both, :] = block.astype(BF)

            each_slot(places, keep, send, fill)


def first_weight_kernel(sc, *refs, n, height, breadth, first_call, pack, cols):
    pixels = height * breadth
    step = pl.program_id(0)
    if pack:
        places, gc1, u1, ak_i, keep, send, shifted, ak = refs
    elif first_call:
        gc1, u1, ak, shifted = refs
    else:
        gc1, u1, ak_i, ak, shifted = refs

    @pl.when(step == 0)
    def _():
        zero_edges(shifted, breadth)
        ak[...] = jnp.zeros_like(ak) if first_call else ak_i[...]

    shift_all(shifted, gc1, n, pixels, breadth)
    conv_weight(shifted, u1[...], ak, n, pixels, breadth)

    if pack:

        @pl.when(step == pl.num_programs(0) - 1)
        def _():
            def fill(ref, i, place):
                ref[i] = ak[rows_of(place >> 1, cols, 8), lanes_of(place)].astype(BF)

            each_slot(places, keep, send, fill)


def first_back_kernel(
    sc, gc1, zh1, inv1, gc2, kt, vec, av_i, mine_o, send_o, av_o, shifted, d_s, *rest,
    n, height, breadth, last_call,
):
    pixels = height * breadth
    av = rest[0] if last_call else av_o

    @pl.when(pl.program_id(0) == 0)
    def _():
        zero_edges(shifted, breadth)
        av[...] = av_i[...]

    shift_all(shifted, gc1, n, pixels, breadth)

    def emit(m, r, rows, grad):
        d_s[rows, :] = grad + gc2[rows, :].astype(F32)
        lines = slice(r // breadth, (r + PASS_ROWS) // breadth)
        shape = (PASS_ROWS // breadth, breadth, 128)
        mine_o[m, lines] = d_s[rows, half_lanes(sc[0])].reshape(shape)
        send_o[m, lines] = d_s[rows, half_lanes(1 - sc[0])].astype(BF).reshape(shape)

    one, two = conv_norm_back(
        shifted, kt, d_s, zh1, inv1, vec[0:1, :], vec[1:2, :], n, pixels, breadth,
        lambda: None, emit,
    )
    av[0:1, :] += two
    av[1:2, :] += one

    if last_call:

        @pl.when(pl.program_id(0) == pl.num_programs(0) - 1)
        def _():
            padded = jnp.concatenate([av[...], jnp.zeros((112, 256), F32)], axis=0)
            av_o[...] = padded.T


class Group:
    def __init__(self, shape, which, block_rows=BLOCK_ROWS):
        self.maps, self.height, self.breadth, self.half = shape
        self.which = which
        self.own = self.maps // 2
        self.pixels = self.height * self.breadth
        self.n = max(1, min(self.own, block_rows // self.pixels))
        self.steps = self.own // self.n
        self.rows = self.n * self.pixels
        self.all_rows = self.own * self.pixels
        self.params = dict(n=self.n, height=self.height, breadth=self.breadth)

    def row_spec(self):
        return pl.BlockSpec((self.rows, 256), lambda i, sc, *_: (i, 0))

    def row_shape(self, dtype):
        return jax.ShapeDtypeStruct((self.all_rows, 256), dtype)

    def map_spec(self, placed):
        steps = self.steps
        shape = (self.n, self.height, self.breadth, 128)
        if placed:
            return pl.BlockSpec(shape, lambda i, sc, *_: (sc[0] * steps + i, 0, 0, 0))
        return pl.BlockSpec(shape, lambda i, sc, *_: (i, 0, 0, 0))

    def flat_spec(self, first):
        first = first // self.rows
        return pl.BlockSpec((self.rows, 128), lambda i, sc, *_: (first + i, 0))

    def map_shape(self, placed, dtype):
        count = self.maps if placed else self.own
        return jax.ShapeDtypeStruct((count, self.height, self.breadth, 128), dtype)

    def stat_spec(self):
        return pl.BlockSpec((1, 32, 256), lambda i, sc, *_: (i, 0, 0))

    def stat_shape(self):
        return jax.ShapeDtypeStruct((self.steps, 32, 256), F32)

    def shifted(self):
        return pltpu.VMEM((self.n, (self.height + 2) * self.breadth, 768), BF)

    def call(self, body, in_specs, out_specs, out_shape, scratch, flops, prefetch=1):
        return pl.pallas_call(
            body,
            grid_spec=pltpu.PrefetchScalarGridSpec(
                num_scalar_prefetch=prefetch,
                grid=(self.steps,),
                in_specs=in_specs,
                out_specs=out_specs,
                scratch_shapes=scratch,
            ),
            out_shape=out_shape,
            compiler_params=pltpu.CompilerParams(vmem_limit_bytes=VMEM_LIMIT),
            cost_estimate=pl.CostEstimate(
                flops=4 * flops, bytes_accessed=self.all_rows * 256 * 8, transcendentals=0
            ),
        )


def whole(shape):
    zeros = (0,) * len(shape)
    return pl.BlockSpec(shape, lambda i, sc, *_: zeros)


def run_first(g, sc, x, x_other, first_row, weights, dims):
    build = len(weights) == 3
    cols, vcols = dims["cols"], dims["vcols"]
    built = [whole((2304, 256)), whole((16, 256))]
    body = functools.partial(first_kernel, build=build, cols=cols, vcols=vcols, **g.params)
    outs = [g.row_spec(), g.row_spec(), g.row_spec(), g.stat_spec()]
    shapes = [g.row_shape(F32), g.row_shape(BF), g.row_shape(BF), g.stat_shape()]
    scratch = [pltpu.VMEM((g.rows, 256), BF), g.shifted()]
    flops = 2 * g.all_rows * 2304 * 256
    maps = [g.map_spec(True), g.flat_spec(first_row)]
    if build:
        places, low, high = weights
        return g.call(
            body,
            maps + [whole(low.shape), whole(high.shape)],
            outs + built,
            shapes
            + [jax.ShapeDtypeStruct((2304, 256), BF), jax.ShapeDtypeStruct((16, 256), F32)],
            scratch + [pltpu.VMEM((256, 128), F32)],
            flops,
            2,
        )(sc, places, x, x_other, low, high)
    return g.call(body, maps + built, outs, shapes, scratch, flops)(sc, x, x_other, *weights)


def run_middle(
    g, sc, c1, st, x, x_other, first_row, gy, gy_other, weights, vec, acc, first_map, dims
):
    build = len(weights) == 4 and weights[0].ndim == 1
    row = g.row_spec()
    big = pltpu.VMEM((g.rows, 256), F32)
    low16 = pltpu.VMEM((g.rows, 256), BF)
    wide = pltpu.VMEM((g.rows, 768), BF)
    body = functools.partial(
        middle_kernel, own=g.own, which=g.which, first_call=acc is None, build=build,
        first_map=first_map, cols=dims["cols"], time_rows=dims["time_rows"],
        qcols=dims["qcols"], pcols=dims["pcols"], **g.params,
    )
    acc_specs = [whole((768, 256)), whole((256, 256)), whole((16, 256))]
    built = [whole((16, 256)), whole((2304, 256)), whole((768, 256)), whole((256, 256))]
    maps = [
        g.map_spec(True), g.flat_spec(first_row), g.map_spec(True), g.flat_spec(0),
    ]
    ins = [row, g.stat_spec()] + maps
    outs = [row, row, g.stat_spec(), row, g.map_spec(True), g.map_spec(False)] + acc_specs
    shapes = [
        g.row_shape(BF), g.row_shape(BF), g.stat_shape(), g.row_shape(BF),
        g.map_shape(True, BF), g.map_shape(False, BF),
        jax.ShapeDtypeStruct((768, 256), F32), jax.ShapeDtypeStruct((256, 256), F32),
        jax.ShapeDtypeStruct((16, 256), F32),
    ]
    scratch = [
        low16, low16, g.shifted(), big, low16, low16, wide, low16, low16, wide,
        pltpu.VMEM((g.pixels, 256), F32), pltpu.VMEM((g.pixels, 256), F32),
        pltpu.VMEM((2, PART_ROWS, g.pixels), F32), pltpu.VMEM((2, PART_ROWS, g.pixels), F32),
        pltpu.VMEM((2, PART_ROWS, g.pixels), BF), pltpu.VMEM((2, PART_ROWS, g.pixels), BF),
    ]
    args = [c1, st, x, x_other, gy, gy_other]
    if build:
        places, low, high, feats = weights
        ins += [whole(low.shape), whole(high.shape), whole(feats.shape)]
        args = [places] + args + [low, high, feats]
        outs += built
        shapes += [
            jax.ShapeDtypeStruct((16, 256), F32), jax.ShapeDtypeStruct((2304, 256), BF),
            jax.ShapeDtypeStruct((768, 256), BF), jax.ShapeDtypeStruct((256, 256), BF),
        ]
        scratch += [
            pltpu.VMEM((feats.shape[1], 256), BF), pltpu.VMEM((768, 256), F32),
            pltpu.VMEM((256, 256), F32),
        ]
    else:
        ins += built
        args += list(weights)
    ins += [whole((16, 256))]
    args += [vec]
    if acc is not None:
        ins += acc_specs
        args += list(acc)
    flops = 2 * g.all_rows * 256 * (2304 + 256 * 12 + 6 * g.pixels)
    return g.call(body, ins, outs, shapes, scratch, flops, 2 if build else 1)(sc, *args)


def run_second_back(g, sc, gc2, u2, zh2, inv2, kt, vec, av, ak, packing, dims):
    row = g.row_spec()
    body = functools.partial(
        second_back_kernel, first_call=ak is None, pack=packing is not None,
        cols=dims["cols"], time_rows=dims["time_rows"], qcols=dims["qcols"],
        pcols=dims["pcols"], **g.params,
    )
    ins = [row, row, row, g.stat_spec(), whole((2304, 256)), whole((16, 256)), whole((16, 256))]
    args = [gc2, u2, zh2, inv2, kt, vec, av]
    outs = [row, whole((16, 256))]
    shapes = [g.row_shape(BF), jax.ShapeDtypeStruct((16, 256), F32)]
    scratch = [g.shifted(), pltpu.VMEM((g.rows, 256), F32)]
    if ak is not None:
        ins += [whole((2304, 256))]
        args += [ak]
    if packing is not None:
        places, aq, ao, feats, ge = packing
        ins += [whole((768, 256)), whole((256, 256)), whole(feats.shape), whole((16, 256))]
        args = [places] + args + [aq, ao, feats, ge]
        slots = (
            dims["places"] // 2,
            dims["cols"] + dims["time_rows"] + 2 * (dims["qcols"] + dims["pcols"]),
            128,
        )
        outs += [whole(slots)] * 2
        shapes += [jax.ShapeDtypeStruct(slots, BF)] * 2
        scratch += [
            pltpu.VMEM((2304, 256), F32), pltpu.VMEM((16, 256), F32),
            pltpu.VMEM((feats.shape[1], 256), F32),
        ]
    else:
        outs += [whole((16, 256)), whole((2304, 256))]
        shapes += [
            jax.ShapeDtypeStruct((16, 256), F32), jax.ShapeDtypeStruct((2304, 256), F32)
        ]
    return g.call(
        body, ins, outs, shapes, scratch, 4 * g.all_rows * 256 * 2304,
        1 if packing is None else 2,
    )(sc, *args)


def run_first_weight(g, sc, gc1, u1, ak, places, dims):
    row = g.row_spec()
    body = functools.partial(
        first_weight_kernel, first_call=ak is None, pack=places is not None,
        cols=dims["cols"], **g.params,
    )
    ins = [row, row]
    args = [gc1, u1]
    scratch = [g.shifted()]
    if ak is not None:
        ins += [whole((2304, 256))]
        args += [ak]
    if places is None:
        outs = whole((2304, 256))
        shapes = jax.ShapeDtypeStruct((2304, 256), F32)
    else:
        args = [places] + args
        slots = (dims["places"] // 2, dims["cols"], 128)
        outs = [whole(slots)] * 2
        shapes = [jax.ShapeDtypeStruct(slots, BF)] * 2
        scratch += [pltpu.VMEM((2304, 256), F32)]
    return g.call(
        body, ins, outs, shapes, scratch, 2 * g.all_rows * 256 * 2304,
        1 if places is None else 2,
    )(sc, *args)


def run_first_back(g, sc, gc1, zh1, inv1, gc2, kt, vec, av, last_call):
    row = g.row_spec()
    shape = (256, 128) if last_call else (16, 256)
    return g.call(
        functools.partial(first_back_kernel, last_call=last_call, **g.params),
        [row, row, g.stat_spec(), row, whole((2304, 256)), whole((16, 256)), whole((16, 256))],
        [g.map_spec(True), g.map_spec(False), whole(shape)],
        [g.map_shape(True, F32), g.map_shape(False, BF), jax.ShapeDtypeStruct(shape, F32)],
        [g.shifted(), pltpu.VMEM((g.rows, 256), F32)]
        + ([pltpu.VMEM((16, 256), F32)] if last_call else []),
        2 * g.all_rows * 256 * 2304,
    )(sc, gc1, zh1, inv1, gc2, kt, vec, av)


def features(steps, index, half_width):
    frequency = jnp.exp(
        (index % half_width).astype(F32) * (-LOG_PERIOD / (half_width - 1))
    )
    angles = steps.astype(F32)[:, None] * frequency[None, :]
    return jax.nn.silu(
        jnp.where(index[None, :] < half_width, jnp.sin(angles), jnp.cos(angles))
    ).astype(BF)


def adam_step(weight, grad, mean, square, rate, decay):
    mean_new = ADAM_ONE * mean + (1.0 - ADAM_ONE) * grad
    square_new = ADAM_TWO * square + (1.0 - ADAM_TWO) * grad * grad
    first_fix = mean_new / (1.0 - ADAM_ONE**STEP_NUMBER)
    second_fix = square_new / (1.0 - ADAM_TWO**STEP_NUMBER)
    weight_new = weight - rate * (first_fix / (jnp.sqrt(second_fix) + ADAM_EPS) + decay * weight)
    return (weight_new, mean_new, square_new)


def other_rows(x, here):
    own = x.shape[0] // 2
    return lax.dynamic_slice_in_dim(x, (1 - here) * own, own, 0).reshape(-1, x.shape[3])


def put_part(full, arrived, here):
    own = arrived.shape[0]
    return lax.dynamic_update_slice_in_dim(
        full, arrived.astype(full.dtype), (1 - here) * own, 0
    )


def per_device(
    small_maps, large_maps, small_steps, large_steps, live_counts,
    small_cotangent, large_cotangent,
    first_conv, second_conv, time_dense, attn_qkv, attn_proj, vectors,
    first_conv_mean, first_conv_square, second_conv_mean, second_conv_square,
    time_dense_mean, time_dense_square, attn_qkv_mean, attn_qkv_square,
    attn_proj_mean, attn_proj_square, vectors_mean, vectors_square,
):
    n_wide = lax.axis_size("wide")
    here = lax.axis_index("narrow")
    channels = attn_qkv.shape[0]
    half = first_conv.shape[0]
    cols = first_conv.shape[1]
    time_rows = time_dense.shape[0]
    feature_width = time_rows * n_wide
    qcols = attn_qkv.shape[1]
    pcols = attn_proj.shape[1]
    vcols = vectors.shape[1]
    dims = dict(
        cols=cols, time_rows=time_rows, qcols=qcols, pcols=pcols, vcols=vcols, places=2 * n_wide
    )
    fits = not (cols % 16 or time_rows % 16 or qcols % 8 or pcols % 8 or vcols % 8)
    order = gather_order()
    devices = device_table(order)
    small = Group(small_maps.shape, 0)
    large = Group(large_maps.shape, 1)
    small_whole = Group(small_maps.shape, 0, 2 * BLOCK_ROWS)
    large_whole = Group(large_maps.shape, 1, 2 * BLOCK_ROWS)

    if fits:
        block_one, block_two = run_prepare(
            first_conv.T, second_conv.T, time_dense, attn_qkv.T, attn_proj.T, vectors.T
        )
    else:
        vec_rows = jnp.pad(
            vectors.astype(BF).T, ((0, 16 - vcols), (0, 128 - vectors.shape[0]))
        )
        block_one = jnp.concatenate([first_conv.astype(BF).T, vec_rows], axis=0)
        attn_rows = jnp.concatenate([attn_qkv.astype(BF).T, attn_proj.astype(BF).T], axis=0)
        block_two = jnp.concatenate(
            [
                second_conv.astype(BF).T, time_dense.astype(BF),
                attn_rows[:, :128], attn_rows[:, 128:],
            ],
            axis=0,
        )
    one, log = block_one[None], []
    for _ in order:
        one, log = gather_step(one, log, order)
    two, log_two = block_two[None], []
    for i in range(len(order) - 1):
        two, log_two = gather_step(two, log_two, order, log[(0, 1, 2)[min(i, 2)]])
    xs = swap_narrow(other_rows(tie(small_maps, (log[0], log_two[0])), here))
    xl = swap_narrow(other_rows(tie(large_maps, (log[1], log_two[0])), here))
    pair_one = (one, log[-1])
    small_steps, large_steps, live_counts = tie((small_steps, large_steps, live_counts), log[2])
    sc = jnp.concatenate([here[None].astype(jnp.int32), live_counts[0]])

    own_small = lax.dynamic_slice_in_dim(small_steps, here * small.own, small.own, 0)
    own_large = lax.dynamic_slice_in_dim(large_steps, here * large.own, large.own, 0)
    own_steps = jnp.pad(
        jnp.concatenate([own_small, own_large]), (0, 16 - small.own - large.own)
    )
    feats = features(own_steps, jnp.arange(feature_width), feature_width // 2)
    if fits:
        weights_one = (devices, *pair_one)
    else:
        table = slot_table(order)
        kt_one, vec = run_unpack(
            jnp.concatenate(pair_one), table, ((0, cols, True), (cols, cols + 16, False))
        )
        vec = vec[:, :vcols, :16].reshape(channels, 16).T.astype(F32)
        weights_one = (kt_one.reshape(n_wide * cols, 2 * half), vec)

    s_c1, s_u1, s_zh1, s_inv1, *built = run_first(
        small, sc, small_maps, xs, 0, weights_one, dims
    )
    weights_one = built if fits else weights_one
    kt_one, vec = weights_one
    gs = swap_narrow(other_rows(tie(small_cotangent, pair_one[1]), here))
    two, log_two = gather_step(two, log_two, order, s_c1)
    pair_two = (two, log_two[-1])
    xl = tie(xl, (s_c1, log_two[-2], gs))
    l_c1, l_u1, l_zh1, l_inv1 = run_first(
        large, sc, large_maps, xl, 0, weights_one, dims
    )
    gl = swap_narrow(other_rows(tie(large_cotangent, s_c1), here))
    if fits:
        weights_two = (devices, *pair_two, feats)
    else:
        top = cols + time_rows
        both = qcols + pcols
        kt_two, wt, attn = run_unpack(
            jnp.concatenate(pair_two), table,
            ((0, cols, True), (cols, top, True), (top, top + 2 * both, False)),
        )
        wt = wt.reshape(feature_width, 2 * half)
        attn = jnp.concatenate([attn[:, :both], attn[:, both:]], axis=2)
        te = jnp.dot(feats, wt, preferred_element_type=F32) + vec[7] + vec[6]
        weights_two = (
            te, kt_two.reshape(n_wide * cols, 2 * half),
            attn[:, :qcols].reshape(3 * channels, channels),
            attn[:, qcols:].reshape(channels, channels),
        )

    (s_u2, s_zh2, s_inv2, s_gc2, s_mine, s_send, aq, ao, av, *built) = run_middle(
        small, sc, s_c1, s_inv1, small_maps, xs, 0, small_cotangent, gs, weights_two, vec, None, 0,
        dims
    )
    out_arrived = swap_narrow(s_send)
    small_out = put_part(s_mine, out_arrived, here)
    weights_two = built if fits else weights_two
    kt_two = weights_two[1]
    (l_u2, l_zh2, l_inv2, l_gc2, l_mine, l_send, aq, ao, av) = run_middle(
        large, sc, l_c1, l_inv1, large_maps, xl, 0, large_cotangent, gl, weights_two,
        vec, (aq, ao, av), small.own, dims,
    )
    s_gc2 = tie(s_gc2, (out_arrived, l_gc2))
    out_arrived = swap_narrow(l_send)
    large_out = put_part(l_mine, out_arrived, here)

    s_gc1, av, ge, ak = run_second_back(
        small, sc, s_gc2, s_u2, s_zh2, s_inv2, kt_two, vec, av, None, None, dims
    )
    if fits:
        l_gc1, av, keep, send = run_second_back(
            large, sc, l_gc2, l_u2, l_zh2, l_inv2, kt_two, vec, av, ak,
            (devices, aq, ao, feats, ge), dims,
        )
    else:
        l_gc1, av, l_ge, ak = run_second_back(
            large, sc, l_gc2, l_u2, l_zh2, l_inv2, kt_two, vec, av, ak, None, dims
        )
        ge = jnp.concatenate([ge[:8], l_ge[:8]])
        gwt = jnp.dot(feats.astype(F32).T, ge, precision=PRECISE)
        packed = run_pack(
            (
                ak.reshape(n_wide, cols, 256), gwt.reshape(n_wide, time_rows, 256),
                aq.reshape(-1, qcols, 256), ao.reshape(-1, pcols, 256),
            ),
            devices, (True, True, False, False),
        )
        attn = jnp.concatenate(packed[2:], axis=1)
        slots = jnp.concatenate(
            [packed[0], packed[1], attn[:, :, :128], attn[:, :, 128:]], axis=1
        )
        keep, send = slots[:n_wide], slots[n_wide:]
    back = list(reversed(order))
    two = scatter_step((keep, send), back[0])
    s_gc1 = tie(s_gc1, (out_arrived, l_gc1))
    ak = run_first_weight(small_whole, sc, s_gc1, s_u1, None, None, dims)
    l_gc1 = tie(l_gc1, (ak, two))
    two = scatter_step(two, back[1])
    if fits:
        one = run_first_weight(large_whole, sc, l_gc1, l_u1, ak, devices, dims)
    else:
        ak = run_first_weight(large_whole, sc, l_gc1, l_u1, ak, None, dims)
        slots = run_pack((ak.reshape(n_wide, cols, 256),), devices, (True,))[0]
        one = (slots[:n_wide], slots[n_wide:])
    s_gc1 = tie(s_gc1, one)
    one = scatter_step(one, back[0])
    s_mine, s_send, av = run_first_back(
        small, sc, s_gc1, s_zh1, s_inv1, s_gc2, kt_one, vec, av, False
    )
    grad_arrived = swap_narrow(s_send)
    l_gc1 = tie(l_gc1, (av, one, two))
    two = scatter_step(two, back[2])
    l_mine, l_send, av = run_first_back(
        large, sc, l_gc1, l_zh1, l_inv1, l_gc2, kt_one, vec, av, True
    )
    large_arrived = swap_narrow(l_send)
    arrived = None
    last = len(back) - 1
    trail = []
    for i in range(1, last + 1):
        one = scatter_step(one, back[i], i == last)
        trail.append(one)
        if i == 1:
            arrived = lax.all_to_all(
                tie(av, one).reshape(2 * n_wide, vcols, 128), ("wide", "narrow"), split_axis=0,
                concat_axis=0, tiled=True,
            )
    late = trail[-2]
    two = tie(two, av)
    for i in range(3, last + 1):
        two = scatter_step(two, back[i], i == last, trail[-3] if i == last else None)
    small_grad = put_part(s_mine, tie(grad_arrived, trail[-3]), here)
    large_grad = put_part(l_mine, tie(large_arrived, late), here)
    arrived = tie(arrived, late)
    sum_one, sum_two = one, two
    sum_vec = arrived.sum(axis=0)[:, :12].T

    top = cols + time_rows
    both = qcols + pcols
    time_sum = sum_two[cols:top]
    attn_sum = jnp.concatenate([sum_two[top : top + both], sum_two[top + both :]], axis=1)
    one_new = adam_step(
        first_conv, sum_one.T, first_conv_mean, first_conv_square, RATE_CONV, DECAY
    )
    two_new = adam_step(
        second_conv, sum_two[:cols].T, second_conv_mean, second_conv_square, RATE_CONV, DECAY
    )
    time_new = adam_step(
        time_dense, time_sum, time_dense_mean, time_dense_square, RATE_TIME, DECAY
    )
    qkv_new = adam_step(
        attn_qkv, attn_sum[:qcols].T, attn_qkv_mean, attn_qkv_square, RATE_QKV, DECAY
    )
    proj_new = adam_step(
        attn_proj, attn_sum[qcols:].T, attn_proj_mean, attn_proj_square, RATE_PROJ, DECAY
    )
    vec_new = adam_step(vectors, sum_vec, vectors_mean, vectors_square, RATE_VECTOR, 0.0)
    return (
        small_out, large_out, small_grad, large_grad,
        *one_new, *two_new, *time_new, *qkv_new, *proj_new, *vec_new,
    )


def solution(mesh):
    maps = P("wide", None, None, "narrow")
    conv = P("narrow", "wide")
    dense = P("wide", "narrow")
    attn = P(None, ("wide", "narrow"))
    return jax.shard_map(
        per_device,
        mesh=mesh,
        in_specs=(
            maps, maps, P("wide"), P("wide"), P("wide", None), maps, maps,
            conv, conv, dense, attn, attn, attn,
            conv, conv, conv, conv, dense, dense, attn, attn, attn, attn, attn, attn,
        ),
        out_specs=(maps,) * 4 + (conv,) * 6 + (dense,) * 3 + (attn,) * 9,
        check_vma=False,
    )
```
